32 devices in a mesh: pipe: 4 (over y, x), expert: 8 (over z, core).
Axes of the slice: x: 2, y: 2, z: 4, core: 2. Of those that a mesh axis runs over, the one named last changes fastest.
Arguments:
- out_grad: bfloat16 [4, 1024, 3840], P('pipe', 'expert'), may hold values from -1.5 to 1.5
- routes: int32 [4, 2, 1024, 2], P('pipe', None, 'expert'), may hold values from 0 to 127, as said below
- positions: int32 [4, 2, 1024, 2], P('pipe', None, 'expert'), may hold values from -1 to 1, as said below
- route_probs: bfloat16 [4, 2, 1024, 2], P('pipe', None, 'expert'), may hold values from 0.049804688 to 0.94921875
- saved_acts: bfloat16 [4, 2, 16, 2, 1024], P('pipe', None, None, None, 'expert'), may hold values from -6 to 6
- w_gate: bfloat16 [4, 3840, 1024], P('pipe', None, 'expert'), may hold values from -0.09375 to 0.09375
- w_up: bfloat16 [4, 3840, 1024], P('pipe', None, 'expert'), may hold values from -0.09375 to 0.09375
- w_down: bfloat16 [4, 1024, 3840], P('pipe', 'expert'), may hold values from -0.375 to 0.375
Outputs:
- in_grad: bfloat16 [4, 1024, 3840], P('pipe', 'expert')
- prob_grad: float32 [4, 2, 1024, 2], P('pipe', None, 'expert')
The draws below stay inside these ranges and needn't reach their ends.
Inputs may be any that keep to these rules, and one draw needn't show every extreme that they name: `routes`: each row names two different experts. In every aligned block of 128 rows (one device's tokens for one section and step), each of the experts 0 to 3 is named by 1 to 2 rows, and at every section and step one of them is named by exactly 2 rows in every block. positions[p, t, i, k] is -1 exactly where routes[p, t, i, k] >= 4; otherwise, within the row's block, the pairs that name one expert hold the positions 0 to their count - 1, each once.
All inputs are finite; a program needn't handle non-finite values.
Results may differ from the reference program's by a relative error of at most 0.0034.
Values may be sent and summed in bfloat16 or wider, within the bound.
No kernel may reach another device: no remote copies, remote signals or barrier semaphores. Data moves between devices by JAX's collectives and lax.ppermute only.
A program may use at most 64 MiB of HBM per device.

```python
import jax
import jax.numpy as jnp

D = 3840
EXPERTS = 128
E_FLY = 4
MOST = 2
STEPS = 2
TOK_DEV = 128
PIPE = 4
FF = 256
TOKENS = 1024
SLOTS = 16


def shuffle_rows(row_key):
    return jax.random.permutation(row_key, TOK_DEV)


def route_table(key):
    block_count = PIPE * STEPS * (TOKENS // TOK_DEV)
    split_keys = jax.random.split(key, 6)
    counts = jax.random.randint(split_keys[0], (block_count, E_FLY), 1, MOST + 1, dtype=jnp.int32)
    full_expert = jax.random.randint(split_keys[1], (PIPE * STEPS, 1, 1), 0, E_FLY, dtype=jnp.int32)
    full_expert = jnp.broadcast_to(full_expert, (PIPE * STEPS, TOKENS // TOK_DEV, 1)).reshape(block_count, 1)
    expert_ids = jnp.arange(E_FLY, dtype=jnp.int32)[None, :]
    counts = jnp.where(expert_ids == full_expert, MOST, counts)
    count_ends = jnp.cumsum(counts, axis=1)
    count_starts = count_ends - counts
    live_total = count_ends[:, -1:]
    pick_ids = jnp.arange(TOK_DEV, dtype=jnp.int32)[None, :]
    pick_expert = jnp.sum((pick_ids[:, :, None] >= count_ends[:, None, :]).astype(jnp.int32), axis=2)
    clipped = jnp.minimum(pick_expert, E_FLY - 1)
    pick_start = jnp.take_along_axis(count_starts, clipped, axis=1)
    in_window = pick_ids < live_total
    others = EXPERTS - E_FLY
    first_other = jax.random.randint(split_keys[2], (block_count, TOK_DEV), E_FLY, EXPERTS, dtype=jnp.int32)
    first_route = jnp.where(in_window, clipped, first_other)
    first_slot = jnp.where(in_window, pick_ids - pick_start, -1)
    offsets = jax.random.randint(split_keys[3], (block_count, TOK_DEV), 1, others, dtype=jnp.int32)
    second_route = E_FLY + (first_route - E_FLY + offsets) % others
    second_slot = jnp.full((block_count, TOK_DEV), -1, jnp.int32)
    order = jax.vmap(shuffle_rows)(jax.random.split(split_keys[4], block_count))
    first_route = jnp.take_along_axis(first_route, order, axis=1)
    first_slot = jnp.take_along_axis(first_slot, order, axis=1)
    second_route = jnp.take_along_axis(second_route, order, axis=1)
    flipped = jax.random.randint(split_keys[5], (block_count, TOK_DEV), 0, 2, dtype=jnp.int32) == 1
    route_zero = jnp.where(flipped, second_route, first_route)
    route_one = jnp.where(flipped, first_route, second_route)
    slot_zero = jnp.where(flipped, second_slot, first_slot)
    slot_one = jnp.where(flipped, first_slot, second_slot)
    route_all = jnp.stack([route_zero, route_one], axis=-1).reshape(PIPE, STEPS, TOKENS, 2)
    slot_all = jnp.stack([slot_zero, slot_one], axis=-1).reshape(PIPE, STEPS, TOKENS, 2)
    return (route_all.astype(jnp.int32), slot_all.astype(jnp.int32))


def draw_routes(key, part):
    return route_table(key)[0]


def draw_positions(key, part):
    return route_table(key)[1]


def block_scale(rng, shape, pieces, smallest, largest):
    factor_of, own = 1.0, jax.random.fold_in(rng, 6)
    for dim, shards_of in pieces:
        heights = jnp.exp(jax.random.uniform(jax.random.fold_in(own, dim), (shards_of,), jnp.float32, smallest / len(pieces), largest / len(pieces)))
        factor_of = factor_of * jnp.repeat(heights, shape[dim] // shards_of).reshape([-1 if axis == dim else 1 for axis in range(len(shape))])
    return factor_of


def bell_draw(own_key, extent, scale, most, pieces=(), kind=jnp.bfloat16):
    level = block_scale(own_key, extent, pieces, -0.22, 0.18) if pieces else 1.0
    entries = jax.random.normal(own_key, extent, jnp.float32) * scale * level
    return jnp.minimum(jnp.maximum(entries, -most), most).astype(kind)


def setup_inputs(seed: int = 0) -> dict:
    arg_keys = jax.random.split(jax.random.key(seed), 9)
    return {
        "out_grad": bell_draw(arg_keys[0], (PIPE, TOKENS, D), 0.25, 1.5, ((0, 4), (1, 8))),
        "routes": draw_routes(jax.random.fold_in(arg_keys[8], 71), 0),
        "positions": draw_positions(jax.random.fold_in(arg_keys[8], 71), 0),
        "route_probs": jnp.clip(0.049804688 + 0.89941406 * jax.random.uniform(arg_keys[3], (PIPE, STEPS, TOKENS, 2), jnp.float32) ** block_scale(arg_keys[3], (PIPE, STEPS, TOKENS, 2), ((0, 4), (2, 8)), -0.2, 0.2), 0.049804688, 0.94921875).astype(jnp.bfloat16),
        "saved_acts": bell_draw(arg_keys[4], (PIPE, STEPS, SLOTS, 2, E_FLY * FF), 1.0, 6.0, ((0, 4), (4, 8))),
        "w_gate": bell_draw(arg_keys[5], (PIPE, D, E_FLY * FF), D ** -0.5, 0.09375, ((0, 4), (2, 8))),
        "w_up": bell_draw(arg_keys[6], (PIPE, D, E_FLY * FF), D ** -0.5, 0.09375, ((0, 4), (2, 8))),
        "w_down": bell_draw(arg_keys[7], (PIPE, E_FLY * FF, D), FF ** -0.5, 0.375, ((0, 4), (1, 8))),
    }


def expert_back(slot_rows, slot_rates, stored, gate_weight, up_weight, down_weight):
    downward = jnp.dot(slot_rows, down_weight.T, preferred_element_type=jnp.float32)
    gate_pre = stored[:, 0, :].astype(jnp.float32)
    upward = stored[:, 1, :].astype(jnp.float32)
    sigmoid_gate = jax.nn.sigmoid(gate_pre)
    active = gate_pre * sigmoid_gate
    hidden = active * upward
    scaled = slot_rates.astype(jnp.float32)[:, None] * downward
    grad_gate = (scaled * upward * sigmoid_gate * (1.0 + gate_pre * (1.0 - sigmoid_gate))).astype(jnp.bfloat16)
    grad_up = (scaled * active).astype(jnp.bfloat16)
    prob_terms = jnp.sum(hidden * downward, axis=1)
    back_rows = jnp.dot(grad_gate, gate_weight.T, preferred_element_type=jnp.float32)
    back_rows = back_rows + jnp.dot(grad_up, up_weight.T, preferred_element_type=jnp.float32)
    return back_rows, prob_terms


def section_back(current, route_part, place_part, rate_part, stored, gate_weight, up_weight, down_weight, source):
    dump_row = E_FLY * SLOTS
    in_window = place_part >= 0
    target = jnp.where(in_window, route_part * SLOTS + source[:, None] * MOST + place_part, dump_row).astype(jnp.int32)
    slot_rows = jnp.zeros((dump_row + 1, D), jnp.bfloat16)
    slot_rows = slot_rows.at[target[:, 0]].set(current).at[target[:, 1]].set(current)
    slot_rates = jnp.zeros((dump_row + 1,), jnp.bfloat16)
    slot_rates = slot_rates.at[target[:, 0]].set(rate_part[:, 0]).at[target[:, 1]].set(rate_part[:, 1])
    backs = []
    probs_list = []
    for expert_index in range(E_FLY):
        column = expert_index * FF
        row_start = expert_index * SLOTS
        back_rows, prob_terms = expert_back(
            slot_rows[row_start:row_start + SLOTS],
            slot_rates[row_start:row_start + SLOTS],
            stored[:, :, column:column + FF],
            gate_weight[:, column:column + FF],
            up_weight[:, column:column + FF],
            down_weight[column:column + FF, :])
        backs.append(back_rows.astype(jnp.bfloat16))
        probs_list.append(prob_terms)
    all_back = jnp.concatenate(backs + [jnp.zeros((1, D), jnp.bfloat16)], axis=0)
    all_terms = jnp.concatenate(probs_list + [jnp.zeros((1,), jnp.float32)], axis=0)
    delta = all_back[target[:, 0]].astype(jnp.float32) + all_back[target[:, 1]].astype(jnp.float32)
    new_grad = (current.astype(jnp.float32) + delta).astype(jnp.bfloat16)
    pair_grads = all_terms[target]
    return new_grad, pair_grads


def reference(out_grad, routes, positions, route_probs, saved_acts, w_gate, w_up, w_down):
    token_ids = jnp.arange(TOKENS, dtype=jnp.int32)
    source = (token_ids // TOK_DEV).astype(jnp.int32)
    section_grads = [out_grad[section_index] for section_index in range(PIPE)]
    final_grads = section_grads
    step_probs = []
    for step_index in range(STEPS):
        new_grads = []
        section_probs = []
        for section_index in range(PIPE):
            new_grad, pair_grads = section_back(
                section_grads[section_index],
                routes[section_index, step_index],
                positions[section_index, step_index],
                route_probs[section_index, step_index],
                saved_acts[section_index, step_index],
                w_gate[section_index], w_up[section_index], w_down[section_index], source)
            new_grads.append(new_grad)
            section_probs.append(pair_grads)
        step_probs.append(jnp.stack(section_probs, axis=0))
        section_grads = new_grads[1:] + [jnp.zeros_like(new_grads[0])]
        final_grads = new_grads
    in_grad = jnp.stack(final_grads, axis=0)
    prob_grad = jnp.stack(step_probs, axis=1)
    return (in_grad, prob_grad)
```

```python
import functools

import jax
import jax.numpy as jnp
from jax import lax
from jax.experimental import pallas as pl
from jax.experimental.pallas import tpu as pltpu
from jax.sharding import PartitionSpec as P

E_FLY = 4
MOST = 2
STEPS = 2
PAIRS = E_FLY * MOST
META = 128
CHUNK = 256
F32 = jnp.float32
BF16 = jnp.bfloat16
NT = (((1,), (1,)), ((), ()))
TN = (((0,), (0,)), ((), ()))


def call(kernel, name, out_shape, scratch=()):
    return pl.pallas_call(
        kernel,
        name=name,
        out_shape=out_shape,
        scratch_shapes=list(scratch),
        compiler_params=pltpu.CompilerParams(vmem_limit_bytes=24 * 2**20),
    )


def place():
    at = lax.axis_index("expert")
    return lax.axis_index("pipe"), at // 2, at % 2


def keys_of(routes, positions, step):
    return jnp.where(positions[step] >= 0, routes[step] * MOST + positions[step], -1)


def labels(rows, expert_of):
    row = lax.broadcasted_iota(jnp.int32, (rows, 1), 0)
    return expert_of(row // MOST) * MOST + row % MOST


def hits(keys, label):
    return keys[0:1] == label, keys[1:2] == label


def one_hot(keys, label):
    first, second = hits(keys, label)
    return jnp.where(first | second, 1.0, 0.0).astype(F32)


def rates_of(keys, rates, label):
    first, second = hits(keys, label)
    picked = jnp.where(first, rates[0:1], 0.0) + jnp.where(second, rates[1:2], 0.0)
    return jnp.sum(picked, axis=1, keepdims=True)


def first_lanes(columns):
    lane = lax.broadcasted_iota(jnp.int32, (columns[0].shape[0], META), 1)
    out = jnp.zeros(lane.shape, F32)
    for index, column in enumerate(columns):
        out = jnp.where(lane == index, column, out)
    return out


def put_rows(outs, rows, meta):
    width = rows.shape[1]
    for k, out in enumerate(outs):
        out[:, :width] = rows[MOST * k:MOST * (k + 1)].astype(BF16)
        out[:, width:] = meta[MOST * k:MOST * (k + 1)].astype(BF16)


def take_rows(scratch, refs):
    for k, ref in enumerate(refs):
        scratch[MOST * k:MOST * (k + 1), :] = ref[...].astype(F32)


def pick_kernel(grad, routes, positions, probs, *outs):
    _, z, _ = place()
    keys = keys_of(routes, positions, 0)
    label = labels(PAIRS, lambda k: (z + k) % E_FLY)
    select = one_hot(keys, label)
    rows = jnp.dot(select.astype(BF16), grad[...], preferred_element_type=F32)
    rate = rates_of(keys, probs[0].astype(F32), label)
    put_rows(outs[:E_FLY], rows, first_lanes([rate]))
    table = outs[E_FLY]
    table[0:2] = keys_of(routes, positions, 1).astype(F32)
    table[2:4] = probs[1].astype(F32)


def ahead_kernel(grad, routes, positions, table, acts, acts_other, *refs):
    outs, factors, gate_at, up_at = refs[:E_FLY], *refs[E_FLY:]
    p, z, c = place()
    keys0 = keys_of(routes, positions, 0)
    keys1 = table[0:2].astype(jnp.int32)
    keys1 = jnp.where(p == 0, -1, keys1)
    label = labels(PAIRS, lambda k: (z + k) % E_FLY)
    select = one_hot(keys1, label)
    rows = jnp.dot(select.astype(BF16), grad[...], preferred_element_type=F32)
    rate = rates_of(keys1, table[2:4], label)
    lane = lax.broadcasted_iota(jnp.int32, (PAIRS, META), 1)
    meta = jnp.where(lane == E_FLY * PAIRS, rate, 0.0)
    column = lax.broadcasted_iota(jnp.int32, (META, 1), 0)
    source, block, spot = column // PAIRS, column // MOST % E_FLY, column % MOST
    row = lax.broadcasted_iota(jnp.int32, (PAIRS, 1), 0)
    for k in range(E_FLY):
        expert = (z + k + E_FLY - source) % E_FLY
        own = (source < E_FLY) & ((source + block) % E_FLY == k)
        step0 = one_hot(keys0, jnp.where(own, expert * MOST + spot, -2))
        match = lax.dot_general(
            select.astype(BF16), step0.astype(BF16), NT, preferred_element_type=F32
        )
        meta = meta + jnp.where(row // MOST == k, match, 0.0)
    put_rows(outs, rows, meta)
    for step in range(STEPS):
        for k in range(E_FLY):
            first = (2 * ((z + E_FLY - k) % E_FLY) + c) * MOST
            for spot_at in range(MOST):
                at = MOST * k + spot_at
                for half, ref in enumerate((acts, acts_other)):
                    pair = ref[step, first + spot_at].astype(F32)
                    width = pair.shape[1]
                    gate_at[at:at + 1, half * width:(half + 1) * width] = pair[0:1]
                    up_at[at:at + 1, half * width:(half + 1) * width] = pair[1:2]
        gate, up = gate_at[...], up_at[...]
        sigmoid = 1.0 / (1.0 + jnp.exp(-gate))
        active = gate * sigmoid
        factors[step, 0] = up * sigmoid * (1.0 + gate * (1.0 - sigmoid))
        factors[step, 1] = active
        factors[step, 2] = active * up


def expert_rows(rows, rate, factors, step, weights):
    down, down_other, gate, gate_other, up, up_other = weights
    features = rows.shape[1]
    v = jnp.zeros((rows.shape[0], 2 * down.shape[0]), F32)
    for at in range(0, features, CHUNK):
        part = slice(at, at + CHUNK)
        both = jnp.concatenate([down[:, part], down_other[:, part]], axis=0)
        v = v + lax.dot_general(rows[:, part], both, NT, preferred_element_type=F32)
    scaled = rate * v
    grad_gate = (scaled * factors[step, 0]).astype(BF16)
    grad_up = (scaled * factors[step, 1]).astype(BF16)
    terms = jnp.sum(factors[step, 2] * v, axis=1, keepdims=True)
    grads = jnp.concatenate([grad_gate, grad_up], axis=1)

    def back(part):
        wide = jnp.concatenate(
            [gate[part], gate_other[part], up[part], up_other[part]], axis=1
        )
        return lax.dot_general(grads, wide, NT, preferred_element_type=F32)

    return back, terms


def step_zero_kernel(*refs):
    got, ahead, (routes, positions, factors) = refs[:4], refs[4:8], refs[8:11]
    weights, (rows_out, ahead_out, terms_out, rows_at) = refs[11:17], refs[17:]
    p, z, _ = place()
    take_rows(rows_at, got)
    features = rows_at.shape[1] - META
    rate = rows_at[:, features:features + 1]
    back, terms = expert_rows(rows_at[:, :features].astype(BF16), rate, factors, 0, weights)
    terms_out[...] = jnp.broadcast_to(terms, terms_out.shape)
    for at in range(0, features, CHUNK):
        rows_out[:, at:at + CHUNK] = back(slice(at, at + CHUNK)).astype(BF16)
    keys = keys_of(routes, positions, 0)
    keys = jnp.where(p == 0, -1, keys)
    select = one_hot(keys, labels(PAIRS, lambda k: (z + k) % E_FLY))
    rows_out[:, features:] = select.astype(BF16)
    take_rows(rows_at, ahead)
    ahead_out[...] = rows_at[...].astype(BF16)


def split(value):
    high = value.astype(BF16).astype(F32)
    middle = (value - high).astype(BF16).astype(F32)
    return [high, middle, value - high - middle]


def step_one_kernel(*refs):
    came, (ahead, factors, terms0) = refs[:4], refs[4:7]
    weights, outs = refs[7:13], refs[13:17]
    features = ahead.shape[1] - META
    meta = ahead[:, features:]
    rate = meta[:, E_FLY * PAIRS:E_FLY * PAIRS + 1].astype(F32)
    match = meta[:, :E_FLY * PAIRS]
    everything = jnp.concatenate([ref[:, :features] for ref in came], axis=0)
    rows = ahead[:, :features].astype(F32) + jnp.dot(
        match, everything, preferred_element_type=F32
    )
    back, terms = expert_rows(rows.astype(BF16), rate, factors, 1, weights)
    for at in range(0, features, CHUNK):
        part = back(slice(at, at + CHUNK))
        for k, out in enumerate(outs):
            out[:, at:at + CHUNK] = part[MOST * k:MOST * (k + 1)].astype(BF16)
    meta = first_lanes(split(terms) + split(terms0[:, 0:1]))
    for k, out in enumerate(outs):
        out[:, features:] = meta[MOST * k:MOST * (k + 1)].astype(BF16)


def final_kernel(*refs):
    shifted, routes, positions = refs[:3]
    came, got, (out, prob_out, rows_at, back_at) = refs[3:7], refs[7:11], refs[11:]
    p, z, _ = place()
    features = out.shape[1]
    label = labels(PAIRS, lambda k: (z + k) % E_FLY)
    for k in range(E_FLY):
        rows = came[(E_FLY - k) % E_FLY][MOST * k:MOST * (k + 1), :features]
        rows_at[MOST * k:MOST * (k + 1), :] = rows.astype(F32)
    take_rows(back_at, got)
    select0 = came[0][:, features:]
    keys = [keys_of(routes, positions, step) for step in range(STEPS)]
    select1 = one_hot(keys[1], label).astype(BF16)
    last = p == lax.axis_size("pipe") - 1
    for at in range(0, features, CHUNK):
        part = slice(at, at + CHUNK)
        base = shifted[:, part].astype(F32)
        base = jnp.where(last, 0.0, base)
        base = base + lax.dot_general(
            select0, rows_at[:, part].astype(BF16), TN, preferred_element_type=F32
        )
        base = base.astype(BF16).astype(F32)
        base = base + lax.dot_general(
            select1, back_at[:, part].astype(BF16), TN, preferred_element_type=F32
        )
        out[:, part] = base.astype(BF16)
    meta = back_at[:, features:]
    for step in range(STEPS):
        first = 3 * (STEPS - 1 - step)
        terms = meta[:, first:first + 1] + (meta[:, first + 1:first + 2] + meta[:, first + 2:first + 3])
        for choice, hit in enumerate(hits(keys[step], label)):
            prob_out[step, choice:choice + 1] = jnp.sum(
                jnp.where(hit, terms, 0.0), axis=0, keepdims=True
            )


def local_chip(out_grad, routes, positions, route_probs, saved_acts, w_gate, w_up, w_down):
    sections = lax.axis_size("pipe")
    devices = lax.axis_size("expert")
    grad = out_grad[0]
    tokens, features = grad.shape
    width = features + META
    routes = routes[0].transpose(0, 2, 1)
    positions = positions[0].transpose(0, 2, 1)
    probs = route_probs[0].transpose(0, 2, 1)
    acts = saved_acts[0]
    hidden = 2 * acts.shape[-1]

    def across(block):
        return lax.ppermute(block, "expert", [(i, i ^ 1) for i in range(devices)])

    def along(block, k):
        if k % E_FLY == 0:
            return block
        return lax.ppermute(
            block, "expert", [(i, (i + 2 * k) % devices) for i in range(devices)]
        )

    def relay(block, distance):
        route = [(i, (i + distance) % sections) for i in range(sections)]
        return lax.ppermute(block, "pipe", route)

    pair = jax.ShapeDtypeStruct((MOST, width), BF16)
    block = jax.ShapeDtypeStruct((PAIRS, width), BF16)
    row_scratch = pltpu.VMEM((PAIRS, width), F32)

    picked = call(
        pick_kernel, "pick_rows", [pair] * E_FLY + [jax.ShapeDtypeStruct((4, tokens), F32)]
    )(grad, routes, positions, probs)
    got = [along(picked[k], k) for k in range(E_FLY)]
    table = relay(picked[E_FLY], 1)
    weights = []
    for array in (w_down[0], w_gate[0], w_up[0]):
        weights += [array, across(array)]
    acts_other = across(acts)
    shifted = relay(grad, -1)
    *ahead, factors = call(
        ahead_kernel,
        "rows_ahead",
        [pair] * E_FLY + [jax.ShapeDtypeStruct((STEPS, 3, PAIRS, hidden), F32)],
        [pltpu.VMEM((PAIRS, hidden), F32)] * 2,
    )(grad, routes, positions, table, acts, acts_other)
    ahead = [along(ahead[k], k) for k in range(E_FLY)]
    rows, ahead_rows, terms0 = call(
        step_zero_kernel,
        "step_zero",
        [block, block, jax.ShapeDtypeStruct((PAIRS, META), F32)],
        [row_scratch],
    )(*got, *ahead, routes, positions, factors, *weights)
    came = relay(rows, -1)
    ahead_rows = relay(ahead_rows, -1)
    came = [along(came, j) for j in range(E_FLY)]
    back = call(step_one_kernel, "step_one", [pair] * E_FLY)(
        *came, ahead_rows, factors, terms0, *weights
    )
    back = [along(back[k], E_FLY - k) for k in range(E_FLY)]
    result, prob = call(
        final_kernel,
        "final_sums",
        [
            jax.ShapeDtypeStruct((tokens, features), BF16),
            jax.ShapeDtypeStruct((STEPS, 2, tokens), F32),
        ],
        [pltpu.VMEM((PAIRS, features), F32), row_scratch],
    )(shifted, routes, positions, *came, *back)
    return result[None], prob.transpose(0, 2, 1)[None]


def shifted(block, axis, distance):
    devices = range(lax.axis_size(axis))
    route = [(i - distance, i) for i in devices if i - distance in devices]
    return lax.ppermute(block, axis, route)


def pair_table(route_part, place_part):
    labels = jnp.arange(E_FLY * MOST, dtype=jnp.int32)
    pair_keys = jnp.where(place_part >= 0, route_part * MOST + place_part, -1)
    return (pair_keys.T[:, None, :] == labels[None, :, None]).astype(jnp.float32)


def assemble(current, onehot, contrib):
    select = (onehot[0] + onehot[1]).astype(jnp.bfloat16)
    delta = lax.dot_general(
        select, contrib, (((0,), (0,)), ((), ())), preferred_element_type=jnp.float32
    )
    return (current.astype(jnp.float32) + delta).astype(jnp.bfloat16)


def expert_back(slot_rows, slot_rates, stored, gate_weight, up_weight, down_weight):
    downward = lax.dot_general(
        slot_rows, down_weight, (((1,), (1,)), ((), ())), preferred_element_type=jnp.float32
    )
    gate_pre = stored[:, 0, :].astype(jnp.float32)
    upward = stored[:, 1, :].astype(jnp.float32)
    sigmoid_gate = jax.nn.sigmoid(gate_pre)
    active = gate_pre * sigmoid_gate
    hidden = active * upward
    scaled = slot_rates.astype(jnp.float32)[:, None] * downward
    grad_gate = (scaled * upward * sigmoid_gate * (1.0 + gate_pre * (1.0 - sigmoid_gate))).astype(
        jnp.bfloat16
    )
    grad_up = (scaled * active).astype(jnp.bfloat16)
    prob_terms = jnp.sum(hidden * downward, axis=1)
    back_rows = lax.dot_general(
        grad_gate, gate_weight, (((1,), (1,)), ((), ())), preferred_element_type=jnp.float32
    )
    back_rows = back_rows + lax.dot_general(
        grad_up, up_weight, (((1,), (1,)), ((), ())), preferred_element_type=jnp.float32
    )
    return (back_rows, prob_terms)


def local_general(out_grad, routes, positions, route_probs, saved_acts, w_gate, w_up, w_down):
    devices = lax.axis_size("expert")
    members = devices // E_FLY
    pair_count = E_FLY * MOST
    gate_weight = w_gate[0]
    up_weight = w_up[0]
    down_weight = w_down[0]
    current_grad = out_grad[0]
    features = current_grad.shape[1]
    final_grad = current_grad
    prob_rows = []
    for step_index in range(STEPS):
        route_part = routes[0, step_index]
        place_part = positions[0, step_index]
        rate_part = route_probs[0, step_index]
        onehot = pair_table(route_part, place_part)
        select = (onehot[0] + onehot[1]).astype(jnp.bfloat16)
        send_rows = jnp.dot(select, current_grad, preferred_element_type=jnp.float32).astype(
            jnp.bfloat16
        )
        send_rates = jnp.sum(
            onehot * rate_part.T.astype(jnp.float32)[:, None, :], axis=(0, 2)
        ).astype(jnp.bfloat16)
        out_rows = jnp.broadcast_to(
            send_rows.reshape(E_FLY, 1, MOST, features), (E_FLY, members, MOST, features)
        ).reshape(devices, MOST, features)
        out_rates = jnp.broadcast_to(
            send_rates.reshape(E_FLY, 1, MOST), (E_FLY, members, MOST)
        ).reshape(devices, MOST)
        got_rows, got_rates = (
            lax.all_to_all(out_rows, "expert", split_axis=0, concat_axis=0, tiled=True),
            lax.all_to_all(out_rates, "expert", split_axis=0, concat_axis=0, tiled=True),
        )
        back_rows, prob_terms = expert_back(
            got_rows.reshape(devices * MOST, features),
            got_rates.reshape(devices * MOST),
            saved_acts[0, step_index],
            gate_weight,
            up_weight,
            down_weight,
        )
        back_rows = back_rows.reshape(devices, MOST, features)
        prob_terms = prob_terms.reshape(devices, MOST)
        came_rows, came_terms = (
            lax.all_to_all(back_rows, "expert", split_axis=0, concat_axis=0, tiled=True),
            lax.all_to_all(prob_terms, "expert", split_axis=0, concat_axis=0, tiled=True),
        )
        contrib = (
            jnp.sum(came_rows.reshape(E_FLY, members, MOST, features), axis=1)
            .astype(jnp.bfloat16)
            .reshape(pair_count, features)
        )
        slot_terms = jnp.sum(came_terms.reshape(E_FLY, members, MOST), axis=1).reshape(pair_count)
        prob_rows.append(jnp.sum(onehot * slot_terms[None, :, None], axis=1).T)
        if step_index + 1 < STEPS:
            current_grad = shifted(assemble(current_grad, onehot, contrib), "pipe", -1)
        else:
            final_grad = assemble(current_grad, onehot, contrib)
    return (final_grad[None], jnp.stack(prob_rows, axis=0)[None])


def solution(mesh):
    in_specs = (
        P("pipe", "expert", None),
        P("pipe", None, "expert", None),
        P("pipe", None, "expert", None),
        P("pipe", None, "expert", None),
        P("pipe", None, None, None, "expert"),
        P("pipe", None, "expert"),
        P("pipe", None, "expert"),
        P("pipe", "expert", None),
    )
    out_specs = (P("pipe", "expert", None), P("pipe", None, "expert", None))
    one_chip = mesh.shape["expert"] == 2 * E_FLY
    local = local_chip if one_chip else local_general
    return jax.shard_map(local, mesh=mesh, in_specs=in_specs, out_specs=out_specs, check_vma=False)
```

```python
import functools

import jax
import jax.numpy as jnp
from jax import lax
from jax.experimental import pallas as pl
from jax.experimental.pallas import tpu as pltpu
from jax.sharding import PartitionSpec as P

E_FLY = 4
MOST = 2
STEPS = 2
PAIRS = E_FLY * MOST
META = 128
CHUNK = 256
COST0 = 20_000_000_000
COST1 = 0
COST2 = 20_000_000_000
COST3 = 20_000_000_000
LIMIT = 50
F32 = jnp.float32
BF16 = jnp.bfloat16
NT = (((1,), (1,)), ((), ()))
TN = (((0,), (0,)), ((), ()))


def call(kernel, name, out_shape, scratch=(), hbm=0, operands=0, limit=24, cost=0):
    specs = [pl.BlockSpec(memory_space=pl.ANY)] * hbm
    specs += [pl.BlockSpec(memory_space=pltpu.VMEM)] * (operands - hbm)
    return pl.pallas_call(
        kernel,
        name=name,
        out_shape=out_shape,
        in_specs=specs,
        scratch_shapes=list(scratch),
        cost_estimate=pl.CostEstimate(flops=cost, bytes_accessed=0, transcendentals=0),
        compiler_params=pltpu.CompilerParams(vmem_limit_bytes=limit * 2**20),
    )


def place():
    at = lax.axis_index("expert")
    return lax.axis_index("pipe"), at // 2, at % 2


def keys_of(routes, positions, step):
    return jnp.where(positions[step] >= 0, routes[step] * MOST + positions[step], -1)


def labels(rows, expert_of):
    row = lax.broadcasted_iota(jnp.int32, (rows, 1), 0)
    return expert_of(row // MOST) * MOST + row % MOST


def hits(keys, label):
    return keys[0:1] == label, keys[1:2] == label


def one_hot(keys, label):
    first, second = hits(keys, label)
    return jnp.where(first | second, 1.0, 0.0).astype(F32)


def rates_of(keys, rates, label):
    first, second = hits(keys, label)
    picked = jnp.where(first, rates[0:1], 0.0) + jnp.where(second, rates[1:2], 0.0)
    return jnp.sum(picked, axis=1, keepdims=True)


def first_lanes(columns):
    lane = lax.broadcasted_iota(jnp.int32, (columns[0].shape[0], META), 1)
    out = jnp.zeros(lane.shape, F32)
    for index, column in enumerate(columns):
        out = jnp.where(lane == index, column, out)
    return out


def put_rows(outs, rows, meta):
    width = rows.shape[1]
    for k, out in enumerate(outs):
        out[:, :width] = rows[MOST * k:MOST * (k + 1)].astype(BF16)
        out[:, width:] = meta[MOST * k:MOST * (k + 1)].astype(BF16)


def take_rows(scratch, refs):
    for k, ref in enumerate(refs):
        scratch[MOST * k:MOST * (k + 1), :] = ref[...].astype(F32)


def table_kernel(routes, positions, probs, table):
    table[0:2] = keys_of(routes, positions, 1).astype(F32)
    table[2:4] = probs[1].astype(F32)


def pick_kernel(grad, routes, positions, probs, *outs):
    _, z, _ = place()
    keys = keys_of(routes, positions, 0)
    label = labels(PAIRS, lambda k: (z + k) % E_FLY)
    select = one_hot(keys, label)
    rows = jnp.dot(select.astype(BF16), grad[...], preferred_element_type=F32)
    rate = rates_of(keys, probs[0].astype(F32), label)
    put_rows(outs, rows, first_lanes([rate]))


def rows_ahead(grad, routes, positions, table, rows_out):
    p, z, c = place()
    keys0 = keys_of(routes, positions, 0)
    keys1 = table[0:2].astype(jnp.int32)
    keys1 = jnp.where(p == 0, -1, keys1)
    label = labels(PAIRS, lambda k: (z + k) % E_FLY)
    select = one_hot(keys1, label)
    rows = jnp.dot(select.astype(BF16), grad[...], preferred_element_type=F32)
    rate = rates_of(keys1, table[2:4], label)
    lane = lax.broadcasted_iota(jnp.int32, (PAIRS, META), 1)
    meta = jnp.where(lane == E_FLY * PAIRS, rate, 0.0)
    column = lax.broadcasted_iota(jnp.int32, (META, 1), 0)
    source, block, spot = column // PAIRS, column // MOST % E_FLY, column % MOST
    row = lax.broadcasted_iota(jnp.int32, (PAIRS, 1), 0)
    for k in range(E_FLY):
        expert = (z + k + E_FLY - source) % E_FLY
        own = (source < E_FLY) & ((source + block) % E_FLY == k)
        step0 = one_hot(keys0, jnp.where(own, expert * MOST + spot, -2))
        match = lax.dot_general(
            select.astype(BF16), step0.astype(BF16), NT, preferred_element_type=F32
        )
        meta = meta + jnp.where(row // MOST == k, match, 0.0)
    features = rows.shape[1]
    rows_out[PAIRS:, :features] = rows.astype(BF16)
    rows_out[PAIRS:, features:] = meta.astype(BF16)
    taken = one_hot(jnp.where(p == 0, -1, keys0), label)
    rows_out[:PAIRS, features:] = taken.astype(BF16)


def act_factors(acts, acts_other, factors, rows_at):
    _, z, c = place()
    steps, slots, _, width = acts.shape
    for half, ref in enumerate((acts, acts_other)):
        for at in range(steps * slots):
            rows_at[2 * at:2 * at + 2, half * width:(half + 1) * width] = ref[
                at // slots, at % slots
            ].astype(F32)
    stored = rows_at[...].astype(BF16)
    row = lax.broadcasted_iota(jnp.int32, (2 * steps * PAIRS, 2 * steps * slots), 0)
    column = lax.broadcasted_iota(jnp.int32, row.shape, 1)
    group, k, spot = row // PAIRS, row // MOST % E_FLY, row % MOST
    slot = (2 * ((z + E_FLY - k) % E_FLY) + c) * MOST + spot
    wanted = 2 * (group // 2 * slots + slot) + group % 2
    pick = jnp.where(column == wanted, 1.0, 0.0).astype(BF16)
    picked = jnp.dot(pick, stored, preferred_element_type=F32)
    for step in range(steps):
        gate = picked[2 * step * PAIRS:(2 * step + 1) * PAIRS]
        up = picked[(2 * step + 1) * PAIRS:(2 * step + 2) * PAIRS]
        sigmoid = 1.0 / (1.0 + jnp.exp(-gate))
        active = gate * sigmoid
        factors[step, 0] = up * sigmoid * (1.0 + gate * (1.0 - sigmoid))
        factors[step, 1] = active
        factors[step, 2] = active * up


def prepare_kernel(*refs):
    grad, *weights = refs[:4]
    (routes, positions, table, acts, acts_other), (rows_out, factors) = refs[4:9], refs[9:11]
    held, (grad_at, rows_at, sems) = refs[11:14], refs[14:]
    copies = [
        pltpu.make_async_copy(source, target, sems.at[index])
        for index, (source, target) in enumerate(zip((grad, *weights), (grad_at, *held)))
    ]
    for copy in copies:
        copy.start()
    act_factors(acts, acts_other, factors, rows_at)
    copies[0].wait()
    rows_ahead(grad_at, routes, positions, table, rows_out)
    for copy in copies[1:]:
        copy.wait()


def expert_rows(rows, rate, factors, step, weights):
    down, down_other, gate, gate_other, up, up_other = weights
    features = rows.shape[1]
    v = jnp.zeros((rows.shape[0], 2 * down.shape[0]), F32)
    for at in range(0, features, CHUNK):
        part = slice(at, at + CHUNK)
        both = jnp.concatenate([down[:, part], down_other[:, part]], axis=0)
        v = v + lax.dot_general(rows[:, part], both, NT, preferred_element_type=F32)
    scaled = rate * v
    grads = jnp.concatenate(
        [(scaled * factors[step, 0]).astype(BF16), (scaled * factors[step, 1]).astype(BF16)],
        axis=1,
    )
    terms = jnp.sum(factors[step, 2] * v, axis=1, keepdims=True)

    def back(at):
        part = slice(at, at + CHUNK)
        wide = jnp.concatenate(
            [gate[part], gate_other[part], up[part], up_other[part]], axis=1
        )
        return part, lax.dot_general(grads, wide, NT, preferred_element_type=F32)

    return [functools.partial(back, at) for at in range(0, features, CHUNK)], terms


def step_zero_kernel(*refs):
    got, (factors, ahead), weights = refs[:4], refs[4:6], refs[6:12]
    rows_out, terms_out, rows_at = refs[12:]
    take_rows(rows_at, got)
    features = rows_at.shape[1] - META
    rate = rows_at[:, features:features + 1]
    backs, terms = expert_rows(rows_at[:, :features].astype(BF16), rate, factors, 0, weights)
    terms_out[...] = jnp.broadcast_to(terms, terms_out.shape)
    for back in backs:
        part, value = back()
        rows_out[:PAIRS, part] = value.astype(BF16)
    rows_out[:PAIRS, features:] = ahead[:PAIRS, features:]
    rows_out[PAIRS:] = ahead[PAIRS:]


def merge_kernel(came, *outs):
    for k, out in enumerate(outs):
        first = PAIRS + MOST * (k + 1)
        out[:PAIRS] = came[:PAIRS]
        out[PAIRS:] = came[first:first + MOST]


def split(value):
    high = value.astype(BF16).astype(F32)
    middle = (value - high).astype(BF16).astype(F32)
    return [high, middle, value - high - middle]


def step_one_kernel(*refs):
    came, (factors, terms0), weights = refs[:4], refs[4:6], refs[6:12]
    outs, ahead_at = refs[12:16], refs[16]
    features = ahead_at.shape[1] - META
    for k in range(E_FLY):
        ahead_at[MOST * k:MOST * (k + 1), :] = came[k][PAIRS:PAIRS + MOST, :].astype(F32)
    meta = ahead_at[:, features:]
    rate = meta[:, E_FLY * PAIRS:E_FLY * PAIRS + 1]
    match = meta[:, :E_FLY * PAIRS].astype(BF16)
    everything = jnp.concatenate([ref[:PAIRS, :features] for ref in came], axis=0)
    rows = ahead_at[:, :features] + jnp.dot(match, everything, preferred_element_type=F32)
    backs, terms = expert_rows(rows.astype(BF16), rate, factors, 1, weights)
    for back in backs:
        part, value = back()
        for k, out in enumerate(outs):
            out[:, part] = value[MOST * k:MOST * (k + 1)].astype(BF16)
    meta = first_lanes(split(terms) + split(terms0[:, 0:1]))
    for k, out in enumerate(outs):
        out[:, features:] = meta[MOST * k:MOST * (k + 1)].astype(BF16)


def final_kernel(*refs):
    shifted, routes, positions = refs[:3]
    came, got, (out, prob_out, rows_at, back_at) = refs[3:7], refs[7:11], refs[11:]
    p, z, _ = place()
    features = out.shape[1]
    label = labels(PAIRS, lambda k: (z + k) % E_FLY)
    for k in range(E_FLY):
        rows = came[(E_FLY - k) % E_FLY][MOST * k:MOST * (k + 1), :features]
        rows_at[MOST * k:MOST * (k + 1), :] = rows.astype(F32)
    take_rows(back_at, got)
    select0 = came[0][:PAIRS, features:]
    keys = [keys_of(routes, positions, step) for step in range(STEPS)]
    select1 = one_hot(keys[1], label).astype(BF16)
    last = p == lax.axis_size("pipe") - 1
    for at in range(0, features, CHUNK):
        part = slice(at, at + CHUNK)
        base = shifted[:, part].astype(F32)
        base = jnp.where(last, 0.0, base)
        base = base + lax.dot_general(
            select0, rows_at[:, part].astype(BF16), TN, preferred_element_type=F32
        )
        base = base.astype(BF16).astype(F32)
        base = base + lax.dot_general(
            select1, back_at[:, part].astype(BF16), TN, preferred_element_type=F32
        )
        out[:, part] = base.astype(BF16)
    meta = back_at[:, features:]
    for step in range(STEPS):
        first = 3 * (STEPS - 1 - step)
        terms = meta[:, first:first + 1] + (meta[:, first + 1:first + 2] + meta[:, first + 2:first + 3])
        for choice, hit in enumerate(hits(keys[step], label)):
            prob_out[step, choice:choice + 1] = jnp.sum(
                jnp.where(hit, terms, 0.0), axis=0, keepdims=True
            )


def local_chip(out_grad, routes, positions, route_probs, saved_acts, w_gate, w_up, w_down):
    sections = lax.axis_size("pipe")
    devices = lax.axis_size("expert")
    grad = out_grad[0]
    tokens, features = grad.shape
    width = features + META
    routes = routes[0].transpose(0, 2, 1)
    positions = positions[0].transpose(0, 2, 1)
    probs = route_probs[0].transpose(0, 2, 1)
    acts = saved_acts[0]
    hidden = 2 * acts.shape[-1]

    def across(block):
        return lax.ppermute(block, "expert", [(i, i ^ 1) for i in range(devices)])

    def along(block, k):
        if k % E_FLY == 0:
            return block
        return lax.ppermute(
            block, "expert", [(i, (i + 2 * k) % devices) for i in range(devices)]
        )

    def relay(block, distance):
        route = [(i, (i + distance) % sections) for i in range(sections)]
        return lax.ppermute(block, "pipe", route)

    pair = jax.ShapeDtypeStruct((MOST, width), BF16)
    block = jax.ShapeDtypeStruct((PAIRS, width), BF16)
    wide = jax.ShapeDtypeStruct((PAIRS + MOST, width), BF16)
    row_scratch = pltpu.VMEM((PAIRS, width), F32)

    acts_other = across(acts)
    weights = []
    for array in (w_down[0], w_gate[0], w_up[0]):
        weights += [array, across(array)]
    table = call(
        table_kernel, "next_table", jax.ShapeDtypeStruct((4, tokens), F32), operands=3
    )(routes, positions, probs)
    table = relay(table, 1)
    picked = list(
        call(pick_kernel, "pick_rows", [pair] * E_FLY, operands=4)(
            grad, routes, positions, probs
        )
    )
    acts_other, picked[1] = lax.optimization_barrier((acts_other, picked[1]))
    weights[1], picked[2] = lax.optimization_barrier((weights[1], picked[2]))
    weights[3], picked[3] = lax.optimization_barrier((weights[3], picked[3]))
    got = [along(picked[k], k) for k in range(E_FLY)]
    own = weights[::2]
    ahead, factors, *own = call(
        prepare_kernel,
        "prepare",
        [pltpu.VMEM((2 * PAIRS, width), BF16), pltpu.VMEM((STEPS, 3, PAIRS, hidden), F32)]
        + [pltpu.VMEM(array.shape, BF16) for array in own],
        [
            pltpu.VMEM(grad.shape, BF16),
            pltpu.VMEM((2 * acts.shape[0] * acts.shape[1], hidden), F32),
            pltpu.SemaphoreType.DMA((4,)),
        ],
        hbm=4,
        operands=9,
        limit=LIMIT,
        cost=COST3,
    )(grad, *own, routes, positions, table, acts, acts_other)
    weights[::2] = own
    rows, terms0 = call(
        step_zero_kernel,
        "step_zero",
        [
            jax.ShapeDtypeStruct((2 * PAIRS, width), BF16),
            jax.ShapeDtypeStruct((PAIRS, META), F32),
        ],
        [row_scratch],
        operands=12,
        cost=COST0,
    )(*got, factors, ahead, *weights)
    came = relay(rows, -1)
    shifted, rows = lax.optimization_barrier((grad, rows))
    shifted = relay(shifted, -1)
    sends = call(merge_kernel, "merge", [wide] * (E_FLY - 1), operands=1, cost=COST2)(came)
    came = [came] + [along(send, k + 1) for k, send in enumerate(sends)]
    back = call(
        step_one_kernel, "step_one", [pair] * E_FLY, [row_scratch], operands=12, cost=COST1
    )(*came, factors, terms0, *weights)
    back = [along(back[k], E_FLY - k) for k in range(E_FLY)]
    result, prob = call(
        final_kernel,
        "final_sums",
        [
            jax.ShapeDtypeStruct((tokens, features), BF16),
            jax.ShapeDtypeStruct((STEPS, 2, tokens), F32),
        ],
        [pltpu.VMEM((PAIRS, features), F32), row_scratch],
        operands=11,
    )(shifted, routes, positions, *came, *back)
    return result[None], prob.transpose(0, 2, 1)[None]


def shifted(block, axis, distance):
    devices = range(lax.axis_size(axis))
    route = [(i - distance, i) for i in devices if i - distance in devices]
    return lax.ppermute(block, axis, route)


def pair_table(route_part, place_part):
    labels = jnp.arange(E_FLY * MOST, dtype=jnp.int32)
    pair_keys = jnp.where(place_part >= 0, route_part * MOST + place_part, -1)
    return (pair_keys.T[:, None, :] == labels[None, :, None]).astype(jnp.float32)


def assemble(current, onehot, contrib):
    select = (onehot[0] + onehot[1]).astype(jnp.bfloat16)
    delta = lax.dot_general(
        select, contrib, (((0,), (0,)), ((), ())), preferred_element_type=jnp.float32
    )
    return (current.astype(jnp.float32) + delta).astype(jnp.bfloat16)


def expert_back(slot_rows, slot_rates, stored, gate_weight, up_weight, down_weight):
    downward = lax.dot_general(
        slot_rows, down_weight, (((1,), (1,)), ((), ())), preferred_element_type=jnp.float32
    )
    gate_pre = stored[:, 0, :].astype(jnp.float32)
    upward = stored[:, 1, :].astype(jnp.float32)
    sigmoid_gate = jax.nn.sigmoid(gate_pre)
    active = gate_pre * sigmoid_gate
    hidden = active * upward
    scaled = slot_rates.astype(jnp.float32)[:, None] * downward
    grad_gate = (scaled * upward * sigmoid_gate * (1.0 + gate_pre * (1.0 - sigmoid_gate))).astype(
        jnp.bfloat16
    )
    grad_up = (scaled * active).astype(jnp.bfloat16)
    prob_terms = jnp.sum(hidden * downward, axis=1)
    back_rows = lax.dot_general(
        grad_gate, gate_weight, (((1,), (1,)), ((), ())), preferred_element_type=jnp.float32
    )
    back_rows = back_rows + lax.dot_general(
        grad_up, up_weight, (((1,), (1,)), ((), ())), preferred_element_type=jnp.float32
    )
    return (back_rows, prob_terms)


def local_general(out_grad, routes, positions, route_probs, saved_acts, w_gate, w_up, w_down):
    devices = lax.axis_size("expert")
    members = devices // E_FLY
    pair_count = E_FLY * MOST
    gate_weight = w_gate[0]
    up_weight = w_up[0]
    down_weight = w_down[0]
    current_grad = out_grad[0]
    features = current_grad.shape[1]
    final_grad = current_grad
    prob_rows = []
    for step_index in range(STEPS):
        route_part = routes[0, step_index]
        place_part = positions[0, step_index]
        rate_part = route_probs[0, step_index]
        onehot = pair_table(route_part, place_part)
        select = (onehot[0] + onehot[1]).astype(jnp.bfloat16)
        send_rows = jnp.dot(select, current_grad, preferred_element_type=jnp.float32).astype(
            jnp.bfloat16
        )
        send_rates = jnp.sum(
            onehot * rate_part.T.astype(jnp.float32)[:, None, :], axis=(0, 2)
        ).astype(jnp.bfloat16)
        out_rows = jnp.broadcast_to(
            send_rows.reshape(E_FLY, 1, MOST, features), (E_FLY, members, MOST, features)
        ).reshape(devices, MOST, features)
        out_rates = jnp.broadcast_to(
            send_rates.reshape(E_FLY, 1, MOST), (E_FLY, members, MOST)
        ).reshape(devices, MOST)
        got_rows, got_rates = (
            lax.all_to_all(out_rows, "expert", split_axis=0, concat_axis=0, tiled=True),
            lax.all_to_all(out_rates, "expert", split_axis=0, concat_axis=0, tiled=True),
        )
        back_rows, prob_terms = expert_back(
            got_rows.reshape(devices * MOST, features),
            got_rates.reshape(devices * MOST),
            saved_acts[0, step_index],
            gate_weight,
            up_weight,
            down_weight,
        )
        back_rows = back_rows.reshape(devices, MOST, features)
        prob_terms = prob_terms.reshape(devices, MOST)
        came_rows, came_terms = (
            lax.all_to_all(back_rows, "expert", split_axis=0, concat_axis=0, tiled=True),
            lax.all_to_all(prob_terms, "expert", split_axis=0, concat_axis=0, tiled=True),
        )
        contrib = (
            jnp.sum(came_rows.reshape(E_FLY, members, MOST, features), axis=1)
            .astype(jnp.bfloat16)
            .reshape(pair_count, features)
        )
        slot_terms = jnp.sum(came_terms.reshape(E_FLY, members, MOST), axis=1).reshape(pair_count)
        prob_rows.append(jnp.sum(onehot * slot_terms[None, :, None], axis=1).T)
        if step_index + 1 < STEPS:
            current_grad = shifted(assemble(current_grad, onehot, contrib), "pipe", -1)
        else:
            final_grad = assemble(current_grad, onehot, contrib)
    return (final_grad[None], jnp.stack(prob_rows, axis=0)[None])


def solution(mesh):
    in_specs = (
        P("pipe", "expert", None),
        P("pipe", None, "expert", None),
        P("pipe", None, "expert", None),
        P("pipe", None, "expert", None),
        P("pipe", None, None, None, "expert"),
        P("pipe", None, "expert"),
        P("pipe", None, "expert"),
        P("pipe", "expert", None),
    )
    out_specs = (P("pipe", "expert", None), P("pipe", None, "expert", None))
    one_chip = mesh.shape["expert"] == 2 * E_FLY
    local = local_chip if one_chip else local_general
    return jax.shard_map(local, mesh=mesh, in_specs=in_specs, out_specs=out_specs, check_vma=False)
```

```python
import functools

import jax
import jax.numpy as jnp
from jax import lax
from jax.experimental import pallas as pl
from jax.experimental.pallas import tpu as pltpu
from jax.sharding import PartitionSpec as P

E_FLY = 4
MOST = 2
STEPS = 2
PAIRS = E_FLY * MOST
META = 128
CHUNK = 256
SPAN = 1024
COST0 = 20_000_000_000
COST1 = 0
COST2 = 20_000_000_000
COST3 = 20_000_000_000
LIMIT = 54
F32 = jnp.float32
BF16 = jnp.bfloat16
NT = (((1,), (1,)), ((), ()))
TN = (((0,), (0,)), ((), ()))


def call(kernel, name, out_shape, scratch=(), hbm=0, operands=0, limit=24, cost=0):
    specs = [pl.BlockSpec(memory_space=pl.ANY)] * hbm
    specs += [pl.BlockSpec(memory_space=pltpu.VMEM)] * (operands - hbm)
    return pl.pallas_call(
        kernel,
        name=name,
        out_shape=out_shape,
        in_specs=specs,
        scratch_shapes=list(scratch),
        cost_estimate=pl.CostEstimate(flops=cost, bytes_accessed=0, transcendentals=0),
        compiler_params=pltpu.CompilerParams(vmem_limit_bytes=limit * 2**20),
    )


def place():
    at = lax.axis_index("expert")
    return lax.axis_index("pipe"), at // 2, at % 2


def keys_of(routes, positions, step):
    return jnp.where(positions[step] >= 0, routes[step] * MOST + positions[step], -1)


def labels(rows, expert_of):
    row = lax.broadcasted_iota(jnp.int32, (rows, 1), 0)
    return expert_of(row // MOST) * MOST + row % MOST


def hits(keys, label):
    return keys[0:1] == label, keys[1:2] == label


def one_hot(keys, label):
    first, second = hits(keys, label)
    return jnp.where(first | second, 1.0, 0.0).astype(F32)


def rates_of(keys, rates, label):
    first, second = hits(keys, label)
    picked = jnp.where(first, rates[0:1], 0.0) + jnp.where(second, rates[1:2], 0.0)
    return jnp.sum(picked, axis=1, keepdims=True)


def first_lanes(columns):
    lane = lax.broadcasted_iota(jnp.int32, (columns[0].shape[0], META), 1)
    out = jnp.zeros(lane.shape, F32)
    for index, column in enumerate(columns):
        out = jnp.where(lane == index, column, out)
    return out


def bring(sources, targets, sems):
    copies = [
        pltpu.make_async_copy(source, target, sems.at[index])
        for index, (source, target) in enumerate(zip(sources, targets))
    ]
    for copy in copies:
        copy.start()
    return copies


def put_rows(outs, rows, meta):
    width = rows.shape[1]
    for k, out in enumerate(outs):
        out[:, :width] = rows[MOST * k:MOST * (k + 1)].astype(BF16)
        out[:, width:] = meta[MOST * k:MOST * (k + 1)].astype(BF16)


def take_rows(scratch, refs):
    for k, ref in enumerate(refs):
        scratch[MOST * k:MOST * (k + 1), :] = ref[...].astype(F32)


def pick_kernel(*refs):
    outs, (table, *weights), held, sems = refs[7:11], refs[11:15], refs[15:19], refs[19]
    copies = bring(refs[:7], (*held, *weights), sems)
    routes, positions, probs, grad = held
    for copy in copies[:3]:
        copy.wait()
    _, z, _ = place()
    keys = keys_of(routes, positions, 0)
    label = labels(PAIRS, lambda k: z ^ k)
    select = one_hot(keys, label)
    rate = rates_of(keys, probs[0].astype(F32), label)
    table[0:2] = keys_of(routes, positions, 1).astype(F32)
    table[2:4] = probs[1].astype(F32)
    copies[3].wait()
    rows = jnp.dot(select.astype(BF16), grad[...], preferred_element_type=F32)
    put_rows(outs, rows, first_lanes([rate]))
    for copy in copies[4:]:
        copy.wait()


def ahead_kernel(grad, routes, positions, table, done, rows_out, held, packed):
    p, z, c = place()
    keys0 = keys_of(routes, positions, 0)
    keys1 = table[0:2].astype(jnp.int32)
    keys1 = jnp.where(p == 0, -1, keys1)
    label = labels(PAIRS, lambda k: z ^ k)
    select = one_hot(keys1, label)
    rows = jnp.dot(select.astype(BF16), grad[...], preferred_element_type=F32)
    rate = rates_of(keys1, table[2:4], label)
    lane = lax.broadcasted_iota(jnp.int32, (PAIRS, META), 1)
    meta = jnp.where(lane == E_FLY * PAIRS, rate, 0.0)
    column = lax.broadcasted_iota(jnp.int32, (META, 1), 0)
    source, block, spot = column // PAIRS, column // MOST % E_FLY, column % MOST
    row = lax.broadcasted_iota(jnp.int32, (PAIRS, 1), 0)
    for k in range(E_FLY):
        expert = z ^ k ^ source
        own = (source < E_FLY) & (source ^ block == k)
        step0 = one_hot(keys0, jnp.where(own, expert * MOST + spot, -2))
        match = lax.dot_general(
            select.astype(BF16), step0.astype(BF16), NT, preferred_element_type=F32
        )
        meta = meta + jnp.where(row // MOST == k, match, 0.0)
    features = rows.shape[1]
    width = features + META
    rows_out[:, :features] = done[...]
    taken = one_hot(jnp.where(p == 0, -1, keys0), label)
    rows_out[:, features:width] = taken.astype(BF16)
    held[:, :features] = rows
    held[:, features:width] = meta
    parts = PAIRS // MOST
    for at in range(PAIRS):
        k, spot = at // MOST, at % MOST
        for part in range(parts):
            piece = held[at:at + 1, part * SPAN:(part + 1) * SPAN]
            packed[parts * spot + part:parts * spot + part + 1, k * SPAN:(k + 1) * SPAN] = piece
    rows_out[:, width:] = packed[...].astype(BF16)


def factor_kernel(acts, acts_other, factors, rows_at):
    _, z, c = place()
    steps, slots, _, width = acts.shape
    for half, ref in enumerate((acts, acts_other)):
        for at in range(steps * slots):
            rows_at[2 * at:2 * at + 2, half * width:(half + 1) * width] = ref[
                at // slots, at % slots
            ].astype(F32)
    stored = rows_at[...].astype(BF16)
    row = lax.broadcasted_iota(jnp.int32, (2 * steps * PAIRS, 2 * steps * slots), 0)
    column = lax.broadcasted_iota(jnp.int32, row.shape, 1)
    group, k, spot = row // PAIRS, row // MOST % E_FLY, row % MOST
    slot = (2 * (z ^ k) + c) * MOST + spot
    wanted = 2 * (group // 2 * slots + slot) + group % 2
    pick = jnp.where(column == wanted, 1.0, 0.0).astype(BF16)
    picked = jnp.dot(pick, stored, preferred_element_type=F32)
    for step in range(steps):
        gate = picked[2 * step * PAIRS:(2 * step + 1) * PAIRS]
        up = picked[(2 * step + 1) * PAIRS:(2 * step + 2) * PAIRS]
        sigmoid = 1.0 / (1.0 + jnp.exp(-gate))
        active = gate * sigmoid
        factors[step, 0] = up * sigmoid * (1.0 + gate * (1.0 - sigmoid))
        factors[step, 1] = active
        factors[step, 2] = active * up


def expert_rows(rows, rate, factors, step, weights):
    down, gate, up = weights[:2], weights[2:4], weights[4:]
    v = jnp.concatenate(
        [lax.dot_general(ref[...], rows, NT, preferred_element_type=F32).T for ref in down],
        axis=1,
    )
    scaled = rate * v
    grads = jnp.concatenate(
        [(scaled * factors[step, 0]).astype(BF16), (scaled * factors[step, 1]).astype(BF16)],
        axis=1,
    )
    terms = jnp.sum(factors[step, 2] * v, axis=1, keepdims=True)

    def back(at):
        part = slice(at, at + CHUNK)
        wide = jnp.concatenate([ref[part] for ref in (*gate, *up)], axis=1)
        return part, lax.dot_general(wide, grads, NT, preferred_element_type=F32).T

    return [functools.partial(back, at) for at in range(0, rows.shape[1], CHUNK)], terms


def step_zero_kernel(*refs):
    got, factors, weights = refs[:4], refs[4], refs[5:11]
    done, terms_out, rows_at = refs[11:]
    take_rows(rows_at, got)
    features = rows_at.shape[1] - META
    rate = rows_at[:, features:features + 1]
    backs, terms = expert_rows(rows_at[:, :features].astype(BF16), rate, factors, 0, weights)
    terms_out[...] = jnp.broadcast_to(terms, terms_out.shape)
    for back in backs:
        part, value = back()
        done[:, part] = value.astype(BF16)


def merge_kernel(came, *outs):
    features = outs[0].shape[1] - SPAN
    for k, out in enumerate(outs):
        first = features + META + SPAN * (k + 1)
        out[:, :features] = came[:, :features]
        out[:, features:] = came[:, first:first + SPAN]


def split(value):
    high = value.astype(BF16).astype(F32)
    middle = (value - high).astype(BF16).astype(F32)
    return [high, middle, value - high - middle]


def step_one_kernel(*refs):
    came, (factors, terms0), weights = refs[:4], refs[4:6], refs[6:12]
    outs, ahead_at = refs[12:16], refs[16]
    features = came[1].shape[1] - SPAN
    parts = PAIRS // MOST
    for k in range(E_FLY):
        first = features + META if k == 0 else features
        pieces = came[k][:, first:first + SPAN].astype(F32)
        for spot in range(MOST):
            at = MOST * k + spot
            for part in range(parts):
                row = parts * spot + part
                ahead_at[at:at + 1, part * SPAN:(part + 1) * SPAN] = pieces[row:row + 1]
    meta = ahead_at[:, features:features + META]
    rate = meta[:, E_FLY * PAIRS:E_FLY * PAIRS + 1]
    match = meta[:, :E_FLY * PAIRS].astype(BF16)
    everything = jnp.concatenate([ref[:, :features] for ref in came], axis=0)
    rows = ahead_at[:, :features] + jnp.dot(match, everything, preferred_element_type=F32)
    backs, terms = expert_rows(rows.astype(BF16), rate, factors, 1, weights)
    for back in backs:
        part, value = back()
        for k, out in enumerate(outs):
            out[:, part] = value[MOST * k:MOST * (k + 1)].astype(BF16)
    meta = first_lanes(split(terms) + split(terms0[:, 0:1]))
    for k, out in enumerate(outs):
        out[:, features:] = meta[MOST * k:MOST * (k + 1)].astype(BF16)


def base_kernel(*refs):
    shifted, came, (out, rows_at) = refs[0], refs[1:5], refs[5:]
    features = out.shape[1]
    for k in range(E_FLY):
        rows = came[k][MOST * k:MOST * (k + 1), :features]
        rows_at[MOST * k:MOST * (k + 1), :] = rows.astype(F32)
    select = came[0][:, features:features + META]
    last = lax.axis_index("pipe") == lax.axis_size("pipe") - 1
    for at in range(0, features, CHUNK):
        part = slice(at, at + CHUNK)
        base = jnp.where(last, 0.0, shifted[:, part].astype(F32))
        base = base + lax.dot_general(
            select, rows_at[:, part].astype(BF16), TN, preferred_element_type=F32
        )
        out[:, part] = base.astype(BF16)


def final_kernel(*refs):
    base, routes, positions = refs[:3]
    got, (out, prob_out, back_at) = refs[3:7], refs[7:]
    _, z, _ = place()
    features = out.shape[1]
    label = labels(PAIRS, lambda k: z ^ k)
    take_rows(back_at, got)
    keys = [keys_of(routes, positions, step) for step in range(STEPS)]
    select = one_hot(keys[1], label).astype(BF16)
    for at in range(0, features, CHUNK):
        part = slice(at, at + CHUNK)
        rows = back_at[:, part].astype(BF16)
        delta = lax.dot_general(select, rows, TN, preferred_element_type=F32)
        out[:, part] = (base[:, part].astype(F32) + delta).astype(BF16)
    meta = back_at[:, features:]
    for step in range(STEPS):
        first = 3 * (STEPS - 1 - step)
        terms = meta[:, first:first + 1] + (meta[:, first + 1:first + 2] + meta[:, first + 2:first + 3])
        for choice, hit in enumerate(hits(keys[step], label)):
            prob_out[step, choice:choice + 1] = jnp.sum(
                jnp.where(hit, terms, 0.0), axis=0, keepdims=True
            )


def local_chip(out_grad, routes, positions, route_probs, saved_acts, w_gate, w_up, w_down):
    sections = lax.axis_size("pipe")
    devices = lax.axis_size("expert")
    grad = out_grad[0]
    tokens, features = grad.shape
    width = features + META
    routes = routes[0].transpose(0, 2, 1)
    positions = positions[0].transpose(0, 2, 1)
    probs = route_probs[0].transpose(0, 2, 1)
    acts = saved_acts[0]
    hidden = 2 * acts.shape[-1]

    def across(block):
        return lax.ppermute(block, "expert", [(i, i ^ 1) for i in range(devices)])

    def along(block, k):
        if k == 0:
            return block
        return lax.ppermute(block, "expert", [(i, i ^ (2 * k)) for i in range(devices)])

    def along_all(blocks):
        return [along(blocks[k], k) for k in reversed(range(E_FLY))][::-1]

    def relay(block, distance):
        route = [(i, (i + distance) % sections) for i in range(sections)]
        return lax.ppermute(block, "pipe", route)

    pair = jax.ShapeDtypeStruct((MOST, width), BF16)
    block = jax.ShapeDtypeStruct((PAIRS, width), BF16)
    wide = jax.ShapeDtypeStruct((PAIRS, features + SPAN), BF16)
    pieces = PAIRS // MOST * SPAN
    row_scratch = pltpu.VMEM((PAIRS, width), F32)

    own = [w_down[0], w_gate[0], w_up[0]]
    acts_other = across(acts)
    others = [across(own[0])]
    small = (routes, positions, probs, grad)
    *picked, table, down, gate, up = call(
        pick_kernel,
        "pick_rows",
        [pltpu.VMEM(pair.shape, BF16)] * E_FLY
        + [pltpu.VMEM((4, tokens), F32)]
        + [pltpu.VMEM(array.shape, BF16) for array in own],
        [pltpu.VMEM(array.shape, array.dtype) for array in small]
        + [pltpu.SemaphoreType.DMA((7,))],
        hbm=7,
        operands=7,
        limit=LIMIT,
    )(*small, *own)
    *own, picked[0] = lax.optimization_barrier((*own, picked[0]))
    others += [across(array) for array in own[1:]]
    others[0], picked[2] = lax.optimization_barrier((others[0], picked[2]))
    acts_other, picked[1] = lax.optimization_barrier((acts_other, picked[1]))
    got = along_all(picked)
    table, others[1] = lax.optimization_barrier((table, others[1]))
    table = relay(table, 1)
    factors = call(
        factor_kernel,
        "factors",
        jax.ShapeDtypeStruct((STEPS, 3, PAIRS, hidden), F32),
        [pltpu.VMEM((2 * acts.shape[0] * acts.shape[1], hidden), F32)],
        operands=2,
        cost=COST3,
    )(acts, acts_other)
    weights = [array for pair_of in zip((down, gate, up), others) for array in pair_of]
    done, terms0 = call(
        step_zero_kernel,
        "step_zero",
        [
            jax.ShapeDtypeStruct((PAIRS, features), BF16),
            jax.ShapeDtypeStruct((PAIRS, META), F32),
        ],
        [row_scratch],
        operands=11,
        cost=COST0,
    )(*got, factors, *weights)
    rows = call(
        ahead_kernel,
        "rows_ahead",
        jax.ShapeDtypeStruct((PAIRS, width + E_FLY * SPAN), BF16),
        [pltpu.VMEM((PAIRS, pieces), F32), pltpu.VMEM((PAIRS, E_FLY * SPAN), F32)],
        operands=5,
    )(grad, routes, positions, table, done)
    came = relay(rows, -1)
    shifted, rows = lax.optimization_barrier((grad, rows))
    shifted = relay(shifted, -1)
    sends = call(merge_kernel, "merge", [wide] * (E_FLY - 1), operands=1, cost=COST2)(came)
    came = [came] + [along(send, k + 1) for k, send in enumerate(sends)]
    back = call(
        step_one_kernel,
        "step_one",
        [pair] * E_FLY,
        [pltpu.VMEM((PAIRS, pieces), F32)],
        operands=12,
        cost=COST1,
    )(*came, factors, terms0, *weights)
    back = along_all(back)
    base = call(
        base_kernel,
        "base_sums",
        pltpu.VMEM((tokens, features), BF16),
        [pltpu.VMEM((PAIRS, features), F32)],
        operands=5,
    )(shifted, *came)
    result, prob = call(
        final_kernel,
        "final_sums",
        [
            jax.ShapeDtypeStruct((tokens, features), BF16),
            jax.ShapeDtypeStruct((STEPS, 2, tokens), F32),
        ],
        [row_scratch],
        operands=7,
    )(base, routes, positions, *back)
    return result[None], prob.transpose(0, 2, 1)[None]


def shifted(block, axis, distance):
    devices = range(lax.axis_size(axis))
    route = [(i - distance, i) for i in devices if i - distance in devices]
    return lax.ppermute(block, axis, route)


def pair_table(route_part, place_part):
    labels = jnp.arange(E_FLY * MOST, dtype=jnp.int32)
    pair_keys = jnp.where(place_part >= 0, route_part * MOST + place_part, -1)
    return (pair_keys.T[:, None, :] == labels[None, :, None]).astype(jnp.float32)


def assemble(current, onehot, contrib):
    select = (onehot[0] + onehot[1]).astype(jnp.bfloat16)
    delta = lax.dot_general(
        select, contrib, (((0,), (0,)), ((), ())), preferred_element_type=jnp.float32
    )
    return (current.astype(jnp.float32) + delta).astype(jnp.bfloat16)


def expert_back(slot_rows, slot_rates, stored, gate_weight, up_weight, down_weight):
    downward = lax.dot_general(
        slot_rows, down_weight, (((1,), (1,)), ((), ())), preferred_element_type=jnp.float32
    )
    gate_pre = stored[:, 0, :].astype(jnp.float32)
    upward = stored[:, 1, :].astype(jnp.float32)
    sigmoid_gate = jax.nn.sigmoid(gate_pre)
    active = gate_pre * sigmoid_gate
    hidden = active * upward
    scaled = slot_rates.astype(jnp.float32)[:, None] * downward
    grad_gate = (scaled * upward * sigmoid_gate * (1.0 + gate_pre * (1.0 - sigmoid_gate))).astype(
        jnp.bfloat16
    )
    grad_up = (scaled * active).astype(jnp.bfloat16)
    prob_terms = jnp.sum(hidden * downward, axis=1)
    back_rows = lax.dot_general(
        grad_gate, gate_weight, (((1,), (1,)), ((), ())), preferred_element_type=jnp.float32
    )
    back_rows = back_rows + lax.dot_general(
        grad_up, up_weight, (((1,), (1,)), ((), ())), preferred_element_type=jnp.float32
    )
    return (back_rows, prob_terms)


def local_general(out_grad, routes, positions, route_probs, saved_acts, w_gate, w_up, w_down):
    devices = lax.axis_size("expert")
    members = devices // E_FLY
    pair_count = E_FLY * MOST
    gate_weight = w_gate[0]
    up_weight = w_up[0]
    down_weight = w_down[0]
    current_grad = out_grad[0]
    features = current_grad.shape[1]
    final_grad = current_grad
    prob_rows = []
    for step_index in range(STEPS):
        route_part = routes[0, step_index]
        place_part = positions[0, step_index]
        rate_part = route_probs[0, step_index]
        onehot = pair_table(route_part, place_part)
        select = (onehot[0] + onehot[1]).astype(jnp.bfloat16)
        send_rows = jnp.dot(select, current_grad, preferred_element_type=jnp.float32).astype(
            jnp.bfloat16
        )
        send_rates = jnp.sum(
            onehot * rate_part.T.astype(jnp.float32)[:, None, :], axis=(0, 2)
        ).astype(jnp.bfloat16)
        out_rows = jnp.broadcast_to(
            send_rows.reshape(E_FLY, 1, MOST, features), (E_FLY, members, MOST, features)
        ).reshape(devices, MOST, features)
        out_rates = jnp.broadcast_to(
            send_rates.reshape(E_FLY, 1, MOST), (E_FLY, members, MOST)
        ).reshape(devices, MOST)
        got_rows, got_rates = (
            lax.all_to_all(out_rows, "expert", split_axis=0, concat_axis=0, tiled=True),
            lax.all_to_all(out_rates, "expert", split_axis=0, concat_axis=0, tiled=True),
        )
        back_rows, prob_terms = expert_back(
            got_rows.reshape(devices * MOST, features),
            got_rates.reshape(devices * MOST),
            saved_acts[0, step_index],
            gate_weight,
            up_weight,
            down_weight,
        )
        back_rows = back_rows.reshape(devices, MOST, features)
        prob_terms = prob_terms.reshape(devices, MOST)
        came_rows, came_terms = (
            lax.all_to_all(back_rows, "expert", split_axis=0, concat_axis=0, tiled=True),
            lax.all_to_all(prob_terms, "expert", split_axis=0, concat_axis=0, tiled=True),
        )
        contrib = (
            jnp.sum(came_rows.reshape(E_FLY, members, MOST, features), axis=1)
            .astype(jnp.bfloat16)
            .reshape(pair_count, features)
        )
        slot_terms = jnp.sum(came_terms.reshape(E_FLY, members, MOST), axis=1).reshape(pair_count)
        prob_rows.append(jnp.sum(onehot * slot_terms[None, :, None], axis=1).T)
        if step_index + 1 < STEPS:
            current_grad = shifted(assemble(current_grad, onehot, contrib), "pipe", -1)
        else:
            final_grad = assemble(current_grad, onehot, contrib)
    return (final_grad[None], jnp.stack(prob_rows, axis=0)[None])


def solution(mesh):
    in_specs = (
        P("pipe", "expert", None),
        P("pipe", None, "expert", None),
        P("pipe", None, "expert", None),
        P("pipe", None, "expert", None),
        P("pipe", None, None, None, "expert"),
        P("pipe", None, "expert"),
        P("pipe", None, "expert"),
        P("pipe", "expert", None),
    )
    out_specs = (P("pipe", "expert", None), P("pipe", None, "expert", None))
    one_chip = mesh.shape["expert"] == 2 * E_FLY
    local = local_chip if one_chip else local_general
    return jax.shard_map(local, mesh=mesh, in_specs=in_specs, out_specs=out_specs, check_vma=False)
```

```python
import functools

import jax
import jax.numpy as jnp
from jax import lax
from jax.experimental import pallas as pl
from jax.experimental.pallas import tpu as pltpu
from jax.sharding import PartitionSpec as P

E_FLY = 4
MOST = 2
STEPS = 2
PAIRS = E_FLY * MOST
META = 128
CHUNK = 256
SPAN = 1024
COST0 = 20000000000
COST1 = 0
COST2 = 20000000000
COST4 = 0
COST3 = 20000000000
LIMIT = 54
EARLY = 24
F32 = jnp.float32
BF16 = jnp.bfloat16
NT = (((1,), (1,)), ((), ()))
TN = (((0,), (0,)), ((), ()))


def call(kernel, name, out_shape, scratch=(), hbm=0, operands=0, limit=24, cost=0):
    specs = [pl.BlockSpec(memory_space=pl.ANY)] * hbm
    specs += [pl.BlockSpec(memory_space=pltpu.VMEM)] * (operands - hbm)
    return pl.pallas_call(
        kernel,
        name=name,
        out_shape=out_shape,
        in_specs=specs,
        scratch_shapes=list(scratch),
        cost_estimate=pl.CostEstimate(flops=cost, bytes_accessed=0, transcendentals=0),
        compiler_params=pltpu.CompilerParams(vmem_limit_bytes=limit * 2**20),
    )


def place():
    at = lax.axis_index("expert")
    return lax.axis_index("pipe"), at // 2, at % 2


def keys_of(routes, positions, step):
    return jnp.where(positions[step] >= 0, routes[step] * MOST + positions[step], -1)


def labels(rows, expert_of):
    row = lax.broadcasted_iota(jnp.int32, (rows, 1), 0)
    return expert_of(row // MOST) * MOST + row % MOST


def hits(keys, label):
    return keys[0:1] == label, keys[1:2] == label


def one_hot(keys, label):
    first, second = hits(keys, label)
    return jnp.where(first | second, 1.0, 0.0).astype(F32)


def rates_of(keys, rates, label):
    first, second = hits(keys, label)
    picked = jnp.where(first, rates[0:1], 0.0) + jnp.where(second, rates[1:2], 0.0)
    return jnp.sum(picked, axis=1, keepdims=True)


def first_lanes(columns):
    lane = lax.broadcasted_iota(jnp.int32, (columns[0].shape[0], META), 1)
    out = jnp.zeros(lane.shape, F32)
    for index, column in enumerate(columns):
        out = jnp.where(lane == index, column, out)
    return out


def picked_rows(select, early, late):
    grad = jnp.concatenate([early[...], late[...]], axis=0)
    return jnp.dot(select.astype(BF16), grad, preferred_element_type=F32)


def bring(sources, targets, sems):
    copies = [
        pltpu.make_async_copy(source, target, sems.at[index])
        for index, (source, target) in enumerate(zip(sources, targets))
    ]
    for copy in copies:
        copy.start()
    return copies


def put_rows(outs, rows, meta):
    width = rows.shape[1]
    for k, out in enumerate(outs):
        out[:, :width] = rows[MOST * k:MOST * (k + 1)].astype(BF16)
        out[:, width:] = meta[MOST * k:MOST * (k + 1)].astype(BF16)


def take_rows(scratch, refs):
    for k, ref in enumerate(refs):
        scratch[MOST * k:MOST * (k + 1), :] = ref[...].astype(F32)


def pick_kernel(*refs):
    grad, *small = refs[:4]
    outs, (table, early, late), held, sems = refs[4:8], refs[8:11], refs[11:14], refs[14]
    first = early.shape[0]
    parts = (grad.at[pl.ds(0, first)], grad.at[pl.ds(first, late.shape[0])])
    copies = bring((*small, *parts), (*held, early, late), sems)
    routes, positions, probs = held
    for copy in copies[:3]:
        copy.wait()
    _, z, _ = place()
    keys = keys_of(routes, positions, 0)
    label = labels(PAIRS, lambda k: z ^ k)
    select = one_hot(keys, label)
    rate = rates_of(keys, probs[0].astype(F32), label)
    table[0:2] = keys_of(routes, positions, 1).astype(F32)
    table[2:4] = probs[1].astype(F32)
    table[4:6] = keys.astype(F32)
    table[6:8] = jnp.zeros_like(table[6:8])
    for copy in copies[3:5]:
        copy.wait()
    rows = picked_rows(select, early, late)
    put_rows(outs, rows, first_lanes([rate]))


def rows_ahead(early, late, table, came_table, rows_out, held, packed):
    p, z, c = place()
    keys0 = table[4:6].astype(jnp.int32)
    keys1 = came_table[0:2].astype(jnp.int32)
    keys1 = jnp.where(p == 0, -1, keys1)
    label = labels(PAIRS, lambda k: z ^ k)
    select = one_hot(keys1, label)
    rows = picked_rows(select, early, late)
    rate = rates_of(keys1, came_table[2:4], label)
    lane = lax.broadcasted_iota(jnp.int32, (PAIRS, META), 1)
    meta = jnp.where(lane == E_FLY * PAIRS, rate, 0.0)
    column = lax.broadcasted_iota(jnp.int32, (META, 1), 0)
    source, block, spot = column // PAIRS, column // MOST % E_FLY, column % MOST
    row = lax.broadcasted_iota(jnp.int32, (PAIRS, 1), 0)
    for k in range(E_FLY):
        expert = z ^ k ^ source
        own = (source < E_FLY) & (source ^ block == k)
        step0 = one_hot(keys0, jnp.where(own, expert * MOST + spot, -2))
        match = lax.dot_general(
            select.astype(BF16), step0.astype(BF16), NT, preferred_element_type=F32
        )
        meta = meta + jnp.where(row // MOST == k, match, 0.0)
    features = rows.shape[1]
    width = features + META
    taken = one_hot(jnp.where(p == 0, -1, keys0), label)
    rows_out[:, :META] = taken.astype(BF16)
    held[:, :features] = rows
    held[:, features:width] = meta
    parts = PAIRS // MOST
    for at in range(PAIRS):
        k, spot = at // MOST, at % MOST
        for part in range(parts):
            piece = held[at:at + 1, part * SPAN:(part + 1) * SPAN]
            packed[parts * spot + part:parts * spot + part + 1, k * SPAN:(k + 1) * SPAN] = piece
    rows_out[:, META:] = packed[...].astype(BF16)


def act_factors(acts, acts_other, factors, rows_at):
    _, z, c = place()
    steps, slots, _, width = acts.shape
    for half, ref in enumerate((acts, acts_other)):
        for at in range(steps * slots):
            rows_at[2 * at:2 * at + 2, half * width:(half + 1) * width] = ref[
                at // slots, at % slots
            ].astype(F32)
    stored = rows_at[...].astype(BF16)
    row = lax.broadcasted_iota(jnp.int32, (2 * steps * PAIRS, 2 * steps * slots), 0)
    column = lax.broadcasted_iota(jnp.int32, row.shape, 1)
    group, k, spot = row // PAIRS, row // MOST % E_FLY, row % MOST
    slot = (2 * (z ^ k) + (c ^ (group // 2))) * MOST + spot
    wanted = 2 * (group // 2 * slots + slot) + group % 2
    pick = jnp.where(column == wanted, 1.0, 0.0).astype(BF16)
    picked = jnp.dot(pick, stored, preferred_element_type=F32)
    for step in range(steps):
        gate = picked[2 * step * PAIRS:(2 * step + 1) * PAIRS]
        up = picked[(2 * step + 1) * PAIRS:(2 * step + 2) * PAIRS]
        sigmoid = 1.0 / (1.0 + jnp.exp(-gate))
        active = gate * sigmoid
        factors[step, 0] = up * sigmoid * (1.0 + gate * (1.0 - sigmoid))
        factors[step, 1] = active
        factors[step, 2] = active * up


def prepare_kernel(*refs):
    ahead, acts, (rows_out, factors, held, packed, acts_at) = refs[:4], refs[4:6], refs[6:]
    act_factors(*acts, factors, acts_at)
    rows_ahead(*ahead, rows_out, held, packed)


def expert_rows(rows, rate, factors, step, weights):
    down, gate, up = weights[:2], weights[2:4], weights[4:]
    v = jnp.concatenate(
        [lax.dot_general(ref[...], rows, NT, preferred_element_type=F32).T for ref in down],
        axis=1,
    )
    scaled = rate * v
    grads = jnp.concatenate(
        [(scaled * factors[step, 0]).astype(BF16), (scaled * factors[step, 1]).astype(BF16)],
        axis=1,
    )
    terms = jnp.sum(factors[step, 2] * v, axis=1, keepdims=True)

    def back(at):
        part = slice(at, at + CHUNK)
        wide = jnp.concatenate([ref[part] for ref in (*gate, *up)], axis=1)
        return part, lax.dot_general(wide, grads, NT, preferred_element_type=F32).T

    return [functools.partial(back, at) for at in range(0, rows.shape[1], CHUNK)], terms


def step_zero_kernel(*refs):
    got, (ahead, factors), weights = refs[:4], refs[4:6], refs[6:12]
    rows_out, terms_out, rows_at = refs[12:]
    take_rows(rows_at, got)
    features = rows_at.shape[1] - META
    rate = rows_at[:, features:features + 1]
    backs, terms = expert_rows(rows_at[:, :features].astype(BF16), rate, factors, 0, weights)
    terms_out[...] = jnp.broadcast_to(terms, terms_out.shape)
    rows_out[:, features:] = ahead[...]
    for back in backs:
        part, value = back()
        rows_out[:, part] = value.astype(BF16)


def merge_kernel(came, *outs):
    features = outs[0].shape[1] - SPAN
    for k, out in enumerate(outs):
        first = features + META + SPAN * (k + 1)
        out[:, :features] = came[:, :features]
        out[:, features:] = came[:, first:first + SPAN]


def split(value):
    high = value.astype(BF16).astype(F32)
    middle = (value - high).astype(BF16).astype(F32)
    return [high, middle, value - high - middle]


def step_one_kernel(*refs):
    came, (factors, terms0), weights = refs[:4], refs[4:6], refs[6:12]
    outs, home, ahead_at, back_at = refs[12:15], *refs[15:]
    features = came[1].shape[1] - SPAN
    parts = PAIRS // MOST
    for k in range(E_FLY):
        first = features + META if k == 0 else features
        pieces = came[k][:, first:first + SPAN].astype(F32)
        for spot in range(MOST):
            at = MOST * k + spot
            for part in range(parts):
                row = parts * spot + part
                ahead_at[at:at + 1, part * SPAN:(part + 1) * SPAN] = pieces[row:row + 1]
    meta = ahead_at[:, features:features + META]
    rate = meta[:, E_FLY * PAIRS:E_FLY * PAIRS + 1]
    match = meta[:, :E_FLY * PAIRS].astype(BF16)
    everything = jnp.concatenate([ref[:, :features] for ref in came], axis=0)
    rows = ahead_at[:, :features] + jnp.dot(match, everything, preferred_element_type=F32)
    backs, terms = expert_rows(rows.astype(BF16), rate, factors, 1, weights)
    for k in range(E_FLY):
        own = came[k][MOST * k:MOST * (k + 1), :features]
        back_at[MOST * k:MOST * (k + 1), :features] = own.astype(F32)
    back_at[:PAIRS, features:] = came[0][:, features:features + META].astype(F32)
    for back in backs:
        part, value = back()
        back_at[PAIRS:, part] = value
        for k, out in enumerate(outs):
            out[:, part] = value[MOST * (k + 1):MOST * (k + 2)].astype(BF16)
    meta = first_lanes(split(terms) + split(terms0[:, 0:1]))
    back_at[PAIRS:, features:] = meta
    for k, out in enumerate(outs):
        out[:, features:] = meta[MOST * (k + 1):MOST * (k + 2)].astype(BF16)
    home[...] = back_at[...].astype(BF16)


def base_kernel(*refs):
    early, late, home, out = refs
    features = out.shape[1]
    select = home[:PAIRS, features:]
    last = lax.axis_index("pipe") == lax.axis_size("pipe") - 1
    for at in range(0, features, CHUNK):
        part = slice(at, at + CHUNK)
        base = jnp.concatenate([early[:, part], late[:, part]], axis=0).astype(F32)
        base = jnp.where(last, 0.0, base)
        base = base + lax.dot_general(
            select, home[:PAIRS, part], TN, preferred_element_type=F32
        )
        out[:, part] = base.astype(BF16)


def final_kernel(*refs):
    base, table, got, (out, prob_out, back_at) = *refs[:2], refs[2:6], refs[6:]
    _, z, _ = place()
    features = out.shape[1]
    label = labels(PAIRS, lambda k: z ^ k)
    take_rows(back_at, [got[0].at[pl.ds(PAIRS, MOST)], *got[1:]])
    keys = [table[first:first + 2].astype(jnp.int32) for first in (4, 0)]
    select = one_hot(keys[1], label).astype(BF16)
    for at in range(0, features, CHUNK):
        part = slice(at, at + CHUNK)
        rows = back_at[:, part].astype(BF16)
        delta = lax.dot_general(select, rows, TN, preferred_element_type=F32)
        out[:, part] = (base[:, part].astype(F32) + delta).astype(BF16)
    meta = back_at[:, features:]
    for step in range(STEPS):
        first = 3 * (STEPS - 1 - step)
        terms = meta[:, first:first + 1] + (meta[:, first + 1:first + 2] + meta[:, first + 2:first + 3])
        for choice, hit in enumerate(hits(keys[step], label)):
            prob_out[step, choice:choice + 1] = jnp.sum(
                jnp.where(hit, terms, 0.0), axis=0, keepdims=True
            )


def local_chip(out_grad, routes, positions, route_probs, saved_acts, w_gate, w_up, w_down):
    sections = lax.axis_size("pipe")
    devices = lax.axis_size("expert")
    grad = out_grad[0]
    tokens, features = grad.shape
    width = features + META
    routes = routes[0].transpose(0, 2, 1)
    positions = positions[0].transpose(0, 2, 1)
    probs = route_probs[0].transpose(0, 2, 1)
    acts = saved_acts[0]
    hidden = 2 * acts.shape[-1]

    def across(block):
        return lax.ppermute(block, "expert", [(i, i ^ 1) for i in range(devices)])

    def along(block, k):
        if k == 0:
            return block
        return lax.ppermute(block, "expert", [(i, i ^ (2 * k)) for i in range(devices)])

    def along_all(blocks):
        return [along(blocks[k], k) for k in reversed(range(E_FLY))][::-1]

    def crossing(block, k):
        return lax.ppermute(block, "expert", [(i, i ^ (2 * k + 1)) for i in range(devices)])

    def relay_crossing(block, distance):
        route = [
            (p * devices + i, (p + distance) % sections * devices + (i ^ 1))
            for p in range(sections)
            for i in range(devices)
        ]
        return lax.ppermute(block, ("pipe", "expert"), route)

    def relay(block, distance):
        route = [(i, (i + distance) % sections) for i in range(sections)]
        return lax.ppermute(block, "pipe", route)

    pair = jax.ShapeDtypeStruct((MOST, width), BF16)
    block = jax.ShapeDtypeStruct((PAIRS, width), BF16)
    wide = jax.ShapeDtypeStruct((PAIRS, features + SPAN), BF16)
    pieces = PAIRS // MOST * SPAN
    row_scratch = pltpu.VMEM((PAIRS, width), F32)

    own = [w_down[0], w_gate[0], w_up[0]]
    acts_other = across(acts)
    others = [across(own[0])]
    first = EARLY * tokens // 128
    small = (routes, positions, probs)
    *picked, table, early, late = call(
        pick_kernel,
        "pick_rows",
        [pltpu.VMEM(pair.shape, BF16)] * E_FLY
        + [pltpu.VMEM((8, tokens), F32)]
        + [pltpu.VMEM((rows, features), BF16) for rows in (first, tokens - first)],
        [pltpu.VMEM(array.shape, array.dtype) for array in small]
        + [pltpu.SemaphoreType.DMA((5,))],
        hbm=4,
        operands=4,
        limit=LIMIT,
        cost=COST4,
    )(grad, *small)
    *own, picked[0] = lax.optimization_barrier((*own, picked[0]))
    others += [across(array) for array in own[1:]]
    others[0], picked[2] = lax.optimization_barrier((others[0], picked[2]))
    acts_other, picked[1] = lax.optimization_barrier((acts_other, picked[1]))
    came_table = relay(table, 1)
    came_early = relay(early, -1)
    got = along_all(picked)
    ahead, factors = call(
        prepare_kernel,
        "prepare",
        [
            jax.ShapeDtypeStruct((PAIRS, META + E_FLY * SPAN), BF16),
            jax.ShapeDtypeStruct((STEPS, 3, PAIRS, hidden), F32),
        ],
        [
            pltpu.VMEM((PAIRS, pieces), F32),
            pltpu.VMEM((PAIRS, E_FLY * SPAN), F32),
            pltpu.VMEM((2 * acts.shape[0] * acts.shape[1], hidden), F32),
        ],
        operands=6,
        cost=COST3,
    )(early, late, table, came_table, acts, acts_other)
    weights = [array for pair_of in zip(own, others) for array in pair_of]
    rows, terms0 = call(
        step_zero_kernel,
        "step_zero",
        [
            jax.ShapeDtypeStruct((PAIRS, width + E_FLY * SPAN), BF16),
            jax.ShapeDtypeStruct((PAIRS, META), F32),
        ],
        [row_scratch],
        operands=12,
        cost=COST0,
    )(*got, ahead, factors, *weights)
    came = relay_crossing(rows, -1)
    terms0 = across(terms0)
    came_early, late = lax.optimization_barrier((came_early, late))
    came_late = relay(late, -1)
    sends = call(merge_kernel, "merge", [wide] * (E_FLY - 1), operands=1, cost=COST2)(came)
    came = along_all([came, *sends])
    *back, home = call(
        step_one_kernel,
        "step_one",
        [pair] * (E_FLY - 1) + [jax.ShapeDtypeStruct((STEPS * PAIRS, width), BF16)],
        [pltpu.VMEM((PAIRS, pieces), F32), pltpu.VMEM((STEPS * PAIRS, width), F32)],
        operands=12,
        cost=COST1,
    )(*came, factors, terms0, *weights)
    back = [crossing(back[k - 1], k) for k in reversed(range(1, E_FLY))][::-1]
    home = crossing(home, 0)
    base = call(
        base_kernel,
        "base_sums",
        pltpu.VMEM((tokens, features), BF16),
        operands=3,
    )(came_early, came_late, home)
    result, prob = call(
        final_kernel,
        "final_sums",
        [
            jax.ShapeDtypeStruct((tokens, features), BF16),
            jax.ShapeDtypeStruct((STEPS, 2, tokens), F32),
        ],
        [row_scratch],
        operands=6,
    )(base, table, home, *back)
    return result[None], prob.transpose(0, 2, 1)[None]


def shifted(block, axis, distance):
    devices = range(lax.axis_size(axis))
    route = [(i - distance, i) for i in devices if i - distance in devices]
    return lax.ppermute(block, axis, route)


def pair_table(route_part, place_part):
    labels = jnp.arange(E_FLY * MOST, dtype=jnp.int32)
    pair_keys = jnp.where(place_part >= 0, route_part * MOST + place_part, -1)
    return (pair_keys.T[:, None, :] == labels[None, :, None]).astype(jnp.float32)


def assemble(current, onehot, contrib):
    select = (onehot[0] + onehot[1]).astype(jnp.bfloat16)
    delta = lax.dot_general(
        select, contrib, (((0,), (0,)), ((), ())), preferred_element_type=jnp.float32
    )
    return (current.astype(jnp.float32) + delta).astype(jnp.bfloat16)


def expert_back(slot_rows, slot_rates, stored, gate_weight, up_weight, down_weight):
    downward = lax.dot_general(
        slot_rows, down_weight, (((1,), (1,)), ((), ())), preferred_element_type=jnp.float32
    )
    gate_pre = stored[:, 0, :].astype(jnp.float32)
    upward = stored[:, 1, :].astype(jnp.float32)
    sigmoid_gate = jax.nn.sigmoid(gate_pre)
    active = gate_pre * sigmoid_gate
    hidden = active * upward
    scaled = slot_rates.astype(jnp.float32)[:, None] * downward
    grad_gate = (scaled * upward * sigmoid_gate * (1.0 + gate_pre * (1.0 - sigmoid_gate))).astype(
        jnp.bfloat16
    )
    grad_up = (scaled * active).astype(jnp.bfloat16)
    prob_terms = jnp.sum(hidden * downward, axis=1)
    back_rows = lax.dot_general(
        grad_gate, gate_weight, (((1,), (1,)), ((), ())), preferred_element_type=jnp.float32
    )
    back_rows = back_rows + lax.dot_general(
        grad_up, up_weight, (((1,), (1,)), ((), ())), preferred_element_type=jnp.float32
    )
    return (back_rows, prob_terms)


def local_general(out_grad, routes, positions, route_probs, saved_acts, w_gate, w_up, w_down):
    devices = lax.axis_size("expert")
    members = devices // E_FLY
    pair_count = E_FLY * MOST
    gate_weight = w_gate[0]
    up_weight = w_up[0]
    down_weight = w_down[0]
    current_grad = out_grad[0]
    features = current_grad.shape[1]
    final_grad = current_grad
    prob_rows = []
    for step_index in range(STEPS):
        route_part = routes[0, step_index]
        place_part = positions[0, step_index]
        rate_part = route_probs[0, step_index]
        onehot = pair_table(route_part, place_part)
        select = (onehot[0] + onehot[1]).astype(jnp.bfloat16)
        send_rows = jnp.dot(select, current_grad, preferred_element_type=jnp.float32).astype(
            jnp.bfloat16
        )
        send_rates = jnp.sum(
            onehot * rate_part.T.astype(jnp.float32)[:, None, :], axis=(0, 2)
        ).astype(jnp.bfloat16)
        out_rows = jnp.broadcast_to(
            send_rows.reshape(E_FLY, 1, MOST, features), (E_FLY, members, MOST, features)
        ).reshape(devices, MOST, features)
        out_rates = jnp.broadcast_to(
            send_rates.reshape(E_FLY, 1, MOST), (E_FLY, members, MOST)
        ).reshape(devices, MOST)
        got_rows, got_rates = (
            lax.all_to_all(out_rows, "expert", split_axis=0, concat_axis=0, tiled=True),
            lax.all_to_all(out_rates, "expert", split_axis=0, concat_axis=0, tiled=True),
        )
        back_rows, prob_terms = expert_back(
            got_rows.reshape(devices * MOST, features),
            got_rates.reshape(devices * MOST),
            saved_acts[0, step_index],
            gate_weight,
            up_weight,
            down_weight,
        )
        back_rows = back_rows.reshape(devices, MOST, features)
        prob_terms = prob_terms.reshape(devices, MOST)
        came_rows, came_terms = (
            lax.all_to_all(back_rows, "expert", split_axis=0, concat_axis=0, tiled=True),
            lax.all_to_all(prob_terms, "expert", split_axis=0, concat_axis=0, tiled=True),
        )
        contrib = (
            jnp.sum(came_rows.reshape(E_FLY, members, MOST, features), axis=1)
            .astype(jnp.bfloat16)
            .reshape(pair_count, features)
        )
        slot_terms = jnp.sum(came_terms.reshape(E_FLY, members, MOST), axis=1).reshape(pair_count)
        prob_rows.append(jnp.sum(onehot * slot_terms[None, :, None], axis=1).T)
        if step_index + 1 < STEPS:
            current_grad = shifted(assemble(current_grad, onehot, contrib), "pipe", -1)
        else:
            final_grad = assemble(current_grad, onehot, contrib)
    return (final_grad[None], jnp.stack(prob_rows, axis=0)[None])


def solution(mesh):
    in_specs = (
        P("pipe", "expert", None),
        P("pipe", None, "expert", None),
        P("pipe", None, "expert", None),
        P("pipe", None, "expert", None),
        P("pipe", None, None, None, "expert"),
        P("pipe", None, "expert"),
        P("pipe", None, "expert"),
        P("pipe", "expert", None),
    )
    out_specs = (P("pipe", "expert", None), P("pipe", None, "expert", None))
    one_chip = mesh.shape["expert"] == 2 * E_FLY
    local = local_chip if one_chip else local_general
    return jax.shard_map(local, mesh=mesh, in_specs=in_specs, out_specs=out_specs, check_vma=False)
```

```python
import functools

import jax
import jax.numpy as jnp
from jax import lax
from jax.experimental import pallas as pl
from jax.experimental.pallas import tpu as pltpu
from jax.sharding import PartitionSpec as P

E_FLY = 4
MOST = 2
STEPS = 2
PAIRS = E_FLY * MOST
META = 128
CHUNK = 256
SPAN = 1024
OUT = 1280
COST0 = 20_000_000_000
COST1 = 0
COST2 = 20_000_000_000
COST3 = 20_000_000_000
LIMIT = 54
F32 = jnp.float32
BF16 = jnp.bfloat16
NT = (((1,), (1,)), ((), ()))
TN = (((0,), (0,)), ((), ()))


def call(kernel, name, out_shape, scratch=(), hbm=0, operands=0, limit=24, cost=0, out_specs=None):
    specs = [pl.BlockSpec(memory_space=pl.ANY)] * hbm
    specs += [pl.BlockSpec(memory_space=pltpu.VMEM)] * (operands - hbm)
    return pl.pallas_call(
        kernel,
        name=name,
        out_shape=out_shape,
        in_specs=specs,
        **({} if out_specs is None else {"out_specs": out_specs}),
        scratch_shapes=list(scratch),
        cost_estimate=pl.CostEstimate(flops=cost, bytes_accessed=0, transcendentals=0),
        compiler_params=pltpu.CompilerParams(vmem_limit_bytes=limit * 2**20),
    )


def place():
    at = lax.axis_index("expert")
    return lax.axis_index("pipe"), at // 2, at % 2


def keys_of(routes, positions, step):
    return jnp.where(positions[step] >= 0, routes[step] * MOST + positions[step], -1)


def labels(rows, expert_of):
    row = lax.broadcasted_iota(jnp.int32, (rows, 1), 0)
    return expert_of(row // MOST) * MOST + row % MOST


def hits(keys, label):
    return keys[0:1] == label, keys[1:2] == label


def one_hot(keys, label):
    first, second = hits(keys, label)
    return jnp.where(first | second, 1.0, 0.0).astype(F32)


def rates_of(keys, rates, label):
    first, second = hits(keys, label)
    picked = jnp.where(first, rates[0:1], 0.0) + jnp.where(second, rates[1:2], 0.0)
    return jnp.sum(picked, axis=1, keepdims=True)


def first_lanes(columns):
    lane = lax.broadcasted_iota(jnp.int32, (columns[0].shape[0], META), 1)
    out = jnp.zeros(lane.shape, F32)
    for index, column in enumerate(columns):
        out = jnp.where(lane == index, column, out)
    return out


def bring(sources, targets, sems):
    copies = [
        pltpu.make_async_copy(source, target, sems.at[index])
        for index, (source, target) in enumerate(zip(sources, targets))
    ]
    for copy in copies:
        copy.start()
    return copies


def put_rows(outs, rows, meta):
    width = rows.shape[1]
    for k, out in enumerate(outs):
        out[:, :width] = rows[MOST * k:MOST * (k + 1)].astype(BF16)
        out[:, width:] = meta[MOST * k:MOST * (k + 1)].astype(BF16)


def take_rows(scratch, refs):
    for k, ref in enumerate(refs):
        scratch[MOST * k:MOST * (k + 1), :] = ref[...].astype(F32)


def pick_kernel(*refs):
    outs, table, held, sems = refs[4:8], refs[8], refs[9:13], refs[13]
    copies = bring(refs[:4], held, sems)
    routes, positions, probs, grad = held
    for copy in copies[:3]:
        copy.wait()
    _, z, _ = place()
    keys = keys_of(routes, positions, 0)
    label = labels(PAIRS, lambda k: z ^ k)
    select = one_hot(keys, label)
    rate = rates_of(keys, probs[0].astype(F32), label)
    table[0:2] = keys_of(routes, positions, 1).astype(F32)
    table[2:4] = probs[1].astype(F32)
    copies[3].wait()
    rows = jnp.dot(select.astype(BF16), grad[...], preferred_element_type=F32)
    put_rows(outs, rows, first_lanes([rate]))


def ahead_kernel(grad, routes, positions, table, done, rows_out, held, packed):
    p, z, c = place()
    keys0 = keys_of(routes, positions, 0)
    keys1 = table[0:2].astype(jnp.int32)
    keys1 = jnp.where(p == 0, -1, keys1)
    label = labels(PAIRS, lambda k: z ^ k)
    select = one_hot(keys1, label)
    rows = jnp.dot(select.astype(BF16), grad[...], preferred_element_type=F32)
    rate = rates_of(keys1, table[2:4], label)
    lane = lax.broadcasted_iota(jnp.int32, (PAIRS, META), 1)
    meta = jnp.where(lane == E_FLY * PAIRS, rate, 0.0)
    column = lax.broadcasted_iota(jnp.int32, (META, 1), 0)
    source, block, spot = column // PAIRS, column // MOST % E_FLY, column % MOST
    row = lax.broadcasted_iota(jnp.int32, (PAIRS, 1), 0)
    for k in range(E_FLY):
        expert = z ^ k ^ source
        own = (source < E_FLY) & (source ^ block == k)
        step0 = one_hot(keys0, jnp.where(own, expert * MOST + spot, -2))
        match = lax.dot_general(
            select.astype(BF16), step0.astype(BF16), NT, preferred_element_type=F32
        )
        meta = meta + jnp.where(row // MOST == k, match, 0.0)
    features = rows.shape[1]
    width = features + META
    rows_out[:, :features] = done[...]
    taken = one_hot(jnp.where(p == 0, -1, keys0), label)
    rows_out[:, features:width] = taken.astype(BF16)
    held[:, :features] = rows
    held[:, features:width] = meta
    parts = PAIRS // MOST
    for at in range(PAIRS):
        k, spot = at // MOST, at % MOST
        for part in range(parts):
            piece = held[at:at + 1, part * SPAN:(part + 1) * SPAN]
            packed[parts * spot + part:parts * spot + part + 1, k * SPAN:(k + 1) * SPAN] = piece
    rows_out[:, width:] = packed[...].astype(BF16)


def factor_kernel(acts, acts_other, factors, rows_at):
    _, z, c = place()
    steps, slots, _, width = acts.shape
    for half, ref in enumerate((acts, acts_other)):
        for at in range(steps * slots):
            rows_at[2 * at:2 * at + 2, half * width:(half + 1) * width] = ref[
                at // slots, at % slots
            ].astype(F32)
    stored = rows_at[...].astype(BF16)
    row = lax.broadcasted_iota(jnp.int32, (2 * steps * PAIRS, 2 * steps * slots), 0)
    column = lax.broadcasted_iota(jnp.int32, row.shape, 1)
    group, k, spot = row // PAIRS, row // MOST % E_FLY, row % MOST
    slot = (2 * (z ^ k) + c) * MOST + spot
    wanted = 2 * (group // 2 * slots + slot) + group % 2
    pick = jnp.where(column == wanted, 1.0, 0.0).astype(BF16)
    picked = jnp.dot(pick, stored, preferred_element_type=F32)
    for step in range(steps):
        gate = picked[2 * step * PAIRS:(2 * step + 1) * PAIRS]
        up = picked[(2 * step + 1) * PAIRS:(2 * step + 2) * PAIRS]
        sigmoid = 1.0 / (1.0 + jnp.exp(-gate))
        active = gate * sigmoid
        factors[step, 0] = up * sigmoid * (1.0 + gate * (1.0 - sigmoid))
        factors[step, 1] = active
        factors[step, 2] = active * up


def expert_rows(rows, rate, factors, step, weights):
    down, gate, up = weights[:2], weights[2:4], weights[4:]
    v = jnp.concatenate(
        [lax.dot_general(ref[...], rows, NT, preferred_element_type=F32).T for ref in down],
        axis=1,
    )
    scaled = rate * v
    grads = jnp.concatenate(
        [(scaled * factors[step, 0]).astype(BF16), (scaled * factors[step, 1]).astype(BF16)],
        axis=1,
    )
    terms = jnp.sum(factors[step, 2] * v, axis=1, keepdims=True)

    def back(at):
        part = slice(at, at + CHUNK)
        wide = jnp.concatenate([ref[part] for ref in (*gate, *up)], axis=1)
        return part, lax.dot_general(wide, grads, NT, preferred_element_type=F32).T

    return [functools.partial(back, at) for at in range(0, rows.shape[1], CHUNK)], terms


def step_zero_kernel(*refs):
    got, factors, weights = refs[:4], refs[4], refs[5:11]
    done, terms_out, rows_at = refs[11:]
    take_rows(rows_at, got)
    features = rows_at.shape[1] - META
    rate = rows_at[:, features:features + 1]
    backs, terms = expert_rows(rows_at[:, :features].astype(BF16), rate, factors, 0, weights)
    terms_out[...] = jnp.broadcast_to(terms, terms_out.shape)
    for back in backs:
        part, value = back()
        done[:, part] = value.astype(BF16)


def merge_kernel(came, *outs):
    features = outs[0].shape[1] - SPAN
    for k, out in enumerate(outs):
        first = features + META + SPAN * (k + 1)
        out[:, :features] = came[:, :features]
        out[:, features:] = came[:, first:first + SPAN]


def split(value):
    high = value.astype(BF16).astype(F32)
    middle = (value - high).astype(BF16).astype(F32)
    return [high, middle, value - high - middle]


def step_one_kernel(*refs):
    came, (factors, terms0), weights = refs[:4], refs[4:6], refs[6:12]
    outs, ahead_at = refs[12:16], refs[16]
    features = came[1].shape[1] - SPAN
    parts = PAIRS // MOST
    for k in range(E_FLY):
        first = features + META if k == 0 else features
        pieces = came[k][:, first:first + SPAN].astype(F32)
        for spot in range(MOST):
            at = MOST * k + spot
            for part in range(parts):
                row = parts * spot + part
                ahead_at[at:at + 1, part * SPAN:(part + 1) * SPAN] = pieces[row:row + 1]
    meta = ahead_at[:, features:features + META]
    rate = meta[:, E_FLY * PAIRS:E_FLY * PAIRS + 1]
    match = meta[:, :E_FLY * PAIRS].astype(BF16)
    everything = jnp.concatenate([ref[:, :features] for ref in came], axis=0)
    rows = ahead_at[:, :features] + jnp.dot(match, everything, preferred_element_type=F32)
    backs, terms = expert_rows(rows.astype(BF16), rate, factors, 1, weights)
    for back in backs:
        part, value = back()
        for k, out in enumerate(outs):
            out[:, part] = value[MOST * k:MOST * (k + 1)].astype(BF16)
    meta = first_lanes(split(terms) + split(terms0[:, 0:1]))
    for k, out in enumerate(outs):
        out[:, features:] = meta[MOST * k:MOST * (k + 1)].astype(BF16)


def own_kernel(*refs):
    routes, positions, came, (rows, takes) = *refs[:2], refs[2:6], refs[6:]
    _, z, _ = place()
    features = rows.shape[1]
    for k in range(E_FLY):
        own = came[k][MOST * k:MOST * (k + 1), :features]
        rows[MOST * k:MOST * (k + 1), :] = own.astype(F32)
    select = one_hot(keys_of(routes, positions, 1), labels(PAIRS, lambda k: z ^ k))
    before = came[0][:, features:features + META].astype(F32)
    takes[...] = jnp.concatenate([before, select], axis=0).astype(BF16)


def final_kernel(*refs):
    shifted, own, takes, routes, positions = refs[:5]
    got, (out, prob_out) = refs[5:9], refs[9:11]
    back_at, out_at, prob_at, sems = refs[11:]
    p, z, _ = place()
    features = out.shape[1]
    label = labels(PAIRS, lambda k: z ^ k)
    take_rows(back_at, got)
    meta = back_at[:, features:]
    for step in range(STEPS):
        first = 3 * (STEPS - 1 - step)
        terms = meta[:, first:first + 1] + (meta[:, first + 1:first + 2] + meta[:, first + 2:first + 3])
        for choice, hit in enumerate(hits(keys_of(routes, positions, step), label)):
            prob_at[step, choice:choice + 1] = jnp.sum(
                jnp.where(hit, terms, 0.0), axis=0, keepdims=True
            )
    copies = [pltpu.make_async_copy(prob_at, prob_out, sems.at[0])]
    copies[0].start()
    last = p == lax.axis_size("pipe") - 1
    for at in range(0, features, CHUNK):
        part = slice(at, at + CHUNK)
        rows = jnp.concatenate([own[:, part], back_at[:, part]], axis=0).astype(BF16)
        delta = lax.dot_general(takes[...], rows, TN, preferred_element_type=F32)
        base = jnp.where(last, 0.0, shifted[:, part].astype(F32))
        out_at[:, part] = (base + delta).astype(BF16)
        if (at + CHUNK) % OUT == 0:
            wide = pl.ds(at + CHUNK - OUT, OUT)
            copies.append(
                pltpu.make_async_copy(
                    out_at.at[:, wide], out.at[:, wide], sems.at[len(copies)]
                )
            )
            copies[-1].start()
    for copy in copies:
        copy.wait()


def local_chip(out_grad, routes, positions, route_probs, saved_acts, w_gate, w_up, w_down):
    sections = lax.axis_size("pipe")
    devices = lax.axis_size("expert")
    grad = out_grad[0]
    tokens, features = grad.shape
    width = features + META
    routes = routes[0].transpose(0, 2, 1)
    positions = positions[0].transpose(0, 2, 1)
    probs = route_probs[0].transpose(0, 2, 1)
    acts = saved_acts[0]
    hidden = 2 * acts.shape[-1]

    def across(block):
        return lax.ppermute(block, "expert", [(i, i ^ 1) for i in range(devices)])

    def along(block, k):
        if k == 0:
            return block
        return lax.ppermute(block, "expert", [(i, i ^ (2 * k)) for i in range(devices)])

    def along_all(blocks):
        return [along(blocks[k], k) for k in reversed(range(E_FLY))][::-1]

    def relay(block, distance):
        route = [(i, (i + distance) % sections) for i in range(sections)]
        return lax.ppermute(block, "pipe", route)

    pair = jax.ShapeDtypeStruct((MOST, width), BF16)
    block = jax.ShapeDtypeStruct((PAIRS, width), BF16)
    wide = jax.ShapeDtypeStruct((PAIRS, features + SPAN), BF16)
    pieces = PAIRS // MOST * SPAN
    row_scratch = pltpu.VMEM((PAIRS, width), F32)

    own = [w_down[0], w_gate[0], w_up[0]]
    acts_other = across(acts)
    others = [across(own[0])]
    small = (routes, positions, probs, grad)
    *picked, table = call(
        pick_kernel,
        "pick_rows",
        [pltpu.VMEM(pair.shape, BF16)] * E_FLY
        + [pltpu.VMEM((4, tokens), F32)],
        [pltpu.VMEM(array.shape, array.dtype) for array in small]
        + [pltpu.SemaphoreType.DMA((4,))],
        hbm=4,
        operands=4,
        limit=LIMIT,
    )(*small)
    *own, picked[0] = lax.optimization_barrier((*own, picked[0]))
    others += [across(array) for array in own[1:]]
    others[0], picked[2] = lax.optimization_barrier((others[0], picked[2]))
    acts_other, picked[1] = lax.optimization_barrier((acts_other, picked[1]))
    got = along_all(picked)
    table, others[1] = lax.optimization_barrier((table, others[1]))
    table = relay(table, 1)
    factors = call(
        factor_kernel,
        "factors",
        jax.ShapeDtypeStruct((STEPS, 3, PAIRS, hidden), F32),
        [pltpu.VMEM((2 * acts.shape[0] * acts.shape[1], hidden), F32)],
        operands=2,
        cost=COST3,
    )(acts, acts_other)
    weights = [array for pair_of in zip(own, others) for array in pair_of]
    done, terms0 = call(
        step_zero_kernel,
        "step_zero",
        [
            jax.ShapeDtypeStruct((PAIRS, features), BF16),
            jax.ShapeDtypeStruct((PAIRS, META), F32),
        ],
        [row_scratch],
        operands=11,
        cost=COST0,
    )(*got, factors, *weights)
    rows = call(
        ahead_kernel,
        "rows_ahead",
        jax.ShapeDtypeStruct((PAIRS, width + E_FLY * SPAN), BF16),
        [pltpu.VMEM((PAIRS, pieces), F32), pltpu.VMEM((PAIRS, E_FLY * SPAN), F32)],
        operands=5,
    )(grad, routes, positions, table, done)
    came = relay(rows, -1)
    shifted, _ = lax.optimization_barrier((grad, across(terms0)))
    shifted = relay(shifted, -1)
    sends = call(merge_kernel, "merge", [wide] * (E_FLY - 1), operands=1, cost=COST2)(came)
    came = [came] + [along(send, k + 1) for k, send in enumerate(sends)]
    back = call(
        step_one_kernel,
        "step_one",
        [pair] * E_FLY,
        [pltpu.VMEM((PAIRS, pieces), F32)],
        operands=12,
        cost=COST1,
    )(*came, factors, terms0, *weights)
    back = along_all(back)
    own_rows, takes = call(
        own_kernel,
        "own_rows",
        [
            jax.ShapeDtypeStruct((PAIRS, features), F32),
            jax.ShapeDtypeStruct((STEPS * PAIRS, tokens), BF16),
        ],
        operands=6,
    )(routes, positions, *came)
    result, prob = call(
        final_kernel,
        "final_sums",
        [
            jax.ShapeDtypeStruct((tokens, features), BF16),
            jax.ShapeDtypeStruct((STEPS, 2, tokens), F32),
        ],
        [
            row_scratch,
            pltpu.VMEM((tokens, features), BF16),
            pltpu.VMEM((STEPS, 2, tokens), F32),
            pltpu.SemaphoreType.DMA((1 + features // OUT,)),
        ],
        operands=9,
        out_specs=[pl.BlockSpec(memory_space=pl.ANY)] * 2,
    )(shifted, own_rows, takes, routes, positions, *back)
    return result[None], prob.transpose(0, 2, 1)[None]


def shifted(block, axis, distance):
    devices = range(lax.axis_size(axis))
    route = [(i - distance, i) for i in devices if i - distance in devices]
    return lax.ppermute(block, axis, route)


def pair_table(route_part, place_part):
    labels = jnp.arange(E_FLY * MOST, dtype=jnp.int32)
    pair_keys = jnp.where(place_part >= 0, route_part * MOST + place_part, -1)
    return (pair_keys.T[:, None, :] == labels[None, :, None]).astype(jnp.float32)


def assemble(current, onehot, contrib):
    select = (onehot[0] + onehot[1]).astype(jnp.bfloat16)
    delta = lax.dot_general(
        select, contrib, (((0,), (0,)), ((), ())), preferred_element_type=jnp.float32
    )
    return (current.astype(jnp.float32) + delta).astype(jnp.bfloat16)


def expert_back(slot_rows, slot_rates, stored, gate_weight, up_weight, down_weight):
    downward = lax.dot_general(
        slot_rows, down_weight, (((1,), (1,)), ((), ())), preferred_element_type=jnp.float32
    )
    gate_pre = stored[:, 0, :].astype(jnp.float32)
    upward = stored[:, 1, :].astype(jnp.float32)
    sigmoid_gate = jax.nn.sigmoid(gate_pre)
    active = gate_pre * sigmoid_gate
    hidden = active * upward
    scaled = slot_rates.astype(jnp.float32)[:, None] * downward
    grad_gate = (scaled * upward * sigmoid_gate * (1.0 + gate_pre * (1.0 - sigmoid_gate))).astype(
        jnp.bfloat16
    )
    grad_up = (scaled * active).astype(jnp.bfloat16)
    prob_terms = jnp.sum(hidden * downward, axis=1)
    back_rows = lax.dot_general(
        grad_gate, gate_weight, (((1,), (1,)), ((), ())), preferred_element_type=jnp.float32
    )
    back_rows = back_rows + lax.dot_general(
        grad_up, up_weight, (((1,), (1,)), ((), ())), preferred_element_type=jnp.float32
    )
    return (back_rows, prob_terms)


def local_general(out_grad, routes, positions, route_probs, saved_acts, w_gate, w_up, w_down):
    devices = lax.axis_size("expert")
    members = devices // E_FLY
    pair_count = E_FLY * MOST
    gate_weight = w_gate[0]
    up_weight = w_up[0]
    down_weight = w_down[0]
    current_grad = out_grad[0]
    features = current_grad.shape[1]
    final_grad = current_grad
    prob_rows = []
    for step_index in range(STEPS):
        route_part = routes[0, step_index]
        place_part = positions[0, step_index]
        rate_part = route_probs[0, step_index]
        onehot = pair_table(route_part, place_part)
        select = (onehot[0] + onehot[1]).astype(jnp.bfloat16)
        send_rows = jnp.dot(select, current_grad, preferred_element_type=jnp.float32).astype(
            jnp.bfloat16
        )
        send_rates = jnp.sum(
            onehot * rate_part.T.astype(jnp.float32)[:, None, :], axis=(0, 2)
        ).astype(jnp.bfloat16)
        out_rows = jnp.broadcast_to(
            send_rows.reshape(E_FLY, 1, MOST, features), (E_FLY, members, MOST, features)
        ).reshape(devices, MOST, features)
        out_rates = jnp.broadcast_to(
            send_rates.reshape(E_FLY, 1, MOST), (E_FLY, members, MOST)
        ).reshape(devices, MOST)
        got_rows, got_rates = (
            lax.all_to_all(out_rows, "expert", split_axis=0, concat_axis=0, tiled=True),
            lax.all_to_all(out_rates, "expert", split_axis=0, concat_axis=0, tiled=True),
        )
        back_rows, prob_terms = expert_back(
            got_rows.reshape(devices * MOST, features),
            got_rates.reshape(devices * MOST),
            saved_acts[0, step_index],
            gate_weight,
            up_weight,
            down_weight,
        )
        back_rows = back_rows.reshape(devices, MOST, features)
        prob_terms = prob_terms.reshape(devices, MOST)
        came_rows, came_terms = (
            lax.all_to_all(back_rows, "expert", split_axis=0, concat_axis=0, tiled=True),
            lax.all_to_all(prob_terms, "expert", split_axis=0, concat_axis=0, tiled=True),
        )
        contrib = (
            jnp.sum(came_rows.reshape(E_FLY, members, MOST, features), axis=1)
            .astype(jnp.bfloat16)
            .reshape(pair_count, features)
        )
        slot_terms = jnp.sum(came_terms.reshape(E_FLY, members, MOST), axis=1).reshape(pair_count)
        prob_rows.append(jnp.sum(onehot * slot_terms[None, :, None], axis=1).T)
        if step_index + 1 < STEPS:
            current_grad = shifted(assemble(current_grad, onehot, contrib), "pipe", -1)
        else:
            final_grad = assemble(current_grad, onehot, contrib)
    return (final_grad[None], jnp.stack(prob_rows, axis=0)[None])


def solution(mesh):
    in_specs = (
        P("pipe", "expert", None),
        P("pipe", None, "expert", None),
        P("pipe", None, "expert", None),
        P("pipe", None, "expert", None),
        P("pipe", None, None, None, "expert"),
        P("pipe", None, "expert"),
        P("pipe", None, "expert"),
        P("pipe", "expert", None),
    )
    out_specs = (P("pipe", "expert", None), P("pipe", None, "expert", None))
    one_chip = mesh.shape["expert"] == 2 * E_FLY
    local = local_chip if one_chip else local_general
    return jax.shard_map(local, mesh=mesh, in_specs=in_specs, out_specs=out_specs, check_vma=False)
```

```python
import functools

import jax
import jax.numpy as jnp
from jax import lax
from jax.experimental import pallas as pl
from jax.experimental.pallas import tpu as pltpu
from jax.sharding import PartitionSpec as P

E_FLY = 4
MOST = 2
STEPS = 2
PAIRS = E_FLY * MOST
META = 128
CHUNK = 384
SPAN = 1024
OUT = 768
COST0 = 20_000_000_000
COST1 = 0
COST2 = 20_000_000_000
COST3 = 20_000_000_000
LIMIT = 54
F32 = jnp.float32
BF16 = jnp.bfloat16
NT = (((1,), (1,)), ((), ()))
TN = (((0,), (0,)), ((), ()))


def call(kernel, name, out_shape, scratch=(), hbm=0, operands=0, limit=24, cost=0, out_specs=None):
    specs = [pl.BlockSpec(memory_space=pl.ANY)] * hbm
    specs += [pl.BlockSpec(memory_space=pltpu.VMEM)] * (operands - hbm)
    return pl.pallas_call(
        kernel,
        name=name,
        out_shape=out_shape,
        in_specs=specs,
        **({} if out_specs is None else {"out_specs": out_specs}),
        scratch_shapes=list(scratch),
        cost_estimate=pl.CostEstimate(flops=cost, bytes_accessed=0, transcendentals=0),
        compiler_params=pltpu.CompilerParams(vmem_limit_bytes=limit * 2**20),
    )


def place():
    at = lax.axis_index("expert")
    return lax.axis_index("pipe"), at // 2, at % 2


def keys_of(routes, positions, step):
    return jnp.where(positions[step] >= 0, routes[step] * MOST + positions[step], -1)


def labels(rows, expert_of):
    row = lax.broadcasted_iota(jnp.int32, (rows, 1), 0)
    return expert_of(row // MOST) * MOST + row % MOST


def hits(keys, label):
    return keys[0:1] == label, keys[1:2] == label


def one_hot(keys, label):
    first, second = hits(keys, label)
    return jnp.where(first | second, 1.0, 0.0).astype(F32)


def rates_of(keys, rates, label):
    first, second = hits(keys, label)
    picked = jnp.where(first, rates[0:1], 0.0) + jnp.where(second, rates[1:2], 0.0)
    return jnp.sum(picked, axis=1, keepdims=True)


def first_lanes(columns):
    lane = lax.broadcasted_iota(jnp.int32, (columns[0].shape[0], META), 1)
    out = jnp.zeros(lane.shape, F32)
    for index, column in enumerate(columns):
        out = jnp.where(lane == index, column, out)
    return out


def bring(sources, targets, sems):
    copies = [
        pltpu.make_async_copy(source, target, sems.at[index])
        for index, (source, target) in enumerate(zip(sources, targets))
    ]
    for copy in copies:
        copy.start()
    return copies


def put_rows(outs, rows, meta):
    width = rows.shape[1]
    for k, out in enumerate(outs):
        out[:, :width] = rows[MOST * k:MOST * (k + 1)].astype(BF16)
        out[:, width:] = meta[MOST * k:MOST * (k + 1)].astype(BF16)


def take_rows(scratch, refs):
    for k, ref in enumerate(refs):
        scratch[MOST * k:MOST * (k + 1), :] = ref[...].astype(F32)


def pick_kernel(*refs):
    outs, table, held, sems = refs[4:8], refs[8], refs[9:13], refs[13]
    copies = bring(refs[:4], held, sems)
    routes, positions, probs, grad = held
    for copy in copies[:3]:
        copy.wait()
    _, z, _ = place()
    keys = keys_of(routes, positions, 0)
    label = labels(PAIRS, lambda k: z ^ k)
    select = one_hot(keys, label)
    rate = rates_of(keys, probs[0].astype(F32), label)
    table[0:2] = keys_of(routes, positions, 1).astype(F32)
    table[2:4] = probs[1].astype(F32)
    copies[3].wait()
    rows = jnp.dot(select.astype(BF16), grad[...], preferred_element_type=F32)
    put_rows(outs, rows, first_lanes([rate]))


def ahead_kernel(grad, routes, positions, table, done, rows_out, held, packed):
    p, z, c = place()
    keys0 = keys_of(routes, positions, 0)
    keys1 = table[0:2].astype(jnp.int32)
    keys1 = jnp.where(p == 0, -1, keys1)
    label = labels(PAIRS, lambda k: z ^ k)
    select = one_hot(keys1, label)
    rows = jnp.dot(select.astype(BF16), grad[...], preferred_element_type=F32)
    rate = rates_of(keys1, table[2:4], label)
    lane = lax.broadcasted_iota(jnp.int32, (PAIRS, META), 1)
    meta = jnp.where(lane == E_FLY * PAIRS, rate, 0.0)
    column = lax.broadcasted_iota(jnp.int32, (META, 1), 0)
    source, block, spot = column // PAIRS, column // MOST % E_FLY, column % MOST
    row = lax.broadcasted_iota(jnp.int32, (PAIRS, 1), 0)
    for k in range(E_FLY):
        expert = z ^ k ^ source
        own = (source < E_FLY) & (source ^ block == k)
        step0 = one_hot(keys0, jnp.where(own, expert * MOST + spot, -2))
        match = lax.dot_general(
            select.astype(BF16), step0.astype(BF16), NT, preferred_element_type=F32
        )
        meta = meta + jnp.where(row // MOST == k, match, 0.0)
    features = rows.shape[1]
    width = features + META
    rows_out[:, :features] = done[...]
    taken = one_hot(jnp.where(p == 0, -1, keys0), label)
    rows_out[:, features:width] = taken.astype(BF16)
    held[:, :features] = rows
    held[:, features:width] = meta
    parts = PAIRS // MOST
    for at in range(PAIRS):
        k, spot = at // MOST, at % MOST
        for part in range(parts):
            piece = held[at:at + 1, part * SPAN:(part + 1) * SPAN]
            packed[parts * spot + part:parts * spot + part + 1, k * SPAN:(k + 1) * SPAN] = piece
    rows_out[:, width:] = packed[...].astype(BF16)


def factor_kernel(acts, acts_other, factors, rows_at):
    _, z, c = place()
    steps, slots, _, width = acts.shape
    for half, ref in enumerate((acts, acts_other)):
        for at in range(steps * slots):
            rows_at[2 * at:2 * at + 2, half * width:(half + 1) * width] = ref[
                at // slots, at % slots
            ].astype(F32)
    stored = rows_at[...].astype(BF16)
    row = lax.broadcasted_iota(jnp.int32, (2 * steps * PAIRS, 2 * steps * slots), 0)
    column = lax.broadcasted_iota(jnp.int32, row.shape, 1)
    group, k, spot = row // PAIRS, row // MOST % E_FLY, row % MOST
    slot = (2 * (z ^ k) + c) * MOST + spot
    wanted = 2 * (group // 2 * slots + slot) + group % 2
    pick = jnp.where(column == wanted, 1.0, 0.0).astype(BF16)
    picked = jnp.dot(pick, stored, preferred_element_type=F32)
    for step in range(steps):
        gate = picked[2 * step * PAIRS:(2 * step + 1) * PAIRS]
        up = picked[(2 * step + 1) * PAIRS:(2 * step + 2) * PAIRS]
        sigmoid = 1.0 / (1.0 + jnp.exp(-gate))
        active = gate * sigmoid
        factors[step, 0] = up * sigmoid * (1.0 + gate * (1.0 - sigmoid))
        factors[step, 1] = active
        factors[step, 2] = active * up


def expert_rows(rows, rate, factors, step, weights):
    down, gate, up = weights[:2], weights[2:4], weights[4:]
    v = jnp.concatenate(
        [lax.dot_general(ref[...], rows, NT, preferred_element_type=F32).T for ref in down],
        axis=1,
    )
    scaled = rate * v
    grads = jnp.concatenate(
        [(scaled * factors[step, 0]).astype(BF16), (scaled * factors[step, 1]).astype(BF16)],
        axis=1,
    )
    terms = jnp.sum(factors[step, 2] * v, axis=1, keepdims=True)

    def back(at):
        part = slice(at, at + CHUNK)
        wide = jnp.concatenate([ref[part] for ref in (*gate, *up)], axis=1)
        return part, lax.dot_general(wide, grads, NT, preferred_element_type=F32).T

    return [functools.partial(back, at) for at in range(0, rows.shape[1], CHUNK)], terms


def step_zero_kernel(*refs):
    got, factors, weights = refs[:4], refs[4], refs[5:11]
    done, terms_out, rows_at = refs[11:]
    take_rows(rows_at, got)
    features = rows_at.shape[1] - META
    rate = rows_at[:, features:features + 1]
    backs, terms = expert_rows(rows_at[:, :features].astype(BF16), rate, factors, 0, weights)
    terms_out[...] = jnp.broadcast_to(terms, terms_out.shape)
    for back in backs:
        part, value = back()
        done[:, part] = value.astype(BF16)


def merge_kernel(came, *outs):
    features = outs[0].shape[1] - SPAN
    for k, out in enumerate(outs):
        first = features + META + SPAN * (k + 1)
        out[:, :features] = came[:, :features]
        out[:, features:] = came[:, first:first + SPAN]


def split(value):
    high = value.astype(BF16).astype(F32)
    middle = (value - high).astype(BF16).astype(F32)
    return [high, middle, value - high - middle]


def step_one_kernel(*refs):
    came, (factors, terms0), weights = refs[:4], refs[4:6], refs[6:12]
    outs, ahead_at = refs[12:16], refs[16]
    features = came[1].shape[1] - SPAN
    parts = PAIRS // MOST
    for k in range(E_FLY):
        first = features + META if k == 0 else features
        pieces = came[k][:, first:first + SPAN].astype(F32)
        for spot in range(MOST):
            at = MOST * k + spot
            for part in range(parts):
                row = parts * spot + part
                ahead_at[at:at + 1, part * SPAN:(part + 1) * SPAN] = pieces[row:row + 1]
    meta = ahead_at[:, features:features + META]
    rate = meta[:, E_FLY * PAIRS:E_FLY * PAIRS + 1]
    match = meta[:, :E_FLY * PAIRS].astype(BF16)
    everything = jnp.concatenate([ref[:, :features] for ref in came], axis=0)
    rows = ahead_at[:, :features] + jnp.dot(match, everything, preferred_element_type=F32)
    backs, terms = expert_rows(rows.astype(BF16), rate, factors, 1, weights)
    for back in backs:
        part, value = back()
        for k, out in enumerate(outs):
            out[:, part] = value[MOST * k:MOST * (k + 1)].astype(BF16)
    meta = first_lanes(split(terms) + split(terms0[:, 0:1]))
    for k, out in enumerate(outs):
        out[:, features:] = meta[MOST * k:MOST * (k + 1)].astype(BF16)


def own_kernel(*refs):
    routes, positions, came, (rows, takes) = *refs[:2], refs[2:6], refs[6:]
    _, z, _ = place()
    features = rows.shape[1]
    for k in range(E_FLY):
        own = came[k][MOST * k:MOST * (k + 1), :features]
        rows[MOST * k:MOST * (k + 1), :] = own.astype(F32)
    select = one_hot(keys_of(routes, positions, 1), labels(PAIRS, lambda k: z ^ k))
    before = came[0][:, features:features + META].astype(F32)
    takes[...] = jnp.concatenate([before, select], axis=0).astype(BF16)


def final_kernel(*refs):
    shifted, own, takes, routes, positions = refs[:5]
    got, (out, prob_out) = refs[5:9], refs[9:11]
    back_at, out_at, prob_at, sems = refs[11:]
    p, z, _ = place()
    features = out.shape[1]
    label = labels(PAIRS, lambda k: z ^ k)
    take_rows(back_at, got)
    copies = []
    last = p == lax.axis_size("pipe") - 1
    for at in range(0, features, CHUNK):
        part = slice(at, at + CHUNK)
        rows = jnp.concatenate([own[:, part], back_at[:, part]], axis=0).astype(BF16)
        delta = lax.dot_general(takes[...], rows, TN, preferred_element_type=F32)
        base = jnp.where(last, 0.0, shifted[:, part].astype(F32))
        out_at[:, part] = (base + delta).astype(BF16)
        if (at + CHUNK) % OUT == 0:
            wide = pl.ds(at + CHUNK - OUT, OUT)
            copies.append(
                pltpu.make_async_copy(
                    out_at.at[:, wide], out.at[:, wide], sems.at[len(copies)]
                )
            )
            copies[-1].start()
    meta = back_at[:, features:]
    for step in range(STEPS):
        first = 3 * (STEPS - 1 - step)
        terms = meta[:, first:first + 1] + (meta[:, first + 1:first + 2] + meta[:, first + 2:first + 3])
        for choice, hit in enumerate(hits(keys_of(routes, positions, step), label)):
            prob_at[step, choice:choice + 1] = jnp.sum(
                jnp.where(hit, terms, 0.0), axis=0, keepdims=True
            )
    copies.append(pltpu.make_async_copy(prob_at, prob_out, sems.at[len(copies)]))
    copies[-1].start()
    for copy in copies:
        copy.wait()


def local_chip(out_grad, routes, positions, route_probs, saved_acts, w_gate, w_up, w_down):
    sections = lax.axis_size("pipe")
    devices = lax.axis_size("expert")
    grad = out_grad[0]
    tokens, features = grad.shape
    width = features + META
    routes = routes[0].transpose(0, 2, 1)
    positions = positions[0].transpose(0, 2, 1)
    probs = route_probs[0].transpose(0, 2, 1)
    acts = saved_acts[0]
    hidden = 2 * acts.shape[-1]

    def across(block):
        return lax.ppermute(block, "expert", [(i, i ^ 1) for i in range(devices)])

    def along(block, k):
        if k == 0:
            return block
        return lax.ppermute(block, "expert", [(i, i ^ (2 * k)) for i in range(devices)])

    def along_all(blocks):
        return [along(blocks[k], k) for k in reversed(range(E_FLY))][::-1]

    def relay(block, distance):
        route = [(i, (i + distance) % sections) for i in range(sections)]
        return lax.ppermute(block, "pipe", route)

    pair = jax.ShapeDtypeStruct((MOST, width), BF16)
    block = jax.ShapeDtypeStruct((PAIRS, width), BF16)
    wide = jax.ShapeDtypeStruct((PAIRS, features + SPAN), BF16)
    pieces = PAIRS // MOST * SPAN
    row_scratch = pltpu.VMEM((PAIRS, width), F32)

    own = [w_down[0], w_gate[0], w_up[0]]
    acts_other = across(acts)
    others = [across(own[0])]
    small = (routes, positions, probs, grad)
    *picked, table = call(
        pick_kernel,
        "pick_rows",
        [pltpu.VMEM(pair.shape, BF16)] * E_FLY
        + [pltpu.VMEM((4, tokens), F32)],
        [pltpu.VMEM(array.shape, array.dtype) for array in small]
        + [pltpu.SemaphoreType.DMA((4,))],
        hbm=4,
        operands=4,
        limit=LIMIT,
    )(*small)
    *own, picked[0] = lax.optimization_barrier((*own, picked[0]))
    others += [across(array) for array in own[1:]]
    others[0], picked[2] = lax.optimization_barrier((others[0], picked[2]))
    acts_other, picked[1] = lax.optimization_barrier((acts_other, picked[1]))
    got = along_all(picked)
    table, others[1] = lax.optimization_barrier((table, others[1]))
    table = relay(table, 1)
    factors = call(
        factor_kernel,
        "factors",
        jax.ShapeDtypeStruct((STEPS, 3, PAIRS, hidden), F32),
        [pltpu.VMEM((2 * acts.shape[0] * acts.shape[1], hidden), F32)],
        operands=2,
        cost=COST3,
    )(acts, acts_other)
    weights = [array for pair_of in zip(own, others) for array in pair_of]
    done, terms0 = call(
        step_zero_kernel,
        "step_zero",
        [
            jax.ShapeDtypeStruct((PAIRS, features), BF16),
            jax.ShapeDtypeStruct((PAIRS, META), F32),
        ],
        [row_scratch],
        operands=11,
        cost=COST0,
    )(*got, factors, *weights)
    rows = call(
        ahead_kernel,
        "rows_ahead",
        jax.ShapeDtypeStruct((PAIRS, width + E_FLY * SPAN), BF16),
        [pltpu.VMEM((PAIRS, pieces), F32), pltpu.VMEM((PAIRS, E_FLY * SPAN), F32)],
        operands=5,
    )(grad, routes, positions, table, done)
    came = relay(rows, -1)
    shifted, _ = lax.optimization_barrier((grad, across(terms0)))
    shifted = relay(shifted, -1)
    sends = call(merge_kernel, "merge", [wide] * (E_FLY - 1), operands=1, cost=COST2)(came)
    came = along_all([came, *sends])
    back = call(
        step_one_kernel,
        "step_one",
        [pair] * E_FLY,
        [pltpu.VMEM((PAIRS, pieces), F32)],
        operands=12,
        cost=COST1,
    )(*came, factors, terms0, *weights)
    back = along_all(back)
    own_rows, takes = call(
        own_kernel,
        "own_rows",
        [
            jax.ShapeDtypeStruct((PAIRS, features), F32),
            jax.ShapeDtypeStruct((STEPS * PAIRS, tokens), BF16),
        ],
        operands=6,
    )(routes, positions, *came)
    result, prob = call(
        final_kernel,
        "final_sums",
        [
            jax.ShapeDtypeStruct((tokens, features), BF16),
            jax.ShapeDtypeStruct((STEPS, 2, tokens), F32),
        ],
        [
            row_scratch,
            pltpu.VMEM((tokens, features), BF16),
            pltpu.VMEM((STEPS, 2, tokens), F32),
            pltpu.SemaphoreType.DMA((1 + features // OUT,)),
        ],
        operands=9,
        out_specs=[pl.BlockSpec(memory_space=pl.ANY)] * 2,
    )(shifted, own_rows, takes, routes, positions, *back)
    return result[None], prob.transpose(0, 2, 1)[None]


def shifted(block, axis, distance):
    devices = range(lax.axis_size(axis))
    route = [(i - distance, i) for i in devices if i - distance in devices]
    return lax.ppermute(block, axis, route)


def pair_table(route_part, place_part):
    labels = jnp.arange(E_FLY * MOST, dtype=jnp.int32)
    pair_keys = jnp.where(place_part >= 0, route_part * MOST + place_part, -1)
    return (pair_keys.T[:, None, :] == labels[None, :, None]).astype(jnp.float32)


def assemble(current, onehot, contrib):
    select = (onehot[0] + onehot[1]).astype(jnp.bfloat16)
    delta = lax.dot_general(
        select, contrib, (((0,), (0,)), ((), ())), preferred_element_type=jnp.float32
    )
    return (current.astype(jnp.float32) + delta).astype(jnp.bfloat16)


def expert_back(slot_rows, slot_rates, stored, gate_weight, up_weight, down_weight):
    downward = lax.dot_general(
        slot_rows, down_weight, (((1,), (1,)), ((), ())), preferred_element_type=jnp.float32
    )
    gate_pre = stored[:, 0, :].astype(jnp.float32)
    upward = stored[:, 1, :].astype(jnp.float32)
    sigmoid_gate = jax.nn.sigmoid(gate_pre)
    active = gate_pre * sigmoid_gate
    hidden = active * upward
    scaled = slot_rates.astype(jnp.float32)[:, None] * downward
    grad_gate = (scaled * upward * sigmoid_gate * (1.0 + gate_pre * (1.0 - sigmoid_gate))).astype(
        jnp.bfloat16
    )
    grad_up = (scaled * active).astype(jnp.bfloat16)
    prob_terms = jnp.sum(hidden * downward, axis=1)
    back_rows = lax.dot_general(
        grad_gate, gate_weight, (((1,), (1,)), ((), ())), preferred_element_type=jnp.float32
    )
    back_rows = back_rows + lax.dot_general(
        grad_up, up_weight, (((1,), (1,)), ((), ())), preferred_element_type=jnp.float32
    )
    return (back_rows, prob_terms)


def local_general(out_grad, routes, positions, route_probs, saved_acts, w_gate, w_up, w_down):
    devices = lax.axis_size("expert")
    members = devices // E_FLY
    pair_count = E_FLY * MOST
    gate_weight = w_gate[0]
    up_weight = w_up[0]
    down_weight = w_down[0]
    current_grad = out_grad[0]
    features = current_grad.shape[1]
    final_grad = current_grad
    prob_rows = []
    for step_index in range(STEPS):
        route_part = routes[0, step_index]
        place_part = positions[0, step_index]
        rate_part = route_probs[0, step_index]
        onehot = pair_table(route_part, place_part)
        select = (onehot[0] + onehot[1]).astype(jnp.bfloat16)
        send_rows = jnp.dot(select, current_grad, preferred_element_type=jnp.float32).astype(
            jnp.bfloat16
        )
        send_rates = jnp.sum(
            onehot * rate_part.T.astype(jnp.float32)[:, None, :], axis=(0, 2)
        ).astype(jnp.bfloat16)
        out_rows = jnp.broadcast_to(
            send_rows.reshape(E_FLY, 1, MOST, features), (E_FLY, members, MOST, features)
        ).reshape(devices, MOST, features)
        out_rates = jnp.broadcast_to(
            send_rates.reshape(E_FLY, 1, MOST), (E_FLY, members, MOST)
        ).reshape(devices, MOST)
        got_rows, got_rates = (
            lax.all_to_all(out_rows, "expert", split_axis=0, concat_axis=0, tiled=True),
            lax.all_to_all(out_rates, "expert", split_axis=0, concat_axis=0, tiled=True),
        )
        back_rows, prob_terms = expert_back(
            got_rows.reshape(devices * MOST, features),
            got_rates.reshape(devices * MOST),
            saved_acts[0, step_index],
            gate_weight,
            up_weight,
            down_weight,
        )
        back_rows = back_rows.reshape(devices, MOST, features)
        prob_terms = prob_terms.reshape(devices, MOST)
        came_rows, came_terms = (
            lax.all_to_all(back_rows, "expert", split_axis=0, concat_axis=0, tiled=True),
            lax.all_to_all(prob_terms, "expert", split_axis=0, concat_axis=0, tiled=True),
        )
        contrib = (
            jnp.sum(came_rows.reshape(E_FLY, members, MOST, features), axis=1)
            .astype(jnp.bfloat16)
            .reshape(pair_count, features)
        )
        slot_terms = jnp.sum(came_terms.reshape(E_FLY, members, MOST), axis=1).reshape(pair_count)
        prob_rows.append(jnp.sum(onehot * slot_terms[None, :, None], axis=1).T)
        if step_index + 1 < STEPS:
            current_grad = shifted(assemble(current_grad, onehot, contrib), "pipe", -1)
        else:
            final_grad = assemble(current_grad, onehot, contrib)
    return (final_grad[None], jnp.stack(prob_rows, axis=0)[None])


def solution(mesh):
    in_specs = (
        P("pipe", "expert", None),
        P("pipe", None, "expert", None),
        P("pipe", None, "expert", None),
        P("pipe", None, "expert", None),
        P("pipe", None, None, None, "expert"),
        P("pipe", None, "expert"),
        P("pipe", None, "expert"),
        P("pipe", "expert", None),
    )
    out_specs = (P("pipe", "expert", None), P("pipe", None, "expert", None))
    one_chip = mesh.shape["expert"] == 2 * E_FLY
    local = local_chip if one_chip else local_general
    return jax.shard_map(local, mesh=mesh, in_specs=in_specs, out_specs=out_specs, check_vma=False)
```

```python
import functools

import jax
import jax.numpy as jnp
from jax import lax
from jax.experimental import pallas as pl
from jax.experimental.pallas import tpu as pltpu
from jax.sharding import PartitionSpec as P

E_FLY = 4
MOST = 2
STEPS = 2
PAIRS = E_FLY * MOST
META = 128
CHUNK = 384
SPAN = 1024
OUT = 768
COST0 = 20_000_000_000
COST1 = 0
COST2 = 20_000_000_000
COST3 = 20_000_000_000
LIMIT = 54
F32 = jnp.float32
BF16 = jnp.bfloat16
NT = (((1,), (1,)), ((), ()))
TN = (((0,), (0,)), ((), ()))


def call(kernel, name, out_shape, scratch=(), hbm=0, operands=0, limit=24, cost=0, out_specs=None):
    specs = [pl.BlockSpec(memory_space=pl.ANY)] * hbm
    specs += [pl.BlockSpec(memory_space=pltpu.VMEM)] * (operands - hbm)
    return pl.pallas_call(
        kernel,
        name=name,
        out_shape=out_shape,
        in_specs=specs,
        **({} if out_specs is None else {"out_specs": out_specs}),
        scratch_shapes=list(scratch),
        cost_estimate=pl.CostEstimate(flops=cost, bytes_accessed=0, transcendentals=0),
        compiler_params=pltpu.CompilerParams(vmem_limit_bytes=limit * 2**20),
    )


def place():
    at = lax.axis_index("expert")
    return lax.axis_index("pipe"), at // 2, at % 2


def keys_of(routes, positions, step):
    return jnp.where(positions[step] >= 0, routes[step] * MOST + positions[step], -1)


def labels(rows, expert_of):
    row = lax.broadcasted_iota(jnp.int32, (rows, 1), 0)
    return expert_of(row // MOST) * MOST + row % MOST


def hits(keys, label):
    return keys[0:1] == label, keys[1:2] == label


def one_hot(keys, label):
    first, second = hits(keys, label)
    return jnp.where(first | second, 1.0, 0.0).astype(F32)


def rates_of(keys, rates, label):
    first, second = hits(keys, label)
    picked = jnp.where(first, rates[0:1], 0.0) + jnp.where(second, rates[1:2], 0.0)
    return jnp.sum(picked, axis=1, keepdims=True)


def first_lanes(columns):
    lane = lax.broadcasted_iota(jnp.int32, (columns[0].shape[0], META), 1)
    out = jnp.zeros(lane.shape, F32)
    for index, column in enumerate(columns):
        out = jnp.where(lane == index, column, out)
    return out


def bring(sources, targets, sems):
    copies = [
        pltpu.make_async_copy(source, target, sems.at[index])
        for index, (source, target) in enumerate(zip(sources, targets))
    ]
    for copy in copies:
        copy.start()
    return copies


def put_rows(outs, rows, meta):
    width = rows.shape[1]
    for k, out in enumerate(outs):
        out[:, :width] = rows[MOST * k:MOST * (k + 1)].astype(BF16)
        out[:, width:] = meta[MOST * k:MOST * (k + 1)].astype(BF16)


def take_rows(scratch, refs):
    for k, ref in enumerate(refs):
        scratch[MOST * k:MOST * (k + 1), :] = ref[...].astype(F32)


def pick_kernel(*refs):
    outs, table, held, sems = refs[4:8], refs[8], refs[9:13], refs[13]
    copies = bring(refs[:4], held, sems)
    routes, positions, probs, grad = held
    for copy in copies[:3]:
        copy.wait()
    _, z, _ = place()
    keys = keys_of(routes, positions, 0)
    label = labels(PAIRS, lambda k: z ^ k)
    select = one_hot(keys, label)
    rate = rates_of(keys, probs[0].astype(F32), label)
    table[0:2] = keys_of(routes, positions, 1).astype(F32)
    table[2:4] = probs[1].astype(F32)
    copies[3].wait()
    rows = jnp.dot(select.astype(BF16), grad[...], preferred_element_type=F32)
    put_rows(outs, rows, first_lanes([rate]))


def ahead_kernel(grad, routes, positions, table, done, rows_out, held, packed):
    p, z, c = place()
    keys0 = keys_of(routes, positions, 0)
    keys1 = table[0:2].astype(jnp.int32)
    keys1 = jnp.where(p == 0, -1, keys1)
    label = labels(PAIRS, lambda k: z ^ k)
    select = one_hot(keys1, label)
    rows = jnp.dot(select.astype(BF16), grad[...], preferred_element_type=F32)
    rate = rates_of(keys1, table[2:4], label)
    lane = lax.broadcasted_iota(jnp.int32, (PAIRS, META), 1)
    meta = jnp.where(lane == E_FLY * PAIRS, rate, 0.0)
    column = lax.broadcasted_iota(jnp.int32, (META, 1), 0)
    source, block, spot = column // PAIRS, column // MOST % E_FLY, column % MOST
    row = lax.broadcasted_iota(jnp.int32, (PAIRS, 1), 0)
    for k in range(E_FLY):
        expert = z ^ k ^ source
        own = (source < E_FLY) & (source ^ block == k)
        step0 = one_hot(keys0, jnp.where(own, expert * MOST + spot, -2))
        match = lax.dot_general(
            select.astype(BF16), step0.astype(BF16), NT, preferred_element_type=F32
        )
        meta = meta + jnp.where(row // MOST == k, match, 0.0)
    features = rows.shape[1]
    width = features + META
    rows_out[:, :features] = done[...]
    taken = one_hot(jnp.where(p == 0, -1, keys0), label)
    rows_out[:, features:width] = taken.astype(BF16)
    held[:, :features] = rows
    held[:, features:width] = meta
    parts = PAIRS // MOST
    for at in range(PAIRS):
        k, spot = at // MOST, at % MOST
        for part in range(parts):
            piece = held[at:at + 1, part * SPAN:(part + 1) * SPAN]
            packed[parts * spot + part:parts * spot + part + 1, k * SPAN:(k + 1) * SPAN] = piece
    rows_out[:, width:] = packed[...].astype(BF16)


def factor_kernel(acts, acts_other, factors, rows_at):
    _, z, c = place()
    steps, slots, _, width = acts.shape
    for half, ref in enumerate((acts, acts_other)):
        for at in range(steps * slots):
            rows_at[2 * at:2 * at + 2, half * width:(half + 1) * width] = ref[
                at // slots, at % slots
            ].astype(F32)
    stored = rows_at[...].astype(BF16)
    row = lax.broadcasted_iota(jnp.int32, (2 * steps * PAIRS, 2 * steps * slots), 0)
    column = lax.broadcasted_iota(jnp.int32, row.shape, 1)
    group, k, spot = row // PAIRS, row // MOST % E_FLY, row % MOST
    slot = (2 * (z ^ k) + c) * MOST + spot
    wanted = 2 * (group // 2 * slots + slot) + group % 2
    pick = jnp.where(column == wanted, 1.0, 0.0).astype(BF16)
    picked = jnp.dot(pick, stored, preferred_element_type=F32)
    for step in range(steps):
        gate = picked[2 * step * PAIRS:(2 * step + 1) * PAIRS]
        up = picked[(2 * step + 1) * PAIRS:(2 * step + 2) * PAIRS]
        sigmoid = 1.0 / (1.0 + jnp.exp(-gate))
        active = gate * sigmoid
        factors[step, 0] = up * sigmoid * (1.0 + gate * (1.0 - sigmoid))
        factors[step, 1] = active
        factors[step, 2] = active * up


def expert_rows(rows, rate, factors, step, weights):
    down, gate, up = weights[:2], weights[2:4], weights[4:]
    v = jnp.concatenate(
        [lax.dot_general(ref[...], rows, NT, preferred_element_type=F32).T for ref in down],
        axis=1,
    )
    scaled = rate * v
    grads = jnp.concatenate(
        [(scaled * factors[step, 0]).astype(BF16), (scaled * factors[step, 1]).astype(BF16)],
        axis=1,
    )
    terms = jnp.sum(factors[step, 2] * v, axis=1, keepdims=True)

    def back(at):
        part = slice(at, at + CHUNK)
        wide = jnp.concatenate([ref[part] for ref in (*gate, *up)], axis=1)
        return part, lax.dot_general(wide, grads, NT, preferred_element_type=F32).T

    return [functools.partial(back, at) for at in range(0, rows.shape[1], CHUNK)], terms


def step_zero_kernel(*refs):
    got, factors, weights = refs[:4], refs[4], refs[5:11]
    done, terms_out, rows_at = refs[11:]
    take_rows(rows_at, got)
    features = rows_at.shape[1] - META
    rate = rows_at[:, features:features + 1]
    backs, terms = expert_rows(rows_at[:, :features].astype(BF16), rate, factors, 0, weights)
    terms_out[...] = jnp.broadcast_to(terms, terms_out.shape)
    for back in backs:
        part, value = back()
        done[:, part] = value.astype(BF16)


def merge_kernel(came, *outs):
    features = outs[0].shape[1] - SPAN
    for k, out in enumerate(outs):
        first = features + META + SPAN * (k + 1)
        out[:, :features] = came[:, :features]
        out[:, features:] = came[:, first:first + SPAN]


def split(value):
    high = value.astype(BF16).astype(F32)
    middle = (value - high).astype(BF16).astype(F32)
    return [high, middle, value - high - middle]


def step_one_kernel(*refs):
    came, (factors, terms0), weights = refs[:4], refs[4:6], refs[6:12]
    outs, ahead_at = refs[12:16], refs[16]
    features = came[1].shape[1] - SPAN
    parts = PAIRS // MOST
    for k in range(E_FLY):
        first = features + META if k == 0 else features
        pieces = came[k][:, first:first + SPAN].astype(F32)
        for spot in range(MOST):
            at = MOST * k + spot
            for part in range(parts):
                row = parts * spot + part
                ahead_at[at:at + 1, part * SPAN:(part + 1) * SPAN] = pieces[row:row + 1]
    meta = ahead_at[:, features:features + META]
    rate = meta[:, E_FLY * PAIRS:E_FLY * PAIRS + 1]
    match = meta[:, :E_FLY * PAIRS].astype(BF16)
    everything = jnp.concatenate([ref[:, :features] for ref in came], axis=0)
    rows = ahead_at[:, :features] + jnp.dot(match, everything, preferred_element_type=F32)
    backs, terms = expert_rows(rows.astype(BF16), rate, factors, 1, weights)
    for back in backs:
        part, value = back()
        for k, out in enumerate(outs):
            out[:, part] = value[MOST * k:MOST * (k + 1)].astype(BF16)
    meta = first_lanes(split(terms) + split(terms0[:, 0:1]))
    for k, out in enumerate(outs):
        out[:, features:] = meta[MOST * k:MOST * (k + 1)].astype(BF16)


def own_kernel(*refs):
    routes, positions, came, (rows, takes) = *refs[:2], refs[2:6], refs[6:]
    _, z, _ = place()
    features = rows.shape[1]
    for k in range(E_FLY):
        own = came[k][MOST * k:MOST * (k + 1), :features]
        rows[MOST * k:MOST * (k + 1), :] = own.astype(F32)
    select = one_hot(keys_of(routes, positions, 1), labels(PAIRS, lambda k: z ^ k))
    before = came[0][:, features:features + META].astype(F32)
    takes[...] = jnp.concatenate([before, select], axis=0).astype(BF16)


def final_kernel(*refs):
    shifted, own, takes, routes, positions = refs[:5]
    got, (out, prob_out) = refs[5:9], refs[9:11]
    back_at, out_at, prob_at, sems = refs[11:]
    p, z, _ = place()
    features = out.shape[1]
    label = labels(PAIRS, lambda k: z ^ k)
    take_rows(back_at, got)
    copies = []
    last = p == lax.axis_size("pipe") - 1
    for at in range(0, features, CHUNK):
        part = slice(at, at + CHUNK)
        rows = jnp.concatenate([own[:, part], back_at[:, part]], axis=0).astype(BF16)
        delta = lax.dot_general(takes[...], rows, TN, preferred_element_type=F32)
        base = jnp.where(last, 0.0, shifted[:, part].astype(F32))
        out_at[:, part] = (base + delta).astype(BF16)
        if (at + CHUNK) % OUT == 0:
            wide = pl.ds(at + CHUNK - OUT, OUT)
            copies.append(
                pltpu.make_async_copy(
                    out_at.at[:, wide], out.at[:, wide], sems.at[len(copies)]
                )
            )
            copies[-1].start()
    meta = back_at[:, features:]
    for step in range(STEPS):
        first = 3 * (STEPS - 1 - step)
        terms = meta[:, first:first + 1] + (meta[:, first + 1:first + 2] + meta[:, first + 2:first + 3])
        for choice, hit in enumerate(hits(keys_of(routes, positions, step), label)):
            prob_at[step, choice:choice + 1] = jnp.sum(
                jnp.where(hit, terms, 0.0), axis=0, keepdims=True
            )
    copies.append(pltpu.make_async_copy(prob_at, prob_out, sems.at[len(copies)]))
    copies[-1].start()
    for copy in copies:
        copy.wait()


def local_chip(out_grad, routes, positions, route_probs, saved_acts, w_gate, w_up, w_down):
    sections = lax.axis_size("pipe")
    devices = lax.axis_size("expert")
    grad = out_grad[0]
    tokens, features = grad.shape
    width = features + META
    routes = routes[0].transpose(0, 2, 1)
    positions = positions[0].transpose(0, 2, 1)
    probs = route_probs[0].transpose(0, 2, 1)
    acts = saved_acts[0]
    hidden = 2 * acts.shape[-1]

    def across(block):
        return lax.ppermute(block, "expert", [(i, i ^ 1) for i in range(devices)])

    def along(block, k):
        if k == 0:
            return block
        return lax.ppermute(block, "expert", [(i, i ^ (2 * k)) for i in range(devices)])

    def along_all(blocks):
        return [along(blocks[k], k) for k in reversed(range(E_FLY))][::-1]

    def relay(block, distance):
        route = [(i, (i + distance) % sections) for i in range(sections)]
        return lax.ppermute(block, "pipe", route)

    pair = jax.ShapeDtypeStruct((MOST, width), BF16)
    block = jax.ShapeDtypeStruct((PAIRS, width), BF16)
    wide = jax.ShapeDtypeStruct((PAIRS, features + SPAN), BF16)
    pieces = PAIRS // MOST * SPAN
    row_scratch = pltpu.VMEM((PAIRS, width), F32)

    own = [w_down[0], w_gate[0], w_up[0]]
    acts_other = across(acts)
    others = [across(own[0])]
    small = (routes, positions, probs, grad)
    *picked, table = call(
        pick_kernel,
        "pick_rows",
        [pltpu.VMEM(pair.shape, BF16)] * E_FLY
        + [pltpu.VMEM((4, tokens), F32)],
        [pltpu.VMEM(array.shape, array.dtype) for array in small]
        + [pltpu.SemaphoreType.DMA((4,))],
        hbm=4,
        operands=4,
        limit=LIMIT,
    )(*small)
    *own, picked[0] = lax.optimization_barrier((*own, picked[0]))
    others += [across(array) for array in own[1:]]
    others[0], picked[2] = lax.optimization_barrier((others[0], picked[2]))
    acts_other, picked[1] = lax.optimization_barrier((acts_other, picked[1]))
    got = along_all(picked)
    table, others[1] = lax.optimization_barrier((table, others[1]))
    table = relay(table, 1)
    factors = call(
        factor_kernel,
        "factors",
        jax.ShapeDtypeStruct((STEPS, 3, PAIRS, hidden), F32),
        [pltpu.VMEM((2 * acts.shape[0] * acts.shape[1], hidden), F32)],
        operands=2,
        cost=COST3,
    )(acts, acts_other)
    weights = [array for pair_of in zip(own, others) for array in pair_of]
    done, terms0 = call(
        step_zero_kernel,
        "step_zero",
        [
            jax.ShapeDtypeStruct((PAIRS, features), BF16),
            jax.ShapeDtypeStruct((PAIRS, META), F32),
        ],
        [row_scratch],
        operands=11,
        cost=COST0,
    )(*got, factors, *weights)
    rows = call(
        ahead_kernel,
        "rows_ahead",
        jax.ShapeDtypeStruct((PAIRS, width + E_FLY * SPAN), BF16),
        [pltpu.VMEM((PAIRS, pieces), F32), pltpu.VMEM((PAIRS, E_FLY * SPAN), F32)],
        operands=5,
    )(grad, routes, positions, table, done)
    came = relay(rows, -1)
    shifted = relay(grad, -1)
    sends = call(merge_kernel, "merge", [wide] * (E_FLY - 1), operands=1, cost=COST2)(came)
    came = along_all([came, *sends])
    back = call(
        step_one_kernel,
        "step_one",
        [pair] * E_FLY,
        [pltpu.VMEM((PAIRS, pieces), F32)],
        operands=12,
        cost=COST1,
    )(*came, factors, terms0, *weights)
    back = along_all(back)
    own_rows, takes = call(
        own_kernel,
        "own_rows",
        [
            jax.ShapeDtypeStruct((PAIRS, features), F32),
            jax.ShapeDtypeStruct((STEPS * PAIRS, tokens), BF16),
        ],
        operands=6,
    )(routes, positions, *came)
    result, prob = call(
        final_kernel,
        "final_sums",
        [
            jax.ShapeDtypeStruct((tokens, features), BF16),
            jax.ShapeDtypeStruct((STEPS, 2, tokens), F32),
        ],
        [
            row_scratch,
            pltpu.VMEM((tokens, features), BF16),
            pltpu.VMEM((STEPS, 2, tokens), F32),
            pltpu.SemaphoreType.DMA((1 + features // OUT,)),
        ],
        operands=9,
        out_specs=[pl.BlockSpec(memory_space=pl.ANY)] * 2,
    )(shifted, own_rows, takes, routes, positions, *back)
    return result[None], prob.transpose(0, 2, 1)[None]


def shifted(block, axis, distance):
    devices = range(lax.axis_size(axis))
    route = [(i - distance, i) for i in devices if i - distance in devices]
    return lax.ppermute(block, axis, route)


def pair_table(route_part, place_part):
    labels = jnp.arange(E_FLY * MOST, dtype=jnp.int32)
    pair_keys = jnp.where(place_part >= 0, route_part * MOST + place_part, -1)
    return (pair_keys.T[:, None, :] == labels[None, :, None]).astype(jnp.float32)


def assemble(current, onehot, contrib):
    select = (onehot[0] + onehot[1]).astype(jnp.bfloat16)
    delta = lax.dot_general(
        select, contrib, (((0,), (0,)), ((), ())), preferred_element_type=jnp.float32
    )
    return (current.astype(jnp.float32) + delta).astype(jnp.bfloat16)


def expert_back(slot_rows, slot_rates, stored, gate_weight, up_weight, down_weight):
    downward = lax.dot_general(
        slot_rows, down_weight, (((1,), (1,)), ((), ())), preferred_element_type=jnp.float32
    )
    gate_pre = stored[:, 0, :].astype(jnp.float32)
    upward = stored[:, 1, :].astype(jnp.float32)
    sigmoid_gate = jax.nn.sigmoid(gate_pre)
    active = gate_pre * sigmoid_gate
    hidden = active * upward
    scaled = slot_rates.astype(jnp.float32)[:, None] * downward
    grad_gate = (scaled * upward * sigmoid_gate * (1.0 + gate_pre * (1.0 - sigmoid_gate))).astype(
        jnp.bfloat16
    )
    grad_up = (scaled * active).astype(jnp.bfloat16)
    prob_terms = jnp.sum(hidden * downward, axis=1)
    back_rows = lax.dot_general(
        grad_gate, gate_weight, (((1,), (1,)), ((), ())), preferred_element_type=jnp.float32
    )
    back_rows = back_rows + lax.dot_general(
        grad_up, up_weight, (((1,), (1,)), ((), ())), preferred_element_type=jnp.float32
    )
    return (back_rows, prob_terms)


def local_general(out_grad, routes, positions, route_probs, saved_acts, w_gate, w_up, w_down):
    devices = lax.axis_size("expert")
    members = devices // E_FLY
    pair_count = E_FLY * MOST
    gate_weight = w_gate[0]
    up_weight = w_up[0]
    down_weight = w_down[0]
    current_grad = out_grad[0]
    features = current_grad.shape[1]
    final_grad = current_grad
    prob_rows = []
    for step_index in range(STEPS):
        route_part = routes[0, step_index]
        place_part = positions[0, step_index]
        rate_part = route_probs[0, step_index]
        onehot = pair_table(route_part, place_part)
        select = (onehot[0] + onehot[1]).astype(jnp.bfloat16)
        send_rows = jnp.dot(select, current_grad, preferred_element_type=jnp.float32).astype(
            jnp.bfloat16
        )
        send_rates = jnp.sum(
            onehot * rate_part.T.astype(jnp.float32)[:, None, :], axis=(0, 2)
        ).astype(jnp.bfloat16)
        out_rows = jnp.broadcast_to(
            send_rows.reshape(E_FLY, 1, MOST, features), (E_FLY, members, MOST, features)
        ).reshape(devices, MOST, features)
        out_rates = jnp.broadcast_to(
            send_rates.reshape(E_FLY, 1, MOST), (E_FLY, members, MOST)
        ).reshape(devices, MOST)
        got_rows, got_rates = (
            lax.all_to_all(out_rows, "expert", split_axis=0, concat_axis=0, tiled=True),
            lax.all_to_all(out_rates, "expert", split_axis=0, concat_axis=0, tiled=True),
        )
        back_rows, prob_terms = expert_back(
            got_rows.reshape(devices * MOST, features),
            got_rates.reshape(devices * MOST),
            saved_acts[0, step_index],
            gate_weight,
            up_weight,
            down_weight,
        )
        back_rows = back_rows.reshape(devices, MOST, features)
        prob_terms = prob_terms.reshape(devices, MOST)
        came_rows, came_terms = (
            lax.all_to_all(back_rows, "expert", split_axis=0, concat_axis=0, tiled=True),
            lax.all_to_all(prob_terms, "expert", split_axis=0, concat_axis=0, tiled=True),
        )
        contrib = (
            jnp.sum(came_rows.reshape(E_FLY, members, MOST, features), axis=1)
            .astype(jnp.bfloat16)
            .reshape(pair_count, features)
        )
        slot_terms = jnp.sum(came_terms.reshape(E_FLY, members, MOST), axis=1).reshape(pair_count)
        prob_rows.append(jnp.sum(onehot * slot_terms[None, :, None], axis=1).T)
        if step_index + 1 < STEPS:
            current_grad = shifted(assemble(current_grad, onehot, contrib), "pipe", -1)
        else:
            final_grad = assemble(current_grad, onehot, contrib)
    return (final_grad[None], jnp.stack(prob_rows, axis=0)[None])


def solution(mesh):
    in_specs = (
        P("pipe", "expert", None),
        P("pipe", None, "expert", None),
        P("pipe", None, "expert", None),
        P("pipe", None, "expert", None),
        P("pipe", None, None, None, "expert"),
        P("pipe", None, "expert"),
        P("pipe", None, "expert"),
        P("pipe", "expert", None),
    )
    out_specs = (P("pipe", "expert", None), P("pipe", None, "expert", None))
    one_chip = mesh.shape["expert"] == 2 * E_FLY
    local = local_chip if one_chip else local_general
    return jax.shard_map(local, mesh=mesh, in_specs=in_specs, out_specs=out_specs, check_vma=False)
```

```python
import functools

import jax
import jax.numpy as jnp
from jax import lax
from jax.experimental import pallas as pl
from jax.experimental.pallas import tpu as pltpu
from jax.sharding import PartitionSpec as P

E_FLY = 4
MOST = 2
STEPS = 2
PAIRS = E_FLY * MOST
META = 128
CHUNK = 384
SPAN = 1024
OUT = 768
COST0 = 20_000_000_000
COST1 = 0
COST2 = 20_000_000_000
COST3 = 20_000_000_000
LIMIT = 54
F32 = jnp.float32
BF16 = jnp.bfloat16
NT = (((1,), (1,)), ((), ()))
TN = (((0,), (0,)), ((), ()))


def call(kernel, name, out_shape, scratch=(), hbm=0, operands=0, limit=24, cost=0, out_specs=None):
    specs = [pl.BlockSpec(memory_space=pl.ANY)] * hbm
    specs += [pl.BlockSpec(memory_space=pltpu.VMEM)] * (operands - hbm)
    return pl.pallas_call(
        kernel,
        name=name,
        out_shape=out_shape,
        in_specs=specs,
        **({} if out_specs is None else {"out_specs": out_specs}),
        scratch_shapes=list(scratch),
        cost_estimate=pl.CostEstimate(flops=cost, bytes_accessed=0, transcendentals=0),
        compiler_params=pltpu.CompilerParams(vmem_limit_bytes=limit * 2**20),
    )


def place():
    at = lax.axis_index("expert")
    return lax.axis_index("pipe"), at // 2, at % 2


def keys_of(routes, positions, step):
    return jnp.where(positions[step] >= 0, routes[step] * MOST + positions[step], -1)


def labels(rows, expert_of):
    row = lax.broadcasted_iota(jnp.int32, (rows, 1), 0)
    return expert_of(row // MOST) * MOST + row % MOST


def hits(keys, label):
    return keys[0:1] == label, keys[1:2] == label


def one_hot(keys, label):
    first, second = hits(keys, label)
    return jnp.where(first | second, 1.0, 0.0).astype(F32)


def rates_of(keys, rates, label):
    first, second = hits(keys, label)
    picked = jnp.where(first, rates[0:1], 0.0) + jnp.where(second, rates[1:2], 0.0)
    return jnp.sum(picked, axis=1, keepdims=True)


def first_lanes(columns):
    lane = lax.broadcasted_iota(jnp.int32, (columns[0].shape[0], META), 1)
    out = jnp.zeros(lane.shape, F32)
    for index, column in enumerate(columns):
        out = jnp.where(lane == index, column, out)
    return out


def bring(sources, targets, sems):
    copies = [
        pltpu.make_async_copy(source, target, sems.at[index])
        for index, (source, target) in enumerate(zip(sources, targets))
    ]
    for copy in copies:
        copy.start()
    return copies


def put_rows(outs, rows, meta):
    width = rows.shape[1]
    for k, out in enumerate(outs):
        out[:, :width] = rows[MOST * k:MOST * (k + 1)].astype(BF16)
        out[:, width:] = meta[MOST * k:MOST * (k + 1)].astype(BF16)


def take_rows(scratch, refs):
    for k, ref in enumerate(refs):
        scratch[MOST * k:MOST * (k + 1), :] = ref[...].astype(F32)


def pick_kernel(*refs):
    outs, table, held, sems = refs[4:8], refs[8], refs[9:13], refs[13]
    copies = bring(refs[:4], held, sems)
    routes, positions, probs, grad = held
    for copy in copies[:3]:
        copy.wait()
    _, z, _ = place()
    keys = keys_of(routes, positions, 0)
    label = labels(PAIRS, lambda k: z ^ k)
    select = one_hot(keys, label)
    rate = rates_of(keys, probs[0].astype(F32), label)
    table[0:2] = keys_of(routes, positions, 1).astype(F32)
    table[2:4] = probs[1].astype(F32)
    copies[3].wait()
    rows = jnp.dot(select.astype(BF16), grad[...], preferred_element_type=F32)
    put_rows(outs, rows, first_lanes([rate]))


def ahead_kernel(grad, routes, positions, table, done, rows_out, held, packed):
    p, z, c = place()
    keys0 = keys_of(routes, positions, 0)
    keys1 = table[0:2].astype(jnp.int32)
    keys1 = jnp.where(p == 0, -1, keys1)
    label = labels(PAIRS, lambda k: z ^ k)
    select = one_hot(keys1, label)
    rows = jnp.dot(select.astype(BF16), grad[...], preferred_element_type=F32)
    rate = rates_of(keys1, table[2:4], label)
    lane = lax.broadcasted_iota(jnp.int32, (PAIRS, META), 1)
    meta = jnp.where(lane == E_FLY * PAIRS, rate, 0.0)
    column = lax.broadcasted_iota(jnp.int32, (META, 1), 0)
    source, block, spot = column // PAIRS, column // MOST % E_FLY, column % MOST
    row = lax.broadcasted_iota(jnp.int32, (PAIRS, 1), 0)
    for k in range(E_FLY):
        expert = z ^ k ^ source
        own = (source < E_FLY) & (source ^ block == k)
        step0 = one_hot(keys0, jnp.where(own, expert * MOST + spot, -2))
        match = lax.dot_general(
            select.astype(BF16), step0.astype(BF16), NT, preferred_element_type=F32
        )
        meta = meta + jnp.where(row // MOST == k, match, 0.0)
    features = rows.shape[1]
    width = features + META
    rows_out[:, :features] = done[...]
    taken = one_hot(jnp.where(p == 0, -1, keys0), label)
    rows_out[:, features:width] = taken.astype(BF16)
    held[:, :features] = rows
    held[:, features:width] = meta
    parts = PAIRS // MOST
    for at in range(PAIRS):
        k, spot = at // MOST, at % MOST
        for part in range(parts):
            piece = held[at:at + 1, part * SPAN:(part + 1) * SPAN]
            packed[parts * spot + part:parts * spot + part + 1, k * SPAN:(k + 1) * SPAN] = piece
    rows_out[:, width:] = packed[...].astype(BF16)


def factor_kernel(acts, acts_other, factors, rows_at):
    _, z, c = place()
    steps, slots, _, width = acts.shape
    for half, ref in enumerate((acts, acts_other)):
        for at in range(steps * slots):
            rows_at[2 * at:2 * at + 2, half * width:(half + 1) * width] = ref[
                at // slots, at % slots
            ].astype(F32)
    stored = rows_at[...].astype(BF16)
    row = lax.broadcasted_iota(jnp.int32, (2 * steps * PAIRS, 2 * steps * slots), 0)
    column = lax.broadcasted_iota(jnp.int32, row.shape, 1)
    group, k, spot = row // PAIRS, row // MOST % E_FLY, row % MOST
    slot = (2 * (z ^ k) + c) * MOST + spot
    wanted = 2 * (group // 2 * slots + slot) + group % 2
    pick = jnp.where(column == wanted, 1.0, 0.0).astype(BF16)
    picked = jnp.dot(pick, stored, preferred_element_type=F32)
    for step in range(steps):
        gate = picked[2 * step * PAIRS:(2 * step + 1) * PAIRS]
        up = picked[(2 * step + 1) * PAIRS:(2 * step + 2) * PAIRS]
        sigmoid = 1.0 / (1.0 + jnp.exp(-gate))
        active = gate * sigmoid
        factors[step, 0] = up * sigmoid * (1.0 + gate * (1.0 - sigmoid))
        factors[step, 1] = active
        factors[step, 2] = active * up


def expert_rows(rows, rate, factors, step, weights):
    down, gate, up = weights[:2], weights[2:4], weights[4:]
    v = jnp.concatenate(
        [lax.dot_general(ref[...], rows, NT, preferred_element_type=F32).T for ref in down],
        axis=1,
    )
    scaled = rate * v
    grads = jnp.concatenate(
        [(scaled * factors[step, 0]).astype(BF16), (scaled * factors[step, 1]).astype(BF16)],
        axis=1,
    )
    terms = jnp.sum(factors[step, 2] * v, axis=1, keepdims=True)

    def back(at):
        part = slice(at, at + CHUNK)
        wide = jnp.concatenate([ref[part] for ref in (*gate, *up)], axis=1)
        return part, lax.dot_general(wide, grads, NT, preferred_element_type=F32).T

    return [functools.partial(back, at) for at in range(0, rows.shape[1], CHUNK)], terms


def step_zero_kernel(*refs):
    got, factors, weights = refs[:4], refs[4], refs[5:11]
    done, terms_out, rows_at = refs[11:]
    take_rows(rows_at, got)
    features = rows_at.shape[1] - META
    rate = rows_at[:, features:features + 1]
    backs, terms = expert_rows(rows_at[:, :features].astype(BF16), rate, factors, 0, weights)
    terms_out[...] = jnp.broadcast_to(terms, terms_out.shape)
    for back in backs:
        part, value = back()
        done[:, part] = value.astype(BF16)


def merge_kernel(came, *outs):
    features = outs[0].shape[1] - SPAN
    for k, out in enumerate(outs):
        first = features + META + SPAN * (k + 1)
        out[:, :features] = came[:, :features]
        out[:, features:] = came[:, first:first + SPAN]


def split(value):
    high = value.astype(BF16).astype(F32)
    middle = (value - high).astype(BF16).astype(F32)
    return [high, middle, value - high - middle]


def step_one_kernel(*refs):
    came, (factors, terms0), weights = refs[:4], refs[4:6], refs[6:12]
    outs, ahead_at = refs[12:16], refs[16]
    features = came[1].shape[1] - SPAN
    parts = PAIRS // MOST
    for k in range(E_FLY):
        first = features + META if k == 0 else features
        pieces = came[k][:, first:first + SPAN].astype(F32)
        for spot in range(MOST):
            at = MOST * k + spot
            for part in range(parts):
                row = parts * spot + part
                ahead_at[at:at + 1, part * SPAN:(part + 1) * SPAN] = pieces[row:row + 1]
    meta = ahead_at[:, features:features + META]
    rate = meta[:, E_FLY * PAIRS:E_FLY * PAIRS + 1]
    match = meta[:, :E_FLY * PAIRS].astype(BF16)
    everything = jnp.concatenate([ref[:, :features] for ref in came], axis=0)
    rows = ahead_at[:, :features] + jnp.dot(match, everything, preferred_element_type=F32)
    backs, terms = expert_rows(rows.astype(BF16), rate, factors, 1, weights)
    for back in backs:
        part, value = back()
        for k, out in enumerate(outs):
            out[:, part] = value[MOST * k:MOST * (k + 1)].astype(BF16)
    meta = first_lanes(split(terms) + split(terms0[:, 0:1]))
    for k, out in enumerate(outs):
        out[:, features:] = meta[MOST * k:MOST * (k + 1)].astype(BF16)


def own_kernel(*refs):
    routes, positions, came, (rows, takes) = *refs[:2], refs[2:6], refs[6:]
    _, z, _ = place()
    features = rows.shape[1]
    for k in range(E_FLY):
        own = came[k][MOST * k:MOST * (k + 1), :features]
        rows[MOST * k:MOST * (k + 1), :] = own.astype(F32)
    select = one_hot(keys_of(routes, positions, 1), labels(PAIRS, lambda k: z ^ k))
    before = came[0][:, features:features + META].astype(F32)
    takes[...] = jnp.concatenate([before, select], axis=0).astype(BF16)


def final_kernel(*refs):
    shifted, own, takes, routes, positions = refs[:5]
    got, (out, prob_out) = refs[5:9], refs[9:11]
    back_at, out_at, prob_at, sems = refs[11:]
    p, z, _ = place()
    features = out.shape[1]
    label = labels(PAIRS, lambda k: z ^ k)
    take_rows(back_at, got)
    copies = []
    last = p == lax.axis_size("pipe") - 1
    for at in range(0, features, CHUNK):
        part = slice(at, at + CHUNK)
        rows = jnp.concatenate([own[:, part], back_at[:, part]], axis=0).astype(BF16)
        delta = lax.dot_general(takes[...], rows, TN, preferred_element_type=F32)
        base = jnp.where(last, 0.0, shifted[:, part].astype(F32))
        out_at[:, part] = (base + delta).astype(BF16)
        if (at + CHUNK) % OUT == 0:
            wide = pl.ds(at + CHUNK - OUT, OUT)
            copies.append(
                pltpu.make_async_copy(
                    out_at.at[:, wide], out.at[:, wide], sems.at[len(copies)]
                )
            )
            copies[-1].start()
    meta = back_at[:, features:]
    for step in range(STEPS):
        first = 3 * (STEPS - 1 - step)
        terms = meta[:, first:first + 1] + (meta[:, first + 1:first + 2] + meta[:, first + 2:first + 3])
        for choice, hit in enumerate(hits(keys_of(routes, positions, step), label)):
            prob_at[step, choice:choice + 1] = jnp.sum(
                jnp.where(hit, terms, 0.0), axis=0, keepdims=True
            )
    copies.append(pltpu.make_async_copy(prob_at, prob_out, sems.at[len(copies)]))
    copies[-1].start()
    for copy in copies:
        copy.wait()


def local_chip(out_grad, routes, positions, route_probs, saved_acts, w_gate, w_up, w_down):
    sections = lax.axis_size("pipe")
    devices = lax.axis_size("expert")
    grad = out_grad[0]
    tokens, features = grad.shape
    width = features + META
    routes = routes[0].transpose(0, 2, 1)
    positions = positions[0].transpose(0, 2, 1)
    probs = route_probs[0].transpose(0, 2, 1)
    acts = saved_acts[0]
    hidden = 2 * acts.shape[-1]

    def across(block):
        return lax.ppermute(block, "expert", [(i, i ^ 1) for i in range(devices)])

    def along(block, k):
        if k == 0:
            return block
        return lax.ppermute(block, "expert", [(i, i ^ (2 * k)) for i in range(devices)])

    def along_all(blocks):
        return [along(blocks[k], k) for k in reversed(range(E_FLY))][::-1]

    def relay(block, distance):
        route = [(i, (i + distance) % sections) for i in range(sections)]
        return lax.ppermute(block, "pipe", route)

    pair = jax.ShapeDtypeStruct((MOST, width), BF16)
    block = jax.ShapeDtypeStruct((PAIRS, width), BF16)
    wide = jax.ShapeDtypeStruct((PAIRS, features + SPAN), BF16)
    pieces = PAIRS // MOST * SPAN
    row_scratch = pltpu.VMEM((PAIRS, width), F32)

    own = [w_down[0], w_gate[0], w_up[0]]
    acts_other = across(acts)
    others = [across(own[0])]
    small = (routes, positions, probs, grad)
    *picked, table = call(
        pick_kernel,
        "pick_rows",
        [pltpu.VMEM(pair.shape, BF16)] * E_FLY
        + [pltpu.VMEM((4, tokens), F32)],
        [pltpu.VMEM(array.shape, array.dtype) for array in small]
        + [pltpu.SemaphoreType.DMA((4,))],
        hbm=4,
        operands=4,
        limit=LIMIT,
    )(*small)
    *own, picked[0] = lax.optimization_barrier((*own, picked[0]))
    others += [across(array) for array in own[1:]]
    others[0], picked[1] = lax.optimization_barrier((others[0], picked[1]))
    got = along_all(picked)
    table, others[1] = lax.optimization_barrier((table, others[1]))
    table = relay(table, 1)
    factors = call(
        factor_kernel,
        "factors",
        jax.ShapeDtypeStruct((STEPS, 3, PAIRS, hidden), F32),
        [pltpu.VMEM((2 * acts.shape[0] * acts.shape[1], hidden), F32)],
        operands=2,
        cost=COST3,
    )(acts, acts_other)
    weights = [array for pair_of in zip(own, others) for array in pair_of]
    done, terms0 = call(
        step_zero_kernel,
        "step_zero",
        [
            jax.ShapeDtypeStruct((PAIRS, features), BF16),
            jax.ShapeDtypeStruct((PAIRS, META), F32),
        ],
        [row_scratch],
        operands=11,
        cost=COST0,
    )(*got, factors, *weights)
    rows = call(
        ahead_kernel,
        "rows_ahead",
        jax.ShapeDtypeStruct((PAIRS, width + E_FLY * SPAN), BF16),
        [pltpu.VMEM((PAIRS, pieces), F32), pltpu.VMEM((PAIRS, E_FLY * SPAN), F32)],
        operands=5,
    )(grad, routes, positions, table, done)
    came = relay(rows, -1)
    shifted = relay(grad, -1)
    sends = call(merge_kernel, "merge", [wide] * (E_FLY - 1), operands=1, cost=COST2)(came)
    came = along_all([came, *sends])
    back = call(
        step_one_kernel,
        "step_one",
        [pair] * E_FLY,
        [pltpu.VMEM((PAIRS, pieces), F32)],
        operands=12,
        cost=COST1,
    )(*came, factors, terms0, *weights)
    back = along_all(back)
    own_rows, takes = call(
        own_kernel,
        "own_rows",
        [
            jax.ShapeDtypeStruct((PAIRS, features), F32),
            jax.ShapeDtypeStruct((STEPS * PAIRS, tokens), BF16),
        ],
        operands=6,
    )(routes, positions, *came)
    result, prob = call(
        final_kernel,
        "final_sums",
        [
            jax.ShapeDtypeStruct((tokens, features), BF16),
            jax.ShapeDtypeStruct((STEPS, 2, tokens), F32),
        ],
        [
            row_scratch,
            pltpu.VMEM((tokens, features), BF16),
            pltpu.VMEM((STEPS, 2, tokens), F32),
            pltpu.SemaphoreType.DMA((1 + features // OUT,)),
        ],
        operands=9,
        out_specs=[pl.BlockSpec(memory_space=pl.ANY)] * 2,
    )(shifted, own_rows, takes, routes, positions, *back)
    return result[None], prob.transpose(0, 2, 1)[None]


def shifted(block, axis, distance):
    devices = range(lax.axis_size(axis))
    route = [(i - distance, i) for i in devices if i - distance in devices]
    return lax.ppermute(block, axis, route)


def pair_table(route_part, place_part):
    labels = jnp.arange(E_FLY * MOST, dtype=jnp.int32)
    pair_keys = jnp.where(place_part >= 0, route_part * MOST + place_part, -1)
    return (pair_keys.T[:, None, :] == labels[None, :, None]).astype(jnp.float32)


def assemble(current, onehot, contrib):
    select = (onehot[0] + onehot[1]).astype(jnp.bfloat16)
    delta = lax.dot_general(
        select, contrib, (((0,), (0,)), ((), ())), preferred_element_type=jnp.float32
    )
    return (current.astype(jnp.float32) + delta).astype(jnp.bfloat16)


def expert_back(slot_rows, slot_rates, stored, gate_weight, up_weight, down_weight):
    downward = lax.dot_general(
        slot_rows, down_weight, (((1,), (1,)), ((), ())), preferred_element_type=jnp.float32
    )
    gate_pre = stored[:, 0, :].astype(jnp.float32)
    upward = stored[:, 1, :].astype(jnp.float32)
    sigmoid_gate = jax.nn.sigmoid(gate_pre)
    active = gate_pre * sigmoid_gate
    hidden = active * upward
    scaled = slot_rates.astype(jnp.float32)[:, None] * downward
    grad_gate = (scaled * upward * sigmoid_gate * (1.0 + gate_pre * (1.0 - sigmoid_gate))).astype(
        jnp.bfloat16
    )
    grad_up = (scaled * active).astype(jnp.bfloat16)
    prob_terms = jnp.sum(hidden * downward, axis=1)
    back_rows = lax.dot_general(
        grad_gate, gate_weight, (((1,), (1,)), ((), ())), preferred_element_type=jnp.float32
    )
    back_rows = back_rows + lax.dot_general(
        grad_up, up_weight, (((1,), (1,)), ((), ())), preferred_element_type=jnp.float32
    )
    return (back_rows, prob_terms)


def local_general(out_grad, routes, positions, route_probs, saved_acts, w_gate, w_up, w_down):
    devices = lax.axis_size("expert")
    members = devices // E_FLY
    pair_count = E_FLY * MOST
    gate_weight = w_gate[0]
    up_weight = w_up[0]
    down_weight = w_down[0]
    current_grad = out_grad[0]
    features = current_grad.shape[1]
    final_grad = current_grad
    prob_rows = []
    for step_index in range(STEPS):
        route_part = routes[0, step_index]
        place_part = positions[0, step_index]
        rate_part = route_probs[0, step_index]
        onehot = pair_table(route_part, place_part)
        select = (onehot[0] + onehot[1]).astype(jnp.bfloat16)
        send_rows = jnp.dot(select, current_grad, preferred_element_type=jnp.float32).astype(
            jnp.bfloat16
        )
        send_rates = jnp.sum(
            onehot * rate_part.T.astype(jnp.float32)[:, None, :], axis=(0, 2)
        ).astype(jnp.bfloat16)
        out_rows = jnp.broadcast_to(
            send_rows.reshape(E_FLY, 1, MOST, features), (E_FLY, members, MOST, features)
        ).reshape(devices, MOST, features)
        out_rates = jnp.broadcast_to(
            send_rates.reshape(E_FLY, 1, MOST), (E_FLY, members, MOST)
        ).reshape(devices, MOST)
        got_rows, got_rates = (
            lax.all_to_all(out_rows, "expert", split_axis=0, concat_axis=0, tiled=True),
            lax.all_to_all(out_rates, "expert", split_axis=0, concat_axis=0, tiled=True),
        )
        back_rows, prob_terms = expert_back(
            got_rows.reshape(devices * MOST, features),
            got_rates.reshape(devices * MOST),
            saved_acts[0, step_index],
            gate_weight,
            up_weight,
            down_weight,
        )
        back_rows = back_rows.reshape(devices, MOST, features)
        prob_terms = prob_terms.reshape(devices, MOST)
        came_rows, came_terms = (
            lax.all_to_all(back_rows, "expert", split_axis=0, concat_axis=0, tiled=True),
            lax.all_to_all(prob_terms, "expert", split_axis=0, concat_axis=0, tiled=True),
        )
        contrib = (
            jnp.sum(came_rows.reshape(E_FLY, members, MOST, features), axis=1)
            .astype(jnp.bfloat16)
            .reshape(pair_count, features)
        )
        slot_terms = jnp.sum(came_terms.reshape(E_FLY, members, MOST), axis=1).reshape(pair_count)
        prob_rows.append(jnp.sum(onehot * slot_terms[None, :, None], axis=1).T)
        if step_index + 1 < STEPS:
            current_grad = shifted(assemble(current_grad, onehot, contrib), "pipe", -1)
        else:
            final_grad = assemble(current_grad, onehot, contrib)
    return (final_grad[None], jnp.stack(prob_rows, axis=0)[None])


def solution(mesh):
    in_specs = (
        P("pipe", "expert", None),
        P("pipe", None, "expert", None),
        P("pipe", None, "expert", None),
        P("pipe", None, "expert", None),
        P("pipe", None, None, None, "expert"),
        P("pipe", None, "expert"),
        P("pipe", None, "expert"),
        P("pipe", "expert", None),
    )
    out_specs = (P("pipe", "expert", None), P("pipe", None, "expert", None))
    one_chip = mesh.shape["expert"] == 2 * E_FLY
    local = local_chip if one_chip else local_general
    return jax.shard_map(local, mesh=mesh, in_specs=in_specs, out_specs=out_specs, check_vma=False)
```

```python
import functools

import jax
import jax.numpy as jnp
from jax import lax
from jax.experimental import pallas as pl
from jax.experimental.pallas import tpu as pltpu
from jax.sharding import PartitionSpec as P

E_FLY = 4
MOST = 2
STEPS = 2
PAIRS = E_FLY * MOST
META = 128
CHUNK = 384
SPAN = 1024
OUT = 768
COST0 = 20_000_000_000
COST1 = 0
COST2 = 20_000_000_000
COST3 = 20_000_000_000
LIMIT = 54
F32 = jnp.float32
BF16 = jnp.bfloat16
NT = (((1,), (1,)), ((), ()))
TN = (((0,), (0,)), ((), ()))


def call(kernel, name, out_shape, scratch=(), hbm=0, operands=0, limit=24, cost=0, out_specs=None):
    specs = [pl.BlockSpec(memory_space=pl.ANY)] * hbm
    specs += [pl.BlockSpec(memory_space=pltpu.VMEM)] * (operands - hbm)
    return pl.pallas_call(
        kernel,
        name=name,
        out_shape=out_shape,
        in_specs=specs,
        **({} if out_specs is None else {"out_specs": out_specs}),
        scratch_shapes=list(scratch),
        cost_estimate=pl.CostEstimate(flops=cost, bytes_accessed=0, transcendentals=0),
        compiler_params=pltpu.CompilerParams(vmem_limit_bytes=limit * 2**20),
    )


def place():
    at = lax.axis_index("expert")
    return lax.axis_index("pipe"), at // 2, at % 2


def keys_of(routes, positions, step):
    return jnp.where(positions[step] >= 0, routes[step] * MOST + positions[step], -1)


def labels(rows, expert_of):
    row = lax.broadcasted_iota(jnp.int32, (rows, 1), 0)
    return expert_of(row // MOST) * MOST + row % MOST


def hits(keys, label):
    return keys[0:1] == label, keys[1:2] == label


def one_hot(keys, label):
    first, second = hits(keys, label)
    return jnp.where(first | second, 1.0, 0.0).astype(F32)


def rates_of(keys, rates, label):
    first, second = hits(keys, label)
    picked = jnp.where(first, rates[0:1], 0.0) + jnp.where(second, rates[1:2], 0.0)
    return jnp.sum(picked, axis=1, keepdims=True)


def first_lanes(columns):
    lane = lax.broadcasted_iota(jnp.int32, (columns[0].shape[0], META), 1)
    out = jnp.zeros(lane.shape, F32)
    for index, column in enumerate(columns):
        out = jnp.where(lane == index, column, out)
    return out


def bring(sources, targets, sems):
    copies = [
        pltpu.make_async_copy(source, target, sems.at[index])
        for index, (source, target) in enumerate(zip(sources, targets))
    ]
    for copy in copies:
        copy.start()
    return copies


def put_rows(outs, rows, meta):
    width = rows.shape[1]
    for k, out in enumerate(outs):
        out[:, :width] = rows[MOST * k:MOST * (k + 1)].astype(BF16)
        out[:, width:] = meta[MOST * k:MOST * (k + 1)].astype(BF16)


def take_rows(scratch, refs):
    for k, ref in enumerate(refs):
        scratch[MOST * k:MOST * (k + 1), :] = ref[...].astype(F32)


def pick_kernel(*refs):
    outs, table, held, sems = refs[4:8], refs[8], refs[9:13], refs[13]
    copies = bring(refs[:4], held, sems)
    routes, positions, probs, grad = held
    for copy in copies[:3]:
        copy.wait()
    _, z, _ = place()
    keys = keys_of(routes, positions, 0)
    label = labels(PAIRS, lambda k: z ^ k)
    select = one_hot(keys, label)
    rate = rates_of(keys, probs[0].astype(F32), label)
    table[0:2] = keys_of(routes, positions, 1).astype(F32)
    table[2:4] = probs[1].astype(F32)
    copies[3].wait()
    rows = jnp.dot(select.astype(BF16), grad[...], preferred_element_type=F32)
    put_rows(outs, rows, first_lanes([rate]))


def ahead_kernel(grad, routes, positions, table, done, rows_out, held, packed):
    p, z, c = place()
    keys0 = keys_of(routes, positions, 0)
    keys1 = table[0:2].astype(jnp.int32)
    keys1 = jnp.where(p == 0, -1, keys1)
    label = labels(PAIRS, lambda k: z ^ k)
    select = one_hot(keys1, label)
    rows = jnp.dot(select.astype(BF16), grad[...], preferred_element_type=F32)
    rate = rates_of(keys1, table[2:4], label)
    lane = lax.broadcasted_iota(jnp.int32, (PAIRS, META), 1)
    meta = jnp.where(lane == E_FLY * PAIRS, rate, 0.0)
    column = lax.broadcasted_iota(jnp.int32, (META, 1), 0)
    source, block, spot = column // PAIRS, column // MOST % E_FLY, column % MOST
    row = lax.broadcasted_iota(jnp.int32, (PAIRS, 1), 0)
    for k in range(E_FLY):
        expert = z ^ k ^ source
        own = (source < E_FLY) & (source ^ block == k)
        step0 = one_hot(keys0, jnp.where(own, expert * MOST + spot, -2))
        match = lax.dot_general(
            select.astype(BF16), step0.astype(BF16), NT, preferred_element_type=F32
        )
        meta = meta + jnp.where(row // MOST == k, match, 0.0)
    features = rows.shape[1]
    width = features + META
    rows_out[:, :features] = done[...]
    taken = one_hot(jnp.where(p == 0, -1, keys0), label)
    rows_out[:, features:width] = taken.astype(BF16)
    held[:, :features] = rows
    held[:, features:width] = meta
    parts = PAIRS // MOST
    for at in range(PAIRS):
        k, spot = at // MOST, at % MOST
        for part in range(parts):
            piece = held[at:at + 1, part * SPAN:(part + 1) * SPAN]
            packed[parts * spot + part:parts * spot + part + 1, k * SPAN:(k + 1) * SPAN] = piece
    rows_out[:, width:] = packed[...].astype(BF16)


def factor_kernel(acts, acts_other, factors, rows_at):
    _, z, c = place()
    steps, slots, _, width = acts.shape
    for half, ref in enumerate((acts, acts_other)):
        for at in range(steps * slots):
            rows_at[2 * at:2 * at + 2, half * width:(half + 1) * width] = ref[
                at // slots, at % slots
            ].astype(F32)
    stored = rows_at[...].astype(BF16)
    row = lax.broadcasted_iota(jnp.int32, (2 * steps * PAIRS, 2 * steps * slots), 0)
    column = lax.broadcasted_iota(jnp.int32, row.shape, 1)
    group, k, spot = row // PAIRS, row // MOST % E_FLY, row % MOST
    slot = (2 * (z ^ k) + c) * MOST + spot
    wanted = 2 * (group // 2 * slots + slot) + group % 2
    pick = jnp.where(column == wanted, 1.0, 0.0).astype(BF16)
    picked = jnp.dot(pick, stored, preferred_element_type=F32)
    for step in range(steps):
        gate = picked[2 * step * PAIRS:(2 * step + 1) * PAIRS]
        up = picked[(2 * step + 1) * PAIRS:(2 * step + 2) * PAIRS]
        sigmoid = 1.0 / (1.0 + jnp.exp(-gate))
        active = gate * sigmoid
        factors[step, 0] = up * sigmoid * (1.0 + gate * (1.0 - sigmoid))
        factors[step, 1] = active
        factors[step, 2] = active * up


def expert_rows(rows, rate, factors, step, weights):
    down, gate, up = weights[:2], weights[2:4], weights[4:]
    v = jnp.concatenate(
        [lax.dot_general(ref[...], rows, NT, preferred_element_type=F32).T for ref in down],
        axis=1,
    )
    scaled = rate * v
    grads = jnp.concatenate(
        [(scaled * factors[step, 0]).astype(BF16), (scaled * factors[step, 1]).astype(BF16)],
        axis=1,
    )
    terms = jnp.sum(factors[step, 2] * v, axis=1, keepdims=True)

    def back(at):
        part = slice(at, at + CHUNK)
        wide = jnp.concatenate([ref[part] for ref in (*gate, *up)], axis=1)
        return part, lax.dot_general(wide, grads, NT, preferred_element_type=F32).T

    return [functools.partial(back, at) for at in range(0, rows.shape[1], CHUNK)], terms


def step_zero_kernel(*refs):
    got, factors, weights = refs[:4], refs[4], refs[5:11]
    done, terms_out, rows_at = refs[11:]
    take_rows(rows_at, got)
    features = rows_at.shape[1] - META
    rate = rows_at[:, features:features + 1]
    backs, terms = expert_rows(rows_at[:, :features].astype(BF16), rate, factors, 0, weights)
    terms_out[...] = jnp.broadcast_to(terms, terms_out.shape)
    for back in backs:
        part, value = back()
        done[:, part] = value.astype(BF16)


def merge_kernel(came, *outs):
    features = outs[0].shape[1] - SPAN
    for k, out in enumerate(outs):
        first = features + META + SPAN * (k + 1)
        out[:, :features] = came[:, :features]
        out[:, features:] = came[:, first:first + SPAN]


def split(value):
    high = value.astype(BF16).astype(F32)
    middle = (value - high).astype(BF16).astype(F32)
    return [high, middle, value - high - middle]


def step_one_kernel(*refs):
    came, (factors, terms0), weights = refs[:4], refs[4:6], refs[6:12]
    outs, ahead_at = refs[12:16], refs[16]
    features = came[1].shape[1] - SPAN
    parts = PAIRS // MOST
    for k in range(E_FLY):
        first = features + META if k == 0 else features
        pieces = came[k][:, first:first + SPAN].astype(F32)
        for spot in range(MOST):
            at = MOST * k + spot
            for part in range(parts):
                row = parts * spot + part
                ahead_at[at:at + 1, part * SPAN:(part + 1) * SPAN] = pieces[row:row + 1]
    meta = ahead_at[:, features:features + META]
    rate = meta[:, E_FLY * PAIRS:E_FLY * PAIRS + 1]
    match = meta[:, :E_FLY * PAIRS].astype(BF16)
    everything = jnp.concatenate([ref[:, :features] for ref in came], axis=0)
    rows = ahead_at[:, :features] + jnp.dot(match, everything, preferred_element_type=F32)
    backs, terms = expert_rows(rows.astype(BF16), rate, factors, 1, weights)
    for back in backs:
        part, value = back()
        for k, out in enumerate(outs):
            out[:, part] = value[MOST * k:MOST * (k + 1)].astype(BF16)
    meta = first_lanes(split(terms) + split(terms0[:, 0:1]))
    for k, out in enumerate(outs):
        out[:, features:] = meta[MOST * k:MOST * (k + 1)].astype(BF16)


def own_kernel(*refs):
    routes, positions, came, (rows, takes) = *refs[:2], refs[2:6], refs[6:]
    _, z, _ = place()
    features = rows.shape[1]
    for k in range(E_FLY):
        own = came[k][MOST * k:MOST * (k + 1), :features]
        rows[MOST * k:MOST * (k + 1), :] = own.astype(F32)
    select = one_hot(keys_of(routes, positions, 1), labels(PAIRS, lambda k: z ^ k))
    before = came[0][:, features:features + META].astype(F32)
    takes[...] = jnp.concatenate([before, select], axis=0).astype(BF16)


def final_kernel(*refs):
    shifted, own, takes, routes, positions = refs[:5]
    got, (out, prob_out) = refs[5:9], refs[9:11]
    back_at, out_at, prob_at, sems = refs[11:]
    p, z, _ = place()
    features = out.shape[1]
    label = labels(PAIRS, lambda k: z ^ k)
    take_rows(back_at, got)
    copies = []
    last = p == lax.axis_size("pipe") - 1
    for at in range(0, features, CHUNK):
        part = slice(at, at + CHUNK)
        rows = jnp.concatenate([own[:, part], back_at[:, part]], axis=0).astype(BF16)
        delta = lax.dot_general(takes[...], rows, TN, preferred_element_type=F32)
        base = jnp.where(last, 0.0, shifted[:, part].astype(F32))
        out_at[:, part] = (base + delta).astype(BF16)
        if (at + CHUNK) % OUT == 0:
            wide = pl.ds(at + CHUNK - OUT, OUT)
            copies.append(
                pltpu.make_async_copy(
                    out_at.at[:, wide], out.at[:, wide], sems.at[len(copies)]
                )
            )
            copies[-1].start()
    meta = back_at[:, features:]
    for step in range(STEPS):
        first = 3 * (STEPS - 1 - step)
        terms = meta[:, first:first + 1] + (meta[:, first + 1:first + 2] + meta[:, first + 2:first + 3])
        for choice, hit in enumerate(hits(keys_of(routes, positions, step), label)):
            prob_at[step, choice:choice + 1] = jnp.sum(
                jnp.where(hit, terms, 0.0), axis=0, keepdims=True
            )
    copies.append(pltpu.make_async_copy(prob_at, prob_out, sems.at[len(copies)]))
    copies[-1].start()
    for copy in copies:
        copy.wait()


def local_chip(out_grad, routes, positions, route_probs, saved_acts, w_gate, w_up, w_down):
    sections = lax.axis_size("pipe")
    devices = lax.axis_size("expert")
    grad = out_grad[0]
    tokens, features = grad.shape
    width = features + META
    routes = routes[0].transpose(0, 2, 1)
    positions = positions[0].transpose(0, 2, 1)
    probs = route_probs[0].transpose(0, 2, 1)
    acts = saved_acts[0]
    hidden = 2 * acts.shape[-1]

    def across(block):
        return lax.ppermute(block, "expert", [(i, i ^ 1) for i in range(devices)])

    def along(block, k):
        if k == 0:
            return block
        return lax.ppermute(block, "expert", [(i, i ^ (2 * k)) for i in range(devices)])

    def along_all(blocks):
        return [along(blocks[k], k) for k in reversed(range(E_FLY))][::-1]

    def relay(block, distance):
        route = [(i, (i + distance) % sections) for i in range(sections)]
        return lax.ppermute(block, "pipe", route)

    pair = jax.ShapeDtypeStruct((MOST, width), BF16)
    block = jax.ShapeDtypeStruct((PAIRS, width), BF16)
    wide = jax.ShapeDtypeStruct((PAIRS, features + SPAN), BF16)
    pieces = PAIRS // MOST * SPAN
    row_scratch = pltpu.VMEM((PAIRS, width), F32)

    own = [w_down[0], w_gate[0], w_up[0]]
    acts_other = across(acts)
    others = [across(own[0])]
    small = (routes, positions, probs, grad)
    *picked, table = call(
        pick_kernel,
        "pick_rows",
        [pltpu.VMEM(pair.shape, BF16)] * E_FLY
        + [pltpu.VMEM((4, tokens), F32)],
        [pltpu.VMEM(array.shape, array.dtype) for array in small]
        + [pltpu.SemaphoreType.DMA((4,))],
        hbm=4,
        operands=4,
        limit=LIMIT,
    )(*small)
    others += [across(array) for array in own[1:]]
    others[0], picked[1] = lax.optimization_barrier((others[0], picked[1]))
    got = along_all(picked)
    table, others[1] = lax.optimization_barrier((table, others[1]))
    table = relay(table, 1)
    factors = call(
        factor_kernel,
        "factors",
        jax.ShapeDtypeStruct((STEPS, 3, PAIRS, hidden), F32),
        [pltpu.VMEM((2 * acts.shape[0] * acts.shape[1], hidden), F32)],
        operands=2,
        cost=COST3,
    )(acts, acts_other)
    weights = [array for pair_of in zip(own, others) for array in pair_of]
    done, terms0 = call(
        step_zero_kernel,
        "step_zero",
        [
            jax.ShapeDtypeStruct((PAIRS, features), BF16),
            jax.ShapeDtypeStruct((PAIRS, META), F32),
        ],
        [row_scratch],
        operands=11,
        cost=COST0,
    )(*got, factors, *weights)
    rows = call(
        ahead_kernel,
        "rows_ahead",
        jax.ShapeDtypeStruct((PAIRS, width + E_FLY * SPAN), BF16),
        [pltpu.VMEM((PAIRS, pieces), F32), pltpu.VMEM((PAIRS, E_FLY * SPAN), F32)],
        operands=5,
    )(grad, routes, positions, table, done)
    came = relay(rows, -1)
    shifted = relay(grad, -1)
    sends = call(merge_kernel, "merge", [wide] * (E_FLY - 1), operands=1, cost=COST2)(came)
    came = along_all([came, *sends])
    back = call(
        step_one_kernel,
        "step_one",
        [pair] * E_FLY,
        [pltpu.VMEM((PAIRS, pieces), F32)],
        operands=12,
        cost=COST1,
    )(*came, factors, terms0, *weights)
    back = along_all(back)
    own_rows, takes = call(
        own_kernel,
        "own_rows",
        [
            jax.ShapeDtypeStruct((PAIRS, features), F32),
            jax.ShapeDtypeStruct((STEPS * PAIRS, tokens), BF16),
        ],
        operands=6,
    )(routes, positions, *came)
    result, prob = call(
        final_kernel,
        "final_sums",
        [
            jax.ShapeDtypeStruct((tokens, features), BF16),
            jax.ShapeDtypeStruct((STEPS, 2, tokens), F32),
        ],
        [
            row_scratch,
            pltpu.VMEM((tokens, features), BF16),
            pltpu.VMEM((STEPS, 2, tokens), F32),
            pltpu.SemaphoreType.DMA((1 + features // OUT,)),
        ],
        operands=9,
        out_specs=[pl.BlockSpec(memory_space=pl.ANY)] * 2,
    )(shifted, own_rows, takes, routes, positions, *back)
    return result[None], prob.transpose(0, 2, 1)[None]


def shifted(block, axis, distance):
    devices = range(lax.axis_size(axis))
    route = [(i - distance, i) for i in devices if i - distance in devices]
    return lax.ppermute(block, axis, route)


def pair_table(route_part, place_part):
    labels = jnp.arange(E_FLY * MOST, dtype=jnp.int32)
    pair_keys = jnp.where(place_part >= 0, route_part * MOST + place_part, -1)
    return (pair_keys.T[:, None, :] == labels[None, :, None]).astype(jnp.float32)


def assemble(current, onehot, contrib):
    select = (onehot[0] + onehot[1]).astype(jnp.bfloat16)
    delta = lax.dot_general(
        select, contrib, (((0,), (0,)), ((), ())), preferred_element_type=jnp.float32
    )
    return (current.astype(jnp.float32) + delta).astype(jnp.bfloat16)


def expert_back(slot_rows, slot_rates, stored, gate_weight, up_weight, down_weight):
    downward = lax.dot_general(
        slot_rows, down_weight, (((1,), (1,)), ((), ())), preferred_element_type=jnp.float32
    )
    gate_pre = stored[:, 0, :].astype(jnp.float32)
    upward = stored[:, 1, :].astype(jnp.float32)
    sigmoid_gate = jax.nn.sigmoid(gate_pre)
    active = gate_pre * sigmoid_gate
    hidden = active * upward
    scaled = slot_rates.astype(jnp.float32)[:, None] * downward
    grad_gate = (scaled * upward * sigmoid_gate * (1.0 + gate_pre * (1.0 - sigmoid_gate))).astype(
        jnp.bfloat16
    )
    grad_up = (scaled * active).astype(jnp.bfloat16)
    prob_terms = jnp.sum(hidden * downward, axis=1)
    back_rows = lax.dot_general(
        grad_gate, gate_weight, (((1,), (1,)), ((), ())), preferred_element_type=jnp.float32
    )
    back_rows = back_rows + lax.dot_general(
        grad_up, up_weight, (((1,), (1,)), ((), ())), preferred_element_type=jnp.float32
    )
    return (back_rows, prob_terms)


def local_general(out_grad, routes, positions, route_probs, saved_acts, w_gate, w_up, w_down):
    devices = lax.axis_size("expert")
    members = devices // E_FLY
    pair_count = E_FLY * MOST
    gate_weight = w_gate[0]
    up_weight = w_up[0]
    down_weight = w_down[0]
    current_grad = out_grad[0]
    features = current_grad.shape[1]
    final_grad = current_grad
    prob_rows = []
    for step_index in range(STEPS):
        route_part = routes[0, step_index]
        place_part = positions[0, step_index]
        rate_part = route_probs[0, step_index]
        onehot = pair_table(route_part, place_part)
        select = (onehot[0] + onehot[1]).astype(jnp.bfloat16)
        send_rows = jnp.dot(select, current_grad, preferred_element_type=jnp.float32).astype(
            jnp.bfloat16
        )
        send_rates = jnp.sum(
            onehot * rate_part.T.astype(jnp.float32)[:, None, :], axis=(0, 2)
        ).astype(jnp.bfloat16)
        out_rows = jnp.broadcast_to(
            send_rows.reshape(E_FLY, 1, MOST, features), (E_FLY, members, MOST, features)
        ).reshape(devices, MOST, features)
        out_rates = jnp.broadcast_to(
            send_rates.reshape(E_FLY, 1, MOST), (E_FLY, members, MOST)
        ).reshape(devices, MOST)
        got_rows, got_rates = (
            lax.all_to_all(out_rows, "expert", split_axis=0, concat_axis=0, tiled=True),
            lax.all_to_all(out_rates, "expert", split_axis=0, concat_axis=0, tiled=True),
        )
        back_rows, prob_terms = expert_back(
            got_rows.reshape(devices * MOST, features),
            got_rates.reshape(devices * MOST),
            saved_acts[0, step_index],
            gate_weight,
            up_weight,
            down_weight,
        )
        back_rows = back_rows.reshape(devices, MOST, features)
        prob_terms = prob_terms.reshape(devices, MOST)
        came_rows, came_terms = (
            lax.all_to_all(back_rows, "expert", split_axis=0, concat_axis=0, tiled=True),
            lax.all_to_all(prob_terms, "expert", split_axis=0, concat_axis=0, tiled=True),
        )
        contrib = (
            jnp.sum(came_rows.reshape(E_FLY, members, MOST, features), axis=1)
            .astype(jnp.bfloat16)
            .reshape(pair_count, features)
        )
        slot_terms = jnp.sum(came_terms.reshape(E_FLY, members, MOST), axis=1).reshape(pair_count)
        prob_rows.append(jnp.sum(onehot * slot_terms[None, :, None], axis=1).T)
        if step_index + 1 < STEPS:
            current_grad = shifted(assemble(current_grad, onehot, contrib), "pipe", -1)
        else:
            final_grad = assemble(current_grad, onehot, contrib)
    return (final_grad[None], jnp.stack(prob_rows, axis=0)[None])


def solution(mesh):
    in_specs = (
        P("pipe", "expert", None),
        P("pipe", None, "expert", None),
        P("pipe", None, "expert", None),
        P("pipe", None, "expert", None),
        P("pipe", None, None, None, "expert"),
        P("pipe", None, "expert"),
        P("pipe", None, "expert"),
        P("pipe", "expert", None),
    )
    out_specs = (P("pipe", "expert", None), P("pipe", None, "expert", None))
    one_chip = mesh.shape["expert"] == 2 * E_FLY
    local = local_chip if one_chip else local_general
    return jax.shard_map(local, mesh=mesh, in_specs=in_specs, out_specs=out_specs, check_vma=False)
```
